128 devices in a mesh: leaf: 64 (over z, x, y), rhs: 2 (over core).
Axes of the slice: x: 4, y: 4, z: 4, core: 2. Of those that a mesh axis runs over, the one named last changes fastest.
Arguments:
- points: float32 [3, 524288], P(None, 'leaf'), may hold values from -6 to 6
- values: float32 [64, 524288], P('rhs', 'leaf'), may hold values from -6 to 6
- near_list: int32 [4096, 27], P('leaf'), may hold values from 0 to 4095, as said below
- near_count: int32 [4096], P('leaf'), may hold values from 2 to 27, as said below
- basis: float32 [4096, 64, 128], P('leaf'), may hold values from -0.5 to 0.5
- transfer: float32 [8128, 64, 64], P('leaf'), may hold values from -0.75 to 0.75
- coupling: float32 [8128, 4, 64, 64], P('leaf'), may hold values from -1 to 1
- partners: int32 [8128, 4], P('leaf'), may hold values from 0 to 4095, as said below
- transfer_top: float32 [62, 64, 64], replicated, may hold values from -0.75 to 0.75
- coupling_top: float32 [60, 4, 64, 64], replicated, may hold values from -1 to 1
- partners_top: int32 [60, 4], replicated, may hold values from 0 to 31, as said below
Outputs:
- potential: float32 [64, 524288], P('rhs', 'leaf')
The draws below stay inside these ranges and needn't reach their ends.
Inputs may be any that keep to these rules, and one draw needn't show every extreme that they name: near_list[i, 0] = i; near_list[i, 1] = i - 1 where i > 0 is the first leaf of its subtree, and i + 1 where i < 4095 is the last leaf of its subtree; every entry names a leaf at most 64 positions from i. `near_count`: some leaf has 27 live slots. `partners`: a partner lies on its cluster's level, differs from it, and is at most 64 >> l positions from it on level l. `partners_top`: a partner lies on its cluster's level and differs from it.
All inputs are finite; a program needn't handle non-finite values.
Results may differ from the reference program's by a relative error of at most 0.0003.
Values sent between devices are 32-bit elements; how exact they have to be, the bound alone decides.
No kernel may reach another device: no remote copies, remote signals or barrier semaphores. Data moves between devices by JAX's collectives and lax.ppermute only.
A program may use at most 256 MiB of HBM per device.

```python
import jax
import jax.numpy as jnp
from jax import lax

LEAF = 128
RANK = 64
NRHS = 64
NEAR = 27
KC = 4
LEVELS_DEV = 6
LEAF_DEV = 64
LEAVES = 4096
NPTS = 524288
LOCN = 127
N_LEAF = 64


def subtree_nodes(devices, leaf_dev):
    node_parts = []
    width_parts = []
    span_width = leaf_dev
    while span_width >= 1:
        node_parts.append(jnp.arange(devices)[:, None] * span_width + jnp.arange(span_width)[None, :])
        width_parts.append(jnp.full((devices, span_width), span_width))
        span_width = span_width // 2
    return (jnp.concatenate(node_parts, axis=1), jnp.concatenate(width_parts, axis=1))


def scaled_entries(key, level_ids, rows):
    scales = jnp.exp2(-0.5 * level_ids) / jnp.sqrt(jnp.float32(KC * RANK))
    entries = jax.random.truncated_normal(key, -4.0, 4.0, (rows, KC, RANK, RANK), jnp.float32)
    return entries * scales[:, None, None, None]


def draw_near_list(key, part):
    key = jax.random.fold_in(key, 1)
    first_key, second_key = jax.random.split(key)
    distance = jax.random.randint(first_key, (LEAVES, NEAR), 0, LEAF_DEV + 1)
    direction = 2 * jax.random.randint(second_key, (LEAVES, NEAR), 0, 2) - 1
    offsets = (distance * direction).at[:, 0].set(0)
    leaf_ids = jnp.arange(LEAVES)[:, None]
    target = leaf_ids + offsets
    target = jnp.where((target < 0) | (target >= LEAVES), leaf_ids - offsets, target)
    flat_ids = jnp.arange(LEAVES)
    within = flat_ids % LEAF_DEV
    second = jnp.where((within == 0) & (flat_ids > 0), flat_ids - 1, jnp.where((within == LEAF_DEV - 1) & (flat_ids < LEAVES - 1), flat_ids + 1, target[:, 1]))
    target = target.at[:, 1].set(second)
    return target.astype(jnp.int32)


def draw_near_count(key, part):
    key = jax.random.fold_in(key, 2)
    devices = LEAVES // LEAF_DEV
    load_key, count_key, pick_key, busy_key = jax.random.split(key, 4)
    loads = jax.random.randint(load_key, (devices,), 2, NEAR + 1)
    busy = jax.random.randint(busy_key, (), 0, devices)
    device_ids = jnp.arange(devices)
    loads = jnp.where(device_ids == busy, NEAR, loads)
    loads = jnp.where(device_ids == (busy + 1) % devices, 2, loads)
    counts = jax.random.randint(count_key, (devices, LEAF_DEV), 2, loads[:, None] + 1)
    picked = jax.random.randint(pick_key, (devices,), 0, LEAF_DEV)
    counts = jnp.where(jnp.arange(LEAF_DEV)[None, :] == picked[:, None], loads[:, None], counts)
    return counts.reshape(LEAVES).astype(jnp.int32)


def draw_coupling(key, part):
    key = jax.random.fold_in(key, 5)
    devices = LEAVES // LEAF_DEV
    level_parts = []
    for level_id in range(LEVELS_DEV + 1):
        level_parts.append(jnp.full((LEAF_DEV >> level_id,), float(level_id), jnp.float32))
    level_ids = jnp.tile(jnp.concatenate(level_parts), devices)
    return scaled_entries(key, level_ids, LOCN * devices)


def draw_coupling_top(key, part):
    key = jax.random.fold_in(key, 6)
    devices = LEAVES // LEAF_DEV
    level_parts = []
    level_size = devices // 2
    level_id = LEVELS_DEV + 1
    while level_size >= 4:
        level_parts.append(jnp.full((level_size,), float(level_id), jnp.float32))
        level_size = level_size // 2
        level_id = level_id + 1
    level_ids = jnp.concatenate(level_parts)
    return scaled_entries(key, level_ids, devices - 4)


def draw_partners(key, part):
    key = jax.random.fold_in(key, 3)
    devices = LEAVES // LEAF_DEV
    node_ids, widths = subtree_nodes(devices, LEAF_DEV)
    node_ids = node_ids.reshape(-1, 1)
    widths = widths.reshape(-1, 1)
    first_key, second_key = jax.random.split(key)
    distance = jax.random.randint(first_key, (node_ids.shape[0], KC), 1, widths + 1)
    direction = 2 * jax.random.randint(second_key, (node_ids.shape[0], KC), 0, 2) - 1
    offsets = distance * direction
    level_size = devices * widths
    target = node_ids + offsets
    target = jnp.where((target < 0) | (target >= level_size), node_ids - offsets, target)
    return target.astype(jnp.int32)


def draw_partners_top(key, part):
    key = jax.random.fold_in(key, 4)
    devices = LEAVES // LEAF_DEV
    node_parts = []
    size_parts = []
    level_size = devices // 2
    while level_size >= 4:
        node_parts.append(jnp.arange(level_size))
        size_parts.append(jnp.full((level_size,), level_size))
        level_size = level_size // 2
    node_ids = jnp.concatenate(node_parts)[:, None]
    sizes_all = jnp.concatenate(size_parts)[:, None]
    offsets = jax.random.randint(key, (node_ids.shape[0], KC), 1, sizes_all)
    return ((node_ids + offsets) % sizes_all).astype(jnp.int32)


def level_of(rng, dims, cuts, low, top_value):
    def one(axis_at, shards_of):
        steps = jax.random.uniform(jax.random.fold_in(jax.random.fold_in(rng, 6), axis_at), (shards_of,), jnp.float32, low / len(cuts), top_value / len(cuts))
        return jnp.repeat(jnp.exp(steps), dims[axis_at] // shards_of).reshape((-1,) + (1,) * (len(dims) - axis_at - 1))

    level = one(*cuts[0])
    for cut in cuts[1:]:
        level = level * one(*cut)
    return level


def noise(key, extent, spread, most, cuts=(), kind=jnp.bfloat16):
    values = spread * jax.random.normal(key, extent, jnp.float32)
    if cuts:
        values = values * level_of(key, extent, cuts, -0.22, 0.18)
    return jnp.clip(values, -most, most).astype(kind)


def setup_inputs(seed: int = 0) -> dict:
    seeds = jax.random.split(jax.random.key(seed), 12)
    points = noise(seeds[0], (3, NPTS), 1.0, 6.0, ((1, 64),), jnp.float32)
    values = noise(seeds[1], (NRHS, NPTS), 1.0, 6.0, ((0, 2), (1, 64)), jnp.float32)
    near_list = draw_near_list(jax.random.fold_in(seeds[11], 71), 0)
    near_count = draw_near_count(jax.random.fold_in(seeds[11], 71), 0)
    basis = noise(seeds[4], (LEAVES, RANK, LEAF), LEAF ** -0.5, 0.5, ((0, 64),), jnp.float32)
    transfer = noise(seeds[5], (LOCN * N_LEAF, RANK, RANK), RANK ** -0.5, 0.75, ((0, 64),), jnp.float32)
    coupling = draw_coupling(jax.random.fold_in(seeds[11], 71), 0)
    partners = draw_partners(jax.random.fold_in(seeds[11], 71), 0)
    transfer_top = noise(seeds[8], (N_LEAF - 2, RANK, RANK), RANK ** -0.5, 0.75, (), jnp.float32)
    coupling_top = draw_coupling_top(jax.random.fold_in(seeds[11], 71), 0)
    partners_top = draw_partners_top(jax.random.fold_in(seeds[11], 71), 0)
    return {"points": points, "values": values, "near_list": near_list, "near_count": near_count, "basis": basis, "transfer": transfer, "coupling": coupling, "partners": partners, "transfer_top": transfer_top, "coupling_top": coupling_top, "partners_top": partners_top}


near_weight = 0.1
smoothing = 0.0025
highest = lax.Precision.HIGHEST

def block_kernel(targets, sources, counts):
    squared = jnp.zeros((targets.shape[1], sources.shape[2], targets.shape[2], sources.shape[3]), jnp.float32)
    for comp_id in range(3):
        differ = targets[comp_id][:, None, :, None] - sources[comp_id][:, :, None, :]
        squared = squared + differ * differ
    kernel = near_weight / jnp.sqrt(squared + smoothing)
    live_mask = (jnp.arange(sources.shape[2])[None, :] < counts[:, None]).astype(jnp.float32)
    kernel = kernel * live_mask[:, :, None, None]
    return jnp.einsum('gsab,cgsb->cga', kernel, sources[3:], precision=highest)

def near_field(sources, targets, near_lists, counts):
    leaf_total = near_lists.shape[0]
    group_size = min(8, leaf_total)
    blocks = leaf_total // group_size
    leaf_size = targets.shape[2]

    def one_block(pieces):
        return block_kernel(pieces[0], jnp.take(sources, pieces[1], axis=1), pieces[2])
    result = lax.map(one_block, (targets.reshape(3, blocks, group_size, leaf_size).transpose(1, 0, 2, 3), near_lists.reshape(blocks, group_size, near_lists.shape[1]), counts.reshape(blocks, group_size)))
    return result.transpose(1, 0, 2, 3).reshape(result.shape[1], leaf_total * leaf_size)

def lift_up(matrices, coeffs):
    return jnp.einsum('nrq,nrc->nqc', matrices, coeffs, precision=highest)

def pair_sum(coeffs):
    return coeffs[0::2] + coeffs[1::2]

def push_down(matrices, parents):
    repeat_by = matrices.shape[0] // parents.shape[0]
    return jnp.einsum('nrq,nqc->nrc', matrices, jnp.repeat(parents, repeat_by, axis=0), precision=highest)

def couple(matrices, indices, sources):
    result = jnp.zeros((indices.shape[0], sources.shape[1], sources.shape[2]), jnp.float32)
    for slot_id in range(indices.shape[1]):
        picked = jnp.take(sources, indices[:, slot_id], axis=0)
        result = result + jnp.einsum('nrq,nqc->nrc', matrices[:, slot_id], picked, precision=highest)
    return result

def upper_tree(first, transfer_top, coupling_top, partners_top):
    levels = [first]
    matrices = []
    used_rows = 0
    while levels[-1].shape[0] > 1:
        level_width = levels[-1].shape[0]
        chosen = transfer_top[used_rows:used_rows + level_width]
        used_rows = used_rows + level_width
        matrices.append(chosen)
        levels.append(pair_sum(lift_up(chosen, levels[-1])))
    offsets = []
    taken_rows = 0
    for coeffs in levels:
        offsets.append(taken_rows)
        if coeffs.shape[0] >= 4:
            taken_rows = taken_rows + coeffs.shape[0]
    parents = jnp.zeros_like(levels[-1])
    for section_id in range(len(levels) - 2, -1, -1):
        parents = push_down(matrices[section_id], parents)
        level_width = levels[section_id].shape[0]
        if level_width >= 4:
            begin_row = offsets[section_id]
            parents = parents + couple(coupling_top[begin_row:begin_row + level_width], partners_top[begin_row:begin_row + level_width], levels[section_id])
    return parents

def reference(points, values, near_list, near_count, basis, transfer, coupling, partners, transfer_top, coupling_top, partners_top):
    devices = LEAVES // LEAF_DEV
    sources = jnp.concatenate([points, values], axis=0).reshape(3 + NRHS, LEAVES, LEAF)
    near_part = near_field(sources, sources[:3], near_list, near_count)

    def level_rows(array, level_id):
        span_width = LEAF_DEV >> level_id
        begin_row = 2 * LEAF_DEV - 2 * span_width
        shaped = array.reshape((devices, LOCN) + array.shape[1:])
        return shaped[:, begin_row:begin_row + span_width].reshape((devices * span_width,) + array.shape[1:])
    coeffs = [jnp.einsum('irb,cib->irc', basis, values.reshape(NRHS, LEAVES, LEAF), precision=highest)]
    for level_id in range(LEVELS_DEV):
        coeffs.append(pair_sum(lift_up(level_rows(transfer, level_id), coeffs[-1])))
    first = pair_sum(lift_up(level_rows(transfer, LEVELS_DEV), coeffs[-1]))
    parents = upper_tree(first, transfer_top, coupling_top, partners_top)
    for level_id in range(LEVELS_DEV, -1, -1):
        parents = push_down(level_rows(transfer, level_id), parents) + couple(level_rows(coupling, level_id), level_rows(partners, level_id), coeffs[level_id])
    far_part = jnp.einsum('irb,irc->cib', basis, parents, precision=highest).reshape(NRHS, NPTS)
    return near_part + far_part
```

```python
import jax, jax.numpy as jnp, functools
from jax import lax
from jax.sharding import PartitionSpec as P
from jax.experimental import pallas as pl
from jax.experimental.pallas import tpu as pltpu
NT = (((1,), (1,)), ((), ()))
SM = pl.BlockSpec(memory_space=pltpu.SMEM)
VM = pl.BlockSpec(memory_space=pltpu.VMEM)
f32 = jnp.float32
bf16 = jnp.bfloat16

def split(x):
    hi = x.astype(bf16)
    return hi, (x - hi.astype(f32)).astype(bf16)

def stack(x):
    hi, lo = split(x)
    return jnp.concatenate([hi, lo], axis=0)

def fold(x):
    half = x.shape[0] // 2
    return x[:half] + x[half:]

def both(x):
    return x + pltpu.roll(x, 64, 1)

def low_lanes(shape):
    return lax.broadcasted_iota(jnp.int32, shape, 1) < 64

def up_body(basis, values, moves, up, top, trans, rows):
    leaves = basis.shape[0]
    columns = values.shape[0]
    nodes = moves.shape[2]
    @pl.loop(0, 64, unroll=4)
    def _(r):
        block = jnp.transpose(moves[r])
        rows[r, 0:nodes] = jnp.concatenate([block, block], axis=1)
    left = low_lanes((64, 128))
    @pl.loop(0, nodes, unroll=4)
    def _(n):
        x = rows[:, n, :]
        hi = x.astype(bf16).astype(f32)
        trans[n] = jnp.where(left, hi, x - hi).astype(bf16)
    half = low_lanes((columns, 128))
    def leaf_up(i):
        v = stack(values[:, pl.ds(pl.multiple_of(i * 128, 128), 128)])
        return both(fold(lax.dot_general(v, stack(basis[i]), NT, preferred_element_type=f32)))
    @pl.loop(0, leaves // 2, unroll=4)
    def _(p):
        up[p] = jnp.where(half, leaf_up(2 * p), leaf_up(2 * p + 1))
    def lift(tile, row):
        t = jnp.concatenate([trans[row], trans[row + 1]], axis=0)
        return both(fold(jnp.dot(stack(up[tile]), t, preferred_element_type=f32)))
    tile0, row0, width = 0, 0, leaves
    while width > 1:
        nxt = tile0 + width // 2
        if width >= 4:
            @pl.loop(0, width // 4, unroll=min(4, width // 4))
            def _(p, tile0=tile0, row0=row0, nxt=nxt):
                up[nxt + p] = jnp.where(half, lift(tile0 + 2 * p, row0 + 4 * p), lift(tile0 + 2 * p + 1, row0 + 4 * p + 2))
        else:
            up[nxt] = lift(tile0, row0)
        tile0, row0, width = nxt, row0 + width, width // 2
    top[...] = both(fold(jnp.dot(stack(up[tile0])[:, 0:64], trans[row0], preferred_element_type=f32)))

def up_pass(basis, values, moves):
    leaves, rank, size = basis.shape
    columns = values.shape[0]
    nodes = moves.shape[2]
    return pl.pallas_call(
        up_body,
        out_shape=(
            jax.ShapeDtypeStruct((leaves, columns, 128), f32),
            jax.ShapeDtypeStruct((columns, 128), f32),
            jax.ShapeDtypeStruct((nodes + 1, 64, 128), bf16),
        ),
        in_specs=[VM, VM, VM],
        out_specs=(VM, VM, VM),
        scratch_shapes=[pltpu.VMEM((64, 128, 128), f32)],
        compiler_params=pltpu.CompilerParams(vmem_limit_bytes=32 << 20),
        cost_estimate=pl.CostEstimate(flops=400_000_000, bytes_accessed=8_000_000, transcendentals=0),
        name="up_pass",
    )(basis, values, moves)

def unbatch_body(matrices, out, rows):
    nodes = matrices.shape[3]
    @pl.loop(0, 64, unroll=2)
    def _(r):
        for h in range(2):
            x = jnp.concatenate([matrices[2 * h, r], matrices[2 * h + 1, r]], axis=0)
            rows[h, r, 0:nodes] = jnp.transpose(x)
    @pl.loop(0, nodes, unroll=2)
    def _(n):
        for h in range(2):
            hi, lo = split(rows[h, :, n, :])
            out[n, 0:64, 128 * h : 128 * h + 128] = hi
            out[n, 64:128, 128 * h : 128 * h + 128] = lo

def unbatch(matrices):
    nodes = matrices.shape[3]
    return pl.pallas_call(
        unbatch_body,
        out_shape=jax.ShapeDtypeStruct((nodes, 128, 256), bf16),
        in_specs=[VM],
        out_specs=VM,
        scratch_shapes=[pltpu.VMEM((2, 64, 128, 128), f32)],
        compiler_params=pltpu.CompilerParams(vmem_limit_bytes=40 << 20),
        cost_estimate=pl.CostEstimate(flops=100_000_000, bytes_accessed=17_000_000, transcendentals=0),
        name="unbatch",
    )(matrices)

def top_body(place, partners, first, moves, matrices, parent, up, block, sem):
    spot = place[0]
    columns = first.shape[1]
    copies = []
    width, row = 32, 0
    for level in range(4):
        index = row + spot // (2 << level)
        copies.append(pltpu.make_async_copy(matrices.at[index], block.at[level], sem.at[level]))
        copies[-1].start()
        row, width = row + width, width // 2
    half = low_lanes((columns, 128))
    up[0:16] = first[...]
    def lift(tile, r):
        t = jnp.concatenate([moves[r], moves[r + 1]], axis=0)
        hi, lo = split(t)
        x = stack(up[tile])
        z = fold(jnp.dot(x, hi, preferred_element_type=f32)) + jnp.dot(x[:columns], lo, preferred_element_type=f32)
        return jnp.concatenate([z, z], axis=1)
    tile0, row, width = 0, 0, 32
    tiles, rows = [], []
    while width >= 4:
        tiles.append(tile0)
        rows.append(row)
        nxt = tile0 + width // 2
        if width > 4:
            for p in range(width // 4):
                up[nxt + p] = jnp.where(half, lift(tile0 + 2 * p, row + 4 * p), lift(tile0 + 2 * p + 1, row + 4 * p + 2))
        tile0, row, width = nxt, row + width, width // 2
    def push(d, r):
        hi, lo = split(moves[r])
        x = stack(d)
        return fold(lax.dot_general(x, hi, NT, preferred_element_type=f32)) + lax.dot_general(x[:columns], lo, NT, preferred_element_type=f32)
    down = jnp.zeros((columns, 64), f32)
    down = push(down, row + spot // 32)
    for level in range(3, -1, -1):
        index = rows[level] + spot // (2 << level)
        down = push(down, index)
        copies[level].wait()
        for k in range(4):
            p = partners[index * 4 + k]
            tile = up[tiles[level] + p // 2]
            x = stack(jnp.where(p % 2 == 0, tile, pltpu.roll(tile, 64, 1))[:, 0:64])
            hi, lo = split(block[level, k])
            down = down + fold(lax.dot_general(x, hi, NT, preferred_element_type=f32)) + lax.dot_general(x[:columns], lo, NT, preferred_element_type=f32)
    parent[...] = jnp.concatenate([down, down], axis=1)

def top_pass(place, partners, first, moves, matrices):
    columns = first.shape[1]
    return pl.pallas_call(
        top_body,
        out_shape=jax.ShapeDtypeStruct((columns, 128), f32),
        in_specs=[SM, SM, VM, VM, pl.BlockSpec(memory_space=pl.ANY)],
        out_specs=VM,
        scratch_shapes=[pltpu.VMEM((32, columns, 128), f32), pltpu.VMEM((4, 4, 64, 64), f32), pltpu.SemaphoreType.DMA((4,))],
        compiler_params=pltpu.CompilerParams(vmem_limit_bytes=16 << 20),
        cost_estimate=pl.CostEstimate(flops=50_000_000, bytes_accessed=2_000_000, transcendentals=0),
        name="top_pass",
    )(place, partners, first, moves, matrices)

def tail_body(core, partners, low, own, high, parent, matrices, trans, basis, near_a, near_b, out, gather, far, down):
    leaves = basis.shape[0]
    columns = out.shape[0]
    nodes = matrices.shape[0]
    half = low_lanes((columns, 128))
    for side, ref in enumerate((low, own, high)):
        @pl.loop(0, leaves, unroll=4)
        def _(t, side=side, ref=ref):
            x = ref[t]
            gather[0, side * leaves + t] = stack(x)
            gather[1, side * leaves + t] = stack(pltpu.roll(x, 64, 1))
    left = low_lanes((2 * columns, 128))
    def pick(n, k, side):
        code = partners[4 * n + k]
        return gather[(code & 1) ^ side, code >> 1]
    @pl.loop(0, nodes, unroll=4)
    def _(n):
        x = jnp.concatenate(
            [jnp.where(left, pick(n, 0, 0), pick(n, 1, 1)), jnp.where(left, pick(n, 2, 0), pick(n, 3, 1))], axis=1)
        far[n] = both(fold(lax.dot_general(x, matrices[n], NT, preferred_element_type=f32)))
    def push(d, n):
        t = trans[n]
        return fold(lax.dot_general(stack(d), jnp.concatenate([t, t], axis=0), NT, preferred_element_type=f32)) + far[n]
    row = nodes - 1
    down[row] = push(parent[...], row)
    width = 2
    while width <= leaves:
        begin = row - width
        if begin < 0:
            break
        @pl.loop(0, width, unroll=min(8, width))
        def _(i, begin=begin, row=row):
            down[begin + i] = push(down[row + i // 2], begin + i)
        row, width = begin, 2 * width
    @pl.loop(0, leaves, unroll=4)
    def _(i):
        at = pl.ds(pl.multiple_of(i * 128, 128), 128)
        out[:, at] = fold(jnp.dot(stack(down[i]), stack(basis[i]), preferred_element_type=f32))
    width = near_a.shape[1]
    out[:, pl.ds(pl.multiple_of(core[0] * width, width), width)] += near_a[...]
    out[:, pl.ds(pl.multiple_of((1 - core[0]) * width, width), width)] += near_b[...]

def tail(core, partners, low, own, high, parent, matrices, trans, basis, near_a, near_b):
    leaves = basis.shape[0]
    columns = own.shape[1]
    nodes = matrices.shape[0]
    return pl.pallas_call(
        tail_body,
        out_shape=jax.ShapeDtypeStruct((columns, leaves * 128), f32),
        in_specs=[SM, SM] + [VM] * 9,
        out_specs=VM,
        scratch_shapes=[pltpu.VMEM((2, 3 * leaves, 2 * columns, 128), bf16), pltpu.VMEM((nodes, columns, 128), f32), pltpu.VMEM((nodes, columns, 128), f32)],
        compiler_params=pltpu.CompilerParams(vmem_limit_bytes=50 << 20),
        cost_estimate=pl.CostEstimate(flops=400_000_000, bytes_accessed=20_000_000, transcendentals=0),
        name="tail",
    )(core, partners, low, own, high, parent, matrices, trans, basis, near_a, near_b)

near_weight = 0.1
smoothing = 0.0025
SLOTS = 28
PAIR = 2


def near_body(unroll, kinds, lists, counts, targets, *refs):
    sources = refs[:kinds]
    refs = refs[kinds:]
    begin = refs[0] if kinds == 4 else None
    if kinds == 4:
        refs = refs[1:]
    mine, other, columns_of, total, first, second, weights, places = refs
    leaves = mine.shape[1] // 128
    width = sources[0].shape[1] // 128
    chunks = kinds // 2
    for c in range(chunks):
        near_ref, far_ref = sources[2 * c], sources[2 * c + 1]

        @pl.loop(0, width, unroll=4)
        def _(j, c=c, near_ref=near_ref, far_ref=far_ref):
            at = pl.ds(pl.multiple_of(j * 128, 128), 128)
            x = near_weight * jnp.concatenate([near_ref[0:32, at], far_ref[0:32, at]], axis=0)
            weights[c * width + j] = stack(x)
            places[c * width + j, 0:3] = near_ref[32:35, at] if chunks == 2 else targets[:, at]

    weights[chunks * width] = jnp.zeros(weights.shape[1:], bf16)
    places[chunks * width] = jnp.zeros(places.shape[1:], f32)
    offset = counts[leaves] * leaves

    @pl.loop(0, leaves, unroll=4)
    def _(leaf):
        at = pl.ds(pl.multiple_of((offset + leaf) * 128, 128), 128)
        row = jnp.concatenate([targets[:, at], jnp.zeros((5, 128), f32)], axis=0)
        t = jnp.transpose(row)
        for c in range(3):
            columns_of[leaf, c] = jnp.broadcast_to(t[:, c : c + 1], (128, 128))
        total[leaf] = jnp.zeros((128, 128), f32)

    items = lax.fori_loop(
        0, leaves, lambda i, s: s + jnp.maximum((counts[i] + PAIR - 1) // PAIR, 1), jnp.int32(0)
    )

    def make(buf, leaf, slot):
        for u in range(PAIR):
            s = places[lists[leaf * SLOTS + slot + u]]
            for r in range(0, 128, 32):
                d = columns_of[leaf, 0, r : r + 32] - s[0:1]
                squared = d * d + smoothing
                d = columns_of[leaf, 1, r : r + 32] - s[1:2]
                squared = squared + d * d
                d = columns_of[leaf, 2, r : r + 32] - s[2:3]
                squared = squared + d * d
                hi, lo = split(lax.rsqrt(squared))
                buf[r : r + 32, u * 256 : u * 256 + 128] = hi
                buf[r : r + 32, u * 256 + 128 : u * 256 + 256] = lo

    def use(buf, leaf, slot):
        parts = []
        for u in range(PAIR):
            x = weights[lists[leaf * SLOTS + slot + u]]
            parts += [x, x]
        total[leaf] += lax.dot_general(
            buf[...], jnp.concatenate(parts, axis=1), NT, preferred_element_type=f32
        )

    def take(leaf, slot):
        found = []
        for u in range(unroll):
            found += [leaf, slot]
            done = slot + PAIR >= counts[leaf]
            leaf = jnp.where(done, jnp.minimum(leaf + 1, leaves - 1), leaf)
            slot = jnp.where(done, 0, slot + PAIR)
        return found, leaf, slot

    def half(carry, source, dest):
        found, leaf, slot = take(carry[-2], carry[-1])
        for u in range(unroll):
            use(source.at[u], carry[2 * u], carry[2 * u + 1])
            make(dest.at[u], found[2 * u], found[2 * u + 1])
        return (*found, leaf, slot)

    def finish(buf, carry, start):
        for u in range(unroll):

            @pl.when(start * unroll + u < items)
            def _(u=u):
                use(buf.at[u], carry[2 * u], carry[2 * u + 1])

    found, leaf, slot = take(jnp.int32(0), jnp.int32(0))
    for u in range(unroll):
        make(first.at[u], found[2 * u], found[2 * u + 1])
    batches = (items + unroll - 1) // unroll
    steps = (batches - 1) // 2
    carry = lax.fori_loop(
        0, steps, lambda b, c: half(half(c, first, second), second, first), (*found, leaf, slot)
    )

    @pl.when(batches - 1 == 2 * steps)
    def _():
        finish(first, carry, 2 * steps)

    @pl.when(batches - 1 > 2 * steps)
    def _():
        finish(second, half(carry, first, second), 2 * steps + 1)

    @pl.loop(0, leaves, unroll=4)
    def _(leaf):
        at = pl.ds(pl.multiple_of(leaf * 128, 128), 128)
        x = jnp.transpose(both(total[leaf]))
        if begin is None:
            mine[:, at] = x[0:32]
            other[:, at] = x[32:64]
        else:
            mine[:, at] = begin[0:32, at] + x[0:32]
            other[:, at] = begin[32:64, at] + x[32:64]


def near_pass(unroll, lists, counts, targets, sources, begin=None):
    leaves = lists.shape[0] // SLOTS
    held = 64 * (len(sources) // 2) + 1
    side = jax.ShapeDtypeStruct((32, leaves * 128), f32)
    extra = [] if begin is None else list(begin)
    if begin is not None:
        extra = [jnp.concatenate(begin, axis=0)]
    return pl.pallas_call(
        functools.partial(near_body, unroll, len(sources)),
        out_shape=(side, side),
        in_specs=[SM, SM] + [VM] * (1 + len(sources) + len(extra)),
        out_specs=(VM, VM),
        scratch_shapes=[
            pltpu.VMEM((leaves, 3, 128, 128), f32),
            pltpu.VMEM((leaves, 128, 128), f32),
            pltpu.VMEM((unroll, 128, PAIR * 256), bf16),
            pltpu.VMEM((unroll, 128, PAIR * 256), bf16),
            pltpu.VMEM((held, 128, 128), bf16),
            pltpu.VMEM((held, 8, 128), f32),
        ],
        compiler_params=pltpu.CompilerParams(vmem_limit_bytes=40 << 20),
        cost_estimate=pl.CostEstimate(flops=16_000_000_000, bytes_accessed=8_000_000, transcendentals=8_000_000),
        name="near_pass",
    )(lists, counts, targets, *sources, *extra)


def arranged(picked, leaf_ids, empty):
    slots = picked.shape[1]
    before = jnp.arange(slots)[:, None] < jnp.arange(slots)[None, :]
    rank = jnp.sum(jnp.where(picked[:, :, None] & before[None], 1, 0), axis=1)
    to = jnp.arange(SLOTS)[None, None, :]
    here = picked[:, :, None] & (rank[:, :, None] == to)
    found = jnp.sum(jnp.where(here, leaf_ids[:, :, None], 0), axis=1)
    count = jnp.sum(picked.astype(jnp.int32), axis=1)
    lists = jnp.where(jnp.arange(SLOTS)[None, :] < count[:, None], found, empty)
    return lists.astype(jnp.int32).reshape(-1), count


def partner_codes(partners, position, leaves):
    spans, starts = [], []
    width, tile = leaves, 0
    while width >= 1:
        spans += [width] * width
        starts += [2 * tile] * width
        tile, width = tile + max(1, width // 2), width // 2
    spans = jnp.array(spans, jnp.int32)[:, None]
    starts = jnp.array(starts, jnp.int32)[:, None]
    local = partners - position * spans
    side = jnp.where(local < 0, 0, jnp.where(local < spans, 1, 2))
    return (side * (2 * leaves) + starts + local - (side - 1) * spans).reshape(-1)


def local(
    points,
    values,
    near_list,
    near_count,
    basis,
    transfer,
    coupling,
    partners,
    transfer_top,
    coupling_top,
    partners_top,
):
    leaves = basis.shape[0]
    position = lax.axis_index("leaf")
    core = lax.axis_index("rhs")
    count = lax.axis_size("leaf")
    forward = [(i, i + 1) for i in range(count - 1)]
    backward = [(target, source) for source, target in forward]
    swap = [(0, 1), (1, 0)]
    packed = jnp.concatenate([values, points], axis=0)
    low = lax.ppermute(packed, "leaf", forward)
    high = lax.ppermute(packed, "leaf", backward)
    across = lax.ppermute(values, "rhs", swap)

    half = leaves // 2
    chosen = lax.dynamic_slice_in_dim(near_list, core * half, half, 0) - position * leaves
    live = lax.dynamic_slice_in_dim(near_count, core * half, half, 0)
    alive = jnp.arange(chosen.shape[1])[None, :] < live[:, None]
    inside = (chosen >= 0) & (chosen < leaves)
    near_ids, near_live = arranged(alive & inside, chosen, leaves)
    outside_ids = jnp.where(chosen < 0, chosen + leaves, chosen)
    far_ids, far_live = arranged(alive & ~inside, outside_ids, 2 * leaves)
    near_live = jnp.concatenate([near_live, core[None]]).astype(jnp.int32)
    far_live = jnp.concatenate([far_live, core[None]]).astype(jnp.int32)
    codes = partner_codes(partners, position, leaves)

    up, top, trans = up_pass(basis, values, transfer.transpose(1, 2, 0))
    up_low = lax.ppermute(up, "leaf", forward)
    up_high = lax.ppermute(up, "leaf", backward)

    def exchange(x, bit):
        return lax.ppermute(x, "leaf", [(i, i ^ (1 << bit)) for i in range(count)])

    def ordered(x, y, bit, axis):
        return jnp.where((position >> bit) & 1 == 0, jnp.concatenate([x, y], axis), jnp.concatenate([y, x], axis))

    level = top + exchange(top, 0)
    level = ordered(level[:, 0:64], exchange(level, 1)[:, 0:64], 1, 1)[None]
    for bit in range(2, count.bit_length() - 1):
        level = ordered(level, exchange(level, bit), bit, 0)

    begin = near_pass(4, near_ids, near_live, points, (values, across))
    matrices = unbatch(coupling.transpose(1, 2, 3, 0))
    parent = top_pass(position[None].astype(jnp.int32), partners_top.reshape(-1), level, transfer_top, coupling_top)
    low_across = lax.ppermute(low, "rhs", swap)
    high_across = lax.ppermute(high, "rhs", swap)
    mine, other = near_pass(4, far_ids, far_live, points, (low, low_across, high, high_across), begin)
    given = lax.ppermute(other, "rhs", swap)
    return tail(core[None].astype(jnp.int32), codes, up_low, up, up_high, parent, matrices, trans, basis, mine, given)


def solution(mesh):
    placed = (
        P(None, "leaf"),
        P("rhs", "leaf"),
        P("leaf", None),
        P("leaf"),
        P("leaf", None, None),
        P("leaf", None, None),
        P("leaf", None, None, None),
        P("leaf", None),
        P(),
        P(),
        P(),
    )
    return jax.shard_map(
        local, mesh=mesh, in_specs=placed, out_specs=P("rhs", "leaf"), check_vma=False
    )
```

```python
import jax, jax.numpy as jnp, functools
from jax import lax
from jax.sharding import PartitionSpec as P
from jax.experimental import pallas as pl
from jax.experimental.pallas import tpu as pltpu
NT = (((1,), (1,)), ((), ()))
SM = pl.BlockSpec(memory_space=pltpu.SMEM)
VM = pl.BlockSpec(memory_space=pltpu.VMEM)
ANY = pl.BlockSpec(memory_space=pl.ANY)
PITCH = 136
f32 = jnp.float32
bf16 = jnp.bfloat16

def split(x):
    hi = x.astype(bf16)
    return hi, (x - hi.astype(f32)).astype(bf16)

def stack(x):
    hi, lo = split(x)
    return jnp.concatenate([hi, lo], axis=0)

def fold(x):
    half = x.shape[0] // 2
    return x[:half] + x[half:]

def both(x):
    return x + pltpu.roll(x, 64, 1)

def low_lanes(shape):
    return lax.broadcasted_iota(jnp.int32, shape, 1) < 64

def up_body(basis, values, moves, up, trans, rows):
    leaves = basis.shape[0]
    columns = values.shape[0]
    nodes = moves.shape[2]

    @pl.loop(0, 64, unroll=4)
    def _(r):
        block = jnp.transpose(moves[r])
        rows[pl.ds(pl.multiple_of(r * PITCH, 8), nodes)] = jnp.concatenate([block, block], axis=1)

    left = low_lanes((64, 128))

    @pl.loop(0, nodes, unroll=4)
    def _(n):
        x = rows[pl.ds(n, 64, stride=PITCH), :]
        hi = x.astype(bf16).astype(f32)
        trans[n] = jnp.where(left, hi, x - hi).astype(bf16)

    half = low_lanes((columns, 128))

    def leaf_up(i):
        v = stack(values[:, pl.ds(pl.multiple_of(i * 128, 128), 128)])
        return both(fold(lax.dot_general(v, stack(basis[i]), NT, preferred_element_type=f32)))

    @pl.loop(0, leaves // 2, unroll=4)
    def _(p):
        up[p] = jnp.where(half, leaf_up(2 * p), leaf_up(2 * p + 1))

    def lift(tile, row):
        t = jnp.concatenate([trans[row], trans[row + 1]], axis=0)
        return both(fold(jnp.dot(stack(tile), t, preferred_element_type=f32)))

    def pair(tile_a, tile_b, row):
        return jnp.where(half, lift(tile_a, row), lift(tile_b, row + 2))

    start, row, width = 0, 0, leaves
    while width > 16:
        after = start + width // 2

        @pl.loop(0, width // 16)
        def _(g, start=start, row=row, after=after):
            made = []
            for p in range(4):
                q = 4 * g + p
                made.append(pair(up[start + 2 * q], up[start + 2 * q + 1], row + 4 * q))
            for p in range(4):
                up[after + 4 * g + p] = made[p]

        start, row, width = after, row + width, width // 2
    tiles = [up[start + p] for p in range(width // 2)]
    while width > 1:
        after = start + width // 2
        if width >= 4:
            tiles = [pair(tiles[2 * p], tiles[2 * p + 1], row + 4 * p) for p in range(width // 4)]
        else:
            tiles = [lift(tiles[0], row)]
        if after < leaves - 1:
            for p, tile in enumerate(tiles):
                up[after + p] = tile
        start, row, width = after, row + width, width // 2
    share = both(fold(jnp.dot(stack(tiles[0])[:, 0:64], trans[row], preferred_element_type=f32)))
    up[leaves - 1] = jnp.where(half, tiles[0], share)


def up_pass(basis, values, moves):
    leaves = basis.shape[0]
    columns = values.shape[0]
    nodes = moves.shape[2]
    return pl.pallas_call(
        up_body,
        out_shape=(
            jax.ShapeDtypeStruct((leaves, columns, 128), f32),
            jax.ShapeDtypeStruct((nodes + 1, 64, 128), bf16),
        ),
        in_specs=[VM, VM, VM],
        out_specs=(VM, VM),
        scratch_shapes=[pltpu.VMEM((64 * PITCH, 128), f32)],
        compiler_params=pltpu.CompilerParams(vmem_limit_bytes=24 << 20),
        cost_estimate=pl.CostEstimate(flops=400_000_000, bytes_accessed=8_000_000, transcendentals=0),
        name="up_pass",
    )(basis, values, moves)


CHUNK = 16


def unbatch_body(matrices, out, held, rows, made, in_sem, out_sem):
    nodes = matrices.shape[3]
    reads = [pltpu.make_async_copy(matrices.at[k], held.at[k], in_sem.at[k]) for k in range(4)]
    for read in reads:
        read.start()
    for h in range(2):
        reads[2 * h].wait()
        reads[2 * h + 1].wait()

        @pl.loop(0, 64, unroll=4)
        def _(r, h=h):
            x = jnp.concatenate([held[2 * h, r], held[2 * h + 1, r]], axis=0)
            rows[pl.ds(pl.multiple_of((h * 64 + r) * PITCH, 8), nodes)] = jnp.transpose(x)

    writes = []
    for begin in range(0, nodes, CHUNK):
        size = min(CHUNK, nodes - begin)

        def one(n):
            for h in range(2):
                hi, lo = split(rows[pl.ds(h * 64 * PITCH + n, 64, stride=PITCH), :])
                made[n, 0:64, 128 * h : 128 * h + 128] = hi
                made[n, 64:128, 128 * h : 128 * h + 128] = lo

        if size == CHUNK:
            pl.loop(begin, begin + size, unroll=4)(one)
        else:
            for n in range(begin, begin + size):
                one(n)
        at = pl.ds(begin, size)
        writes.append(pltpu.make_async_copy(made.at[at], out.at[at], out_sem.at[begin // CHUNK]))
        writes[-1].start()
    for write in writes:
        write.wait()


def unbatch(matrices):
    nodes = matrices.shape[3]
    return pl.pallas_call(
        unbatch_body,
        out_shape=jax.ShapeDtypeStruct((nodes, 128, 256), bf16),
        in_specs=[ANY],
        out_specs=ANY,
        scratch_shapes=[
            pltpu.VMEM(matrices.shape, f32),
            pltpu.VMEM((2 * 64 * PITCH, 128), f32),
            pltpu.VMEM((nodes, 128, 256), bf16),
            pltpu.SemaphoreType.DMA((4,)),
            pltpu.SemaphoreType.DMA((-(-nodes // CHUNK),)),
        ],
        compiler_params=pltpu.CompilerParams(vmem_limit_bytes=36 << 20),
        cost_estimate=pl.CostEstimate(flops=100_000_000, bytes_accessed=17_000_000, transcendentals=0),
        name="unbatch",
    )(matrices)


def top_body(place, partners, first, moves, matrices, parent, up, block, sem):
    spot = place[0]
    columns = first.shape[1]
    copies = []
    width, row = 32, 0
    for level in range(4):
        index = row + spot // (2 << level)
        copies.append(pltpu.make_async_copy(matrices.at[index], block.at[level], sem.at[level]))
        copies[-1].start()
        row, width = row + width, width // 2
    half = low_lanes((columns, 128))
    up[0:16] = first[...]
    def lift(tile, r):
        t = jnp.concatenate([moves[r], moves[r + 1]], axis=0)
        hi, lo = split(t)
        x = stack(up[tile])
        z = fold(jnp.dot(x, hi, preferred_element_type=f32)) + jnp.dot(x[:columns], lo, preferred_element_type=f32)
        return jnp.concatenate([z, z], axis=1)
    tile0, row, width = 0, 0, 32
    tiles, rows = [], []
    while width >= 4:
        tiles.append(tile0)
        rows.append(row)
        nxt = tile0 + width // 2
        if width > 4:
            for p in range(width // 4):
                up[nxt + p] = jnp.where(half, lift(tile0 + 2 * p, row + 4 * p), lift(tile0 + 2 * p + 1, row + 4 * p + 2))
        tile0, row, width = nxt, row + width, width // 2
    def push(d, r):
        hi, lo = split(moves[r])
        x = stack(d)
        return fold(lax.dot_general(x, hi, NT, preferred_element_type=f32)) + lax.dot_general(x[:columns], lo, NT, preferred_element_type=f32)
    down = jnp.zeros((columns, 64), f32)
    down = push(down, row + spot // 32)
    for level in range(3, -1, -1):
        index = rows[level] + spot // (2 << level)
        down = push(down, index)
        copies[level].wait()
        for k in range(4):
            p = partners[index * 4 + k]
            tile = up[tiles[level] + p // 2]
            x = stack(jnp.where(p % 2 == 0, tile, pltpu.roll(tile, 64, 1))[:, 0:64])
            hi, lo = split(block[level, k])
            down = down + fold(lax.dot_general(x, hi, NT, preferred_element_type=f32)) + lax.dot_general(x[:columns], lo, NT, preferred_element_type=f32)
    parent[...] = jnp.concatenate([down, down], axis=1)

def top_pass(place, partners, first, moves, matrices):
    columns = first.shape[1]
    return pl.pallas_call(
        top_body,
        out_shape=jax.ShapeDtypeStruct((columns, 128), f32),
        in_specs=[SM, SM, VM, VM, pl.BlockSpec(memory_space=pl.ANY)],
        out_specs=VM,
        scratch_shapes=[pltpu.VMEM((32, columns, 128), f32), pltpu.VMEM((4, 4, 64, 64), f32), pltpu.SemaphoreType.DMA((4,))],
        compiler_params=pltpu.CompilerParams(vmem_limit_bytes=16 << 20),
        cost_estimate=pl.CostEstimate(flops=50_000_000, bytes_accessed=2_000_000, transcendentals=0),
        name="top_pass",
    )(place, partners, first, moves, matrices)


def couple_body(codes, low, own, high, matrices, far, gather, held, sem):
    leaves = own.shape[0]
    columns = own.shape[1]
    nodes = matrices.shape[0]
    read = pltpu.make_async_copy(matrices, held, sem)
    read.start()
    half = low_lanes((columns, 128))
    left = low_lanes((2 * columns, 128))
    for side, ref in enumerate((low, own, high)):

        @pl.loop(0, leaves, unroll=16)
        def _(t, side=side, ref=ref):
            x = ref[t]
            gather[0, side * leaves + t] = stack(x)
            gather[1, side * leaves + t] = stack(pltpu.roll(x, 64, 1))

    read.wait()

    def pick(n, k, side):
        code = codes[4 * n + k]
        return gather[(code & 1) ^ side, code >> 1]

    def one(n):
        x = jnp.concatenate(
            [
                jnp.where(left, pick(n, 0, 0), pick(n, 1, 1)),
                jnp.where(left, pick(n, 2, 0), pick(n, 3, 1)),
            ],
            axis=1,
        )
        return both(fold(lax.dot_general(x, held[n], NT, preferred_element_type=f32)))

    @pl.loop(0, leaves - 1, unroll=7)
    def _(t):
        far[t] = jnp.where(half, one(2 * t), one(2 * t + 1))

    far[leaves - 1] = one(nodes - 1)


def couple_pass(codes, low, own, high, matrices):
    leaves, columns, _ = own.shape
    return pl.pallas_call(
        couple_body,
        out_shape=jax.ShapeDtypeStruct((leaves, columns, 128), f32),
        in_specs=[SM, VM, VM, VM, ANY],
        out_specs=VM,
        scratch_shapes=[
            pltpu.VMEM((2, 3 * leaves, 2 * columns, 128), bf16),
            pltpu.VMEM(matrices.shape, bf16),
            pltpu.SemaphoreType.DMA,
        ],
        compiler_params=pltpu.CompilerParams(vmem_limit_bytes=28 << 20),
        cost_estimate=pl.CostEstimate(flops=400_000_000, bytes_accessed=12_000_000, transcendentals=0),
        name="couple_pass",
    )(codes, low, own, high, matrices)


def down_body(core, parent, far, trans, basis, mine, given, out, held):
    leaves = basis.shape[0]
    columns = out.shape[0]
    half = low_lanes((columns, 128))

    def push(d, row, tile):
        t = jnp.concatenate([trans[row], trans[row + 1]], axis=0)
        return fold(lax.dot_general(stack(d), t, NT, preferred_element_type=f32)) + far[tile]

    def spread(tile):
        turned = pltpu.roll(tile, 64, 1)
        return jnp.where(half, tile, turned), jnp.where(half, turned, tile)

    last = leaves - 1
    t = trans[2 * last]
    d = fold(
        lax.dot_general(
            stack(parent[...]), jnp.concatenate([t, t], axis=0), NT, preferred_element_type=f32
        )
    )
    sources = [d + far[last]]
    start, width = last, 1
    while width < 16:
        start = start - max(1, width)
        made = [push(d, 2 * (start + i), start + i) for i, d in enumerate(sources)]
        sources = [d for tile in made for d in spread(tile)]
        width = 2 * width
    for i, tile in enumerate(made):
        held[i] = tile
    first = start - width

    @pl.loop(0, len(made), unroll=2)
    def _(i):
        results = []
        for j, d in enumerate(spread(held[i])):
            above = 2 * i + j
            for u, e in enumerate(spread(push(d, 2 * (first + above), first + above))):
                tile = 2 * above + u
                for w, x in enumerate(spread(push(e, 2 * tile, tile))):
                    leaf = 2 * tile + w
                    results.append(
                        (leaf, fold(jnp.dot(stack(x), stack(basis[leaf]), preferred_element_type=f32)))
                    )
        for leaf, x in results:
            out[:, pl.ds(pl.multiple_of(leaf * 128, 128), 128)] = x

    size = mine.shape[1]
    out[:, pl.ds(pl.multiple_of(core[0] * size, size), size)] += mine[...]
    out[:, pl.ds(pl.multiple_of((1 - core[0]) * size, size), size)] += given[...]


def down_pass(core, parent, far, trans, basis, mine, given):
    leaves = basis.shape[0]
    columns = parent.shape[0]
    return pl.pallas_call(
        down_body,
        out_shape=jax.ShapeDtypeStruct((columns, leaves * 128), f32),
        in_specs=[SM] + [VM] * 6,
        out_specs=VM,
        scratch_shapes=[pltpu.VMEM((8, columns, 128), f32)],
        compiler_params=pltpu.CompilerParams(vmem_limit_bytes=20 << 20),
        cost_estimate=pl.CostEstimate(flops=200_000_000, bytes_accessed=7_000_000, transcendentals=0),
        name="down_pass",
    )(core, parent, far, trans, basis, mine, given)


near_weight = 0.1
smoothing = 0.0025
SLOTS = 28
PAIR = 2

def near_body(unroll, kinds, lists, counts, targets, *refs):
    sources, refs = refs[:kinds], refs[kinds:]
    begin = None
    if kinds == 4:
        begin, refs = refs[0], refs[1:]
    mine, other, columns_of, total, weights, places = refs
    leaves = mine.shape[1] // 128
    width = sources[0].shape[1] // 128
    chunks = kinds // 2
    core = counts[leaves]
    for c in range(chunks):
        near_ref, far_ref = sources[2 * c], sources[2 * c + 1]
        lower = 0 if chunks == 1 or c == 1 else core * (leaves // 8)
        upper = width // 8 if chunks == 1 or c == 0 else (core + 1) * (leaves // 8)

        @pl.loop(lower, upper)
        def _(g, c=c, near_ref=near_ref, far_ref=far_ref):
            for u in range(8):
                j = 8 * g + u
                at = pl.ds(pl.multiple_of(j * 128, 128), 128)
                x = near_weight * jnp.concatenate([near_ref[0:32, at], far_ref[0:32, at]], axis=0)
                weights[c * width + j] = stack(x)
                places[c * width + j, 0:3] = near_ref[32:35, at] if chunks == 2 else targets[:, at]

    weights[chunks * width] = jnp.zeros(weights.shape[1:], bf16)
    places[chunks * width] = jnp.zeros(places.shape[1:], f32)
    blank = jnp.zeros((5, 128), f32)

    @pl.loop(0, leaves // 16)
    def _(g):
        rows = []
        for u in range(16):
            at = pl.ds(pl.multiple_of((core * leaves + 16 * g + u) * 128, 128), 128)
            rows += [targets[:, at], blank]
        t = jnp.transpose(jnp.concatenate(rows, axis=0))
        for u in range(16):
            for c in range(3):
                columns_of[16 * g + u, c] = jnp.broadcast_to(t[:, 8 * u + c : 8 * u + c + 1], (128, 128))
            total[16 * g + u] = jnp.zeros((128, 128), f32)

    items = lax.fori_loop(
        0, leaves, lambda i, s: s + jnp.maximum((counts[i] + PAIR - 1) // PAIR, 1), jnp.int32(0)
    )

    def block(leaf, slot):
        kernels, parts = [], []
        for u in range(PAIR):
            j = lists[leaf * SLOTS + slot + u]
            s = places[j]
            d = columns_of[leaf, 0] - s[0:1]
            squared = d * d + smoothing
            d = columns_of[leaf, 1] - s[1:2]
            squared = squared + d * d
            d = columns_of[leaf, 2] - s[2:3]
            squared = squared + d * d
            kernels += split(lax.rsqrt(squared))
            x = weights[j]
            parts += [x, x]
        return lax.dot_general(
            jnp.concatenate(kernels, axis=1),
            jnp.concatenate(parts, axis=1),
            NT,
            preferred_element_type=f32,
        )

    def step(b, carry):
        leaf, slot = carry
        made = []
        for u in range(unroll):
            place = jnp.where(b * unroll + u < items, leaf, leaves)
            made.append((place, block(leaf, slot)))
            done = slot + PAIR >= counts[leaf]
            leaf = jnp.where(done, jnp.minimum(leaf + 1, leaves - 1), leaf)
            slot = jnp.where(done, 0, slot + PAIR)
        for place, x in made:
            total[place] += x
        return leaf, slot

    lax.fori_loop(0, (items + unroll - 1) // unroll, step, (jnp.int32(0), jnp.int32(0)))

    @pl.loop(0, leaves, unroll=8)
    def _(leaf):
        at = pl.ds(pl.multiple_of(leaf * 128, 128), 128)
        x = jnp.transpose(both(total[leaf]))
        if begin is None:
            mine[:, at] = x[0:32]
            other[:, at] = x[32:64]
        else:
            mine[:, at] = begin[0:32, at] + x[0:32]
            other[:, at] = begin[32:64, at] + x[32:64]


def near_pass(unroll, lists, counts, targets, sources, begin=None):
    leaves = lists.shape[0] // SLOTS
    held = 64 * (len(sources) // 2) + 1
    side = jax.ShapeDtypeStruct((32, leaves * 128), f32)
    extra = [] if begin is None else list(begin)
    if begin is not None:
        extra = [jnp.concatenate(begin, axis=0)]
    return pl.pallas_call(
        functools.partial(near_body, unroll, len(sources)),
        out_shape=(side, side),
        in_specs=[SM, SM] + [VM] * (1 + len(sources) + len(extra)),
        out_specs=(VM, VM),
        scratch_shapes=[
            pltpu.VMEM((leaves, 3, 128, 128), f32),
            pltpu.VMEM((leaves + 1, 128, 128), f32),
            pltpu.VMEM((held, 128, 128), bf16),
            pltpu.VMEM((held, 8, 128), f32),
        ],
        compiler_params=pltpu.CompilerParams(vmem_limit_bytes=40 << 20),
        cost_estimate=pl.CostEstimate(flops=1_000, bytes_accessed=1_000, transcendentals=0),
        name="near_pass",
    )(lists, counts, targets, *sources, *extra)


def arranged(picked, leaf_ids, empty):
    slots = picked.shape[1]
    before = jnp.arange(slots)[:, None] < jnp.arange(slots)[None, :]
    rank = jnp.sum(jnp.where(picked[:, :, None] & before[None], 1, 0), axis=1)
    to = jnp.arange(SLOTS)[None, None, :]
    here = picked[:, :, None] & (rank[:, :, None] == to)
    found = jnp.sum(jnp.where(here, leaf_ids[:, :, None], 0), axis=1)
    count = jnp.sum(picked.astype(jnp.int32), axis=1)
    lists = jnp.where(jnp.arange(SLOTS)[None, :] < count[:, None], found, empty)
    return lists.astype(jnp.int32).reshape(-1), count


def partner_codes(partners, position, leaves):
    spans, starts = [], []
    width, tile = leaves, 0
    while width >= 1:
        spans += [width] * width
        starts += [2 * tile] * width
        tile, width = tile + max(1, width // 2), width // 2
    spans = jnp.array(spans, jnp.int32)[:, None]
    starts = jnp.array(starts, jnp.int32)[:, None]
    local = partners - position * spans
    side = jnp.where(local < 0, 0, jnp.where(local < spans, 1, 2))
    return (side * (2 * leaves) + starts + local - (side - 1) * spans).reshape(-1)


def local(
    points,
    values,
    near_list,
    near_count,
    basis,
    transfer,
    coupling,
    partners,
    transfer_top,
    coupling_top,
    partners_top,
):
    leaves = basis.shape[0]
    position = lax.axis_index("leaf")
    core = lax.axis_index("rhs")
    count = lax.axis_size("leaf")
    forward = [(i, i + 1) for i in range(count - 1)]
    backward = [(target, source) for source, target in forward]
    swap = [(0, 1), (1, 0)]
    packed = jnp.concatenate([values, points], axis=0)
    low = lax.ppermute(packed, "leaf", forward)
    high = lax.ppermute(packed, "leaf", backward)
    across = lax.ppermute(values, "rhs", swap)

    half = leaves // 2
    chosen = lax.dynamic_slice_in_dim(near_list, core * half, half, 0) - position * leaves
    live = lax.dynamic_slice_in_dim(near_count, core * half, half, 0)
    alive = jnp.arange(chosen.shape[1])[None, :] < live[:, None]
    inside = (chosen >= 0) & (chosen < leaves)
    near_ids, near_live = arranged(alive & inside, chosen, leaves)
    outside_ids = jnp.where(chosen < 0, chosen + leaves, chosen)
    far_ids, far_live = arranged(alive & ~inside, outside_ids, 2 * leaves)
    near_live = jnp.concatenate([near_live, core[None]]).astype(jnp.int32)
    far_live = jnp.concatenate([far_live, core[None]]).astype(jnp.int32)
    codes = partner_codes(partners, position, leaves)

    def exchange(x, bit):
        return lax.ppermute(x, "leaf", [(i, i ^ (1 << bit)) for i in range(count)])

    def ordered(x, y, bit, axis):
        return jnp.where(
            (position >> bit) & 1 == 0,
            jnp.concatenate([x, y], axis),
            jnp.concatenate([y, x], axis),
        )

    after = lax.optimization_barrier
    up, trans = up_pass(basis, values, transfer.transpose(1, 2, 0))
    up_low = lax.ppermute(up, "leaf", forward)
    up_high = lax.ppermute(up, "leaf", backward)
    near_ids, up = after((near_ids, up))
    begin = near_pass(8, near_ids, near_live, points, (values, across))
    low, high, coupling, begin = after((low, high, coupling, begin))
    low_across = lax.ppermute(low, "rhs", swap)
    high_across = lax.ppermute(high, "rhs", swap)
    matrices = unbatch(coupling.transpose(1, 2, 3, 0))
    far_ids, up_low, up_high, matrices = after((far_ids, up_low, up_high, matrices))
    sibling = jnp.where(position % 2 == 0, up_high[leaves - 1, :, 64:], up_low[leaves - 1, :, 64:])
    level = up[leaves - 1, :, 64:] + sibling
    pair = exchange(level, 1)
    mine, other = near_pass(8, far_ids, far_live, points, (low, low_across, high, high_across), begin)
    pair, mine, other = after((pair, mine, other))
    level = ordered(level, pair, 1, 1)[None]
    for bit in range(2, 5):
        level = ordered(level, exchange(level, bit), bit, 0)
    pair = exchange(level, 5)
    given = lax.ppermute(other, "rhs", swap)
    codes, level, mine = after((codes, level, mine))
    far = couple_pass(codes, up_low, up, up_high, matrices)
    pair, far = after((pair, far))
    level = ordered(level, pair, 5, 0)
    parent = top_pass(
        position[None].astype(jnp.int32), partners_top.reshape(-1), level, transfer_top, coupling_top
    )
    return down_pass(core[None].astype(jnp.int32), parent, far, trans, basis, mine, given)


def solution(mesh):
    placed = (
        P(None, "leaf"),
        P("rhs", "leaf"),
        P("leaf", None),
        P("leaf"),
        P("leaf", None, None),
        P("leaf", None, None),
        P("leaf", None, None, None),
        P("leaf", None),
        P(),
        P(),
        P(),
    )
    return jax.shard_map(
        local, mesh=mesh, in_specs=placed, out_specs=P("rhs", "leaf"), check_vma=False
    )
```

```python
import jax, jax.numpy as jnp, functools
from jax import lax
from jax.sharding import PartitionSpec as P
from jax.experimental import pallas as pl
from jax.experimental.pallas import tpu as pltpu
NT = (((1,), (1,)), ((), ()))
SM = pl.BlockSpec(memory_space=pltpu.SMEM)
VM = pl.BlockSpec(memory_space=pltpu.VMEM)
HBM = pl.BlockSpec(memory_space=pltpu.HBM)
PITCH = 136
f32 = jnp.float32
bf16 = jnp.bfloat16

def split(x):
    hi = x.astype(bf16)
    return hi, (x - hi.astype(f32)).astype(bf16)

def stack(x):
    hi, lo = split(x)
    return jnp.concatenate([hi, lo], axis=0)

def fold(x):
    half = x.shape[0] // 2
    return x[:half] + x[half:]

def both(x):
    return x + pltpu.roll(x, 64, 1)

def low_lanes(shape):
    return lax.broadcasted_iota(jnp.int32, shape, 1) < 64

def up_body(basis_hbm, values_hbm, moves_hbm, up, trans, rows, basis, values, moves, sem):
    leaves = basis.shape[0]
    columns = values.shape[0]
    nodes = moves.shape[2]
    reads = []
    for i in range(4):
        at = pl.ds(16 * i, 16)
        reads.append(pltpu.make_async_copy(moves_hbm.at[at], moves.at[at], sem.at[i]))
    reads.append(pltpu.make_async_copy(values_hbm, values, sem.at[4]))
    reads.append(pltpu.make_async_copy(basis_hbm, basis, sem.at[5]))
    for read in reads:
        read.start()
    for i in range(4):
        reads[i].wait()

        @pl.loop(16 * i, 16 * i + 16, unroll=4)
        def _(r):
            block = jnp.transpose(moves[r])
            rows[pl.ds(pl.multiple_of(r * PITCH, 8), nodes)] = jnp.concatenate([block, block], axis=1)

    left = low_lanes((64, 128))

    @pl.loop(0, nodes, unroll=4)
    def _(n):
        x = rows[pl.ds(n, 64, stride=PITCH), :]
        hi = x.astype(bf16).astype(f32)
        trans[n] = jnp.where(left, hi, x - hi).astype(bf16)

    half = low_lanes((columns, 128))

    for read in reads[4:]:
        read.wait()

    def leaf_up(i):
        v = stack(values[:, pl.ds(pl.multiple_of(i * 128, 128), 128)])
        return both(fold(lax.dot_general(v, stack(basis[i]), NT, preferred_element_type=f32)))

    @pl.loop(0, leaves // 2, unroll=4)
    def _(p):
        up[p] = jnp.where(half, leaf_up(2 * p), leaf_up(2 * p + 1))

    def lift(tile, row):
        t = jnp.concatenate([trans[row], trans[row + 1]], axis=0)
        return both(fold(jnp.dot(stack(tile), t, preferred_element_type=f32)))

    def pair(tile_a, tile_b, row):
        return jnp.where(half, lift(tile_a, row), lift(tile_b, row + 2))

    start, row, width = 0, 0, leaves
    while width > 16:
        after = start + width // 2

        @pl.loop(0, width // 16)
        def _(g, start=start, row=row, after=after):
            made = []
            for p in range(4):
                q = 4 * g + p
                made.append(pair(up[start + 2 * q], up[start + 2 * q + 1], row + 4 * q))
            for p in range(4):
                up[after + 4 * g + p] = made[p]

        start, row, width = after, row + width, width // 2
    tiles = [up[start + p] for p in range(width // 2)]
    while width > 1:
        after = start + width // 2
        if width >= 4:
            tiles = [pair(tiles[2 * p], tiles[2 * p + 1], row + 4 * p) for p in range(width // 4)]
        else:
            tiles = [lift(tiles[0], row)]
        if after < leaves - 1:
            for p, tile in enumerate(tiles):
                up[after + p] = tile
        start, row, width = after, row + width, width // 2
    share = both(fold(jnp.dot(stack(tiles[0])[:, 0:64], trans[row], preferred_element_type=f32)))
    up[leaves - 1] = jnp.where(half, tiles[0], share)


def up_pass(basis, values, moves):
    leaves = basis.shape[0]
    columns = values.shape[0]
    nodes = moves.shape[2]
    return pl.pallas_call(
        up_body,
        out_shape=(
            jax.ShapeDtypeStruct((leaves, columns, 128), f32),
            jax.ShapeDtypeStruct((nodes + 1, 64, 128), bf16),
        ),
        in_specs=[HBM, HBM, HBM],
        out_specs=(VM, VM),
        scratch_shapes=[
            pltpu.VMEM((64 * PITCH, 128), f32),
            pltpu.VMEM(basis.shape, f32),
            pltpu.VMEM(values.shape, f32),
            pltpu.VMEM(moves.shape, f32),
            pltpu.SemaphoreType.DMA((6,)),
        ],
        compiler_params=pltpu.CompilerParams(vmem_limit_bytes=56 << 20),
        cost_estimate=pl.CostEstimate(flops=400_000_000, bytes_accessed=8_000_000, transcendentals=0),
        name="up_pass",
    )(basis, values, moves)


def unbatch_body(part, matrices, out, rows):
    nodes = matrices.shape[3]

    @pl.loop(0, 64, unroll=4)
    def _(r):
        x = jnp.concatenate([matrices[2 * part, r], matrices[2 * part + 1, r]], axis=0)
        rows[pl.ds(pl.multiple_of(r * PITCH, 8), nodes)] = jnp.transpose(x)

    def one(n):
        hi, lo = split(rows[pl.ds(n, 64, stride=PITCH), :])
        out[n, 0:64] = hi
        out[n, 64:128] = lo

    whole = nodes // 8 * 8
    pl.loop(0, whole, unroll=8)(one)
    for n in range(whole, nodes):
        one(n)


def unbatch(matrices, part):
    nodes = matrices.shape[3]
    return pl.pallas_call(
        functools.partial(unbatch_body, part),
        out_shape=jax.ShapeDtypeStruct((nodes, 128, 128), bf16),
        in_specs=[VM],
        out_specs=VM,
        scratch_shapes=[pltpu.VMEM((64 * PITCH, 128), f32)],
        compiler_params=pltpu.CompilerParams(vmem_limit_bytes=20 << 20),
        cost_estimate=pl.CostEstimate(flops=50_000_000, bytes_accessed=9_000_000, transcendentals=0),
        name="unbatch",
    )(matrices)


def top_body(place, partners, first, moves, matrices, parent, up, block, sem):
    spot = place[0]
    columns = first.shape[1]
    copies = []
    width, row = 32, 0
    for level in range(4):
        index = row + spot // (2 << level)
        copies.append(pltpu.make_async_copy(matrices.at[index], block.at[level], sem.at[level]))
        copies[-1].start()
        row, width = row + width, width // 2
    half = low_lanes((columns, 128))
    up[0:16] = first[...]
    def lift(tile, r):
        t = jnp.concatenate([moves[r], moves[r + 1]], axis=0)
        hi, lo = split(t)
        x = stack(up[tile])
        z = fold(jnp.dot(x, hi, preferred_element_type=f32)) + jnp.dot(x[:columns], lo, preferred_element_type=f32)
        return jnp.concatenate([z, z], axis=1)
    tile0, row, width = 0, 0, 32
    tiles, rows = [], []
    while width >= 4:
        tiles.append(tile0)
        rows.append(row)
        nxt = tile0 + width // 2
        if width > 4:
            for p in range(width // 4):
                up[nxt + p] = jnp.where(half, lift(tile0 + 2 * p, row + 4 * p), lift(tile0 + 2 * p + 1, row + 4 * p + 2))
        tile0, row, width = nxt, row + width, width // 2
    def push(d, r):
        hi, lo = split(moves[r])
        x = stack(d)
        return fold(lax.dot_general(x, hi, NT, preferred_element_type=f32)) + lax.dot_general(x[:columns], lo, NT, preferred_element_type=f32)
    down = jnp.zeros((columns, 64), f32)
    down = push(down, row + spot // 32)
    for level in range(3, -1, -1):
        index = rows[level] + spot // (2 << level)
        down = push(down, index)
        copies[level].wait()
        for k in range(4):
            p = partners[index * 4 + k]
            tile = up[tiles[level] + p // 2]
            x = stack(jnp.where(p % 2 == 0, tile, pltpu.roll(tile, 64, 1))[:, 0:64])
            hi, lo = split(block[level, k])
            down = down + fold(lax.dot_general(x, hi, NT, preferred_element_type=f32)) + lax.dot_general(x[:columns], lo, NT, preferred_element_type=f32)
    parent[...] = jnp.concatenate([down, down], axis=1)

def top_pass(place, partners, first, moves, matrices):
    columns = first.shape[1]
    return pl.pallas_call(
        top_body,
        out_shape=jax.ShapeDtypeStruct((columns, 128), f32),
        in_specs=[SM, SM, VM, VM, HBM],
        out_specs=VM,
        scratch_shapes=[pltpu.VMEM((32, columns, 128), f32), pltpu.VMEM((4, 4, 64, 64), f32), pltpu.SemaphoreType.DMA((4,))],
        compiler_params=pltpu.CompilerParams(vmem_limit_bytes=56 << 20),
        cost_estimate=pl.CostEstimate(flops=50_000_000, bytes_accessed=2_000_000, transcendentals=0),
        name="top_pass",
    )(place, partners, first, moves, matrices)


def couple_body(codes, low, own, high, first, second, far, gather):
    leaves = own.shape[0]
    columns = own.shape[1]
    nodes = first.shape[0]
    half = low_lanes((columns, 128))
    left = low_lanes((2 * columns, 128))
    for side, ref in enumerate((low, own, high)):

        @pl.loop(0, leaves, unroll=16)
        def _(t, side=side, ref=ref):
            x = ref[t]
            gather[0, side * leaves + t] = stack(x)
            gather[1, side * leaves + t] = stack(pltpu.roll(x, 64, 1))

    def pick(n, k, side):
        code = codes[4 * n + k]
        return gather[(code & 1) ^ side, code >> 1]

    def one(n):
        x = jnp.concatenate(
            [
                jnp.where(left, pick(n, 0, 0), pick(n, 1, 1)),
                jnp.where(left, pick(n, 2, 0), pick(n, 3, 1)),
            ],
            axis=1,
        )
        m = jnp.concatenate([first[n], second[n]], axis=1)
        return both(fold(lax.dot_general(x, m, NT, preferred_element_type=f32)))

    @pl.loop(0, leaves - 1, unroll=7)
    def _(t):
        far[t] = jnp.where(half, one(2 * t), one(2 * t + 1))

    far[leaves - 1] = one(nodes - 1)


def couple_pass(codes, low, own, high, first, second):
    leaves, columns, _ = own.shape
    return pl.pallas_call(
        couple_body,
        out_shape=jax.ShapeDtypeStruct((leaves, columns, 128), f32),
        in_specs=[SM] + [VM] * 5,
        out_specs=VM,
        scratch_shapes=[pltpu.VMEM((2, 3 * leaves, 2 * columns, 128), bf16)],
        compiler_params=pltpu.CompilerParams(vmem_limit_bytes=24 << 20),
        cost_estimate=pl.CostEstimate(flops=400_000_000, bytes_accessed=12_000_000, transcendentals=0),
        name="couple_pass",
    )(codes, low, own, high, first, second)


def down_body(core, parent, far, trans, basis, mine, given, out, held):
    leaves = basis.shape[0]
    columns = out.shape[0]
    half = low_lanes((columns, 128))

    def push(d, row, tile):
        t = jnp.concatenate([trans[row], trans[row + 1]], axis=0)
        return fold(lax.dot_general(stack(d), t, NT, preferred_element_type=f32)) + far[tile]

    def spread(tile):
        turned = pltpu.roll(tile, 64, 1)
        return jnp.where(half, tile, turned), jnp.where(half, turned, tile)

    last = leaves - 1
    t = trans[2 * last]
    d = fold(
        lax.dot_general(
            stack(parent[...]), jnp.concatenate([t, t], axis=0), NT, preferred_element_type=f32
        )
    )
    sources = [d + far[last]]
    start, width = last, 1
    while width < 16:
        start = start - max(1, width)
        made = [push(d, 2 * (start + i), start + i) for i, d in enumerate(sources)]
        sources = [d for tile in made for d in spread(tile)]
        width = 2 * width
    for i, tile in enumerate(made):
        held[i] = tile
    first = start - width

    @pl.loop(0, len(made), unroll=2)
    def _(i):
        results = []
        for j, d in enumerate(spread(held[i])):
            above = 2 * i + j
            for u, e in enumerate(spread(push(d, 2 * (first + above), first + above))):
                tile = 2 * above + u
                for w, x in enumerate(spread(push(e, 2 * tile, tile))):
                    leaf = 2 * tile + w
                    results.append(
                        (leaf, fold(jnp.dot(stack(x), stack(basis[leaf]), preferred_element_type=f32)))
                    )
        for leaf, x in results:
            out[:, pl.ds(pl.multiple_of(leaf * 128, 128), 128)] = x

    size = mine.shape[1]
    out[:, pl.ds(pl.multiple_of(core[0] * size, size), size)] += mine[...]
    out[:, pl.ds(pl.multiple_of((1 - core[0]) * size, size), size)] += given[...]


def down_pass(core, parent, far, trans, basis, mine, given):
    leaves = basis.shape[0]
    columns = parent.shape[0]
    return pl.pallas_call(
        down_body,
        out_shape=jax.ShapeDtypeStruct((columns, leaves * 128), f32),
        in_specs=[SM] + [VM] * 6,
        out_specs=VM,
        scratch_shapes=[pltpu.VMEM((8, columns, 128), f32)],
        compiler_params=pltpu.CompilerParams(vmem_limit_bytes=14 << 20),
        cost_estimate=pl.CostEstimate(flops=200_000_000, bytes_accessed=7_000_000, transcendentals=0),
        name="down_pass",
    )(core, parent, far, trans, basis, mine, given)


near_weight = 0.1
smoothing = 0.0025
SLOTS = 28
PAIR = 2

def near_body(unroll, chunks, lists, counts, targets, *refs):
    sources, refs = refs[: 2 * chunks], refs[2 * chunks :]
    begin, spots = None, [targets]
    if chunks == 2:
        begin, spots, refs = refs[0:2], refs[2:4], refs[4:]
    mine, other, columns_of, total, weights, places = refs
    leaves = mine.shape[1] // 128
    width = sources[0].shape[1] // 128
    core = counts[leaves]
    for c in range(chunks):
        near_ref, far_ref = sources[2 * c], sources[2 * c + 1]
        lower = 0 if chunks == 1 or c == 1 else core * (leaves // 8)
        upper = width // 8 if chunks == 1 or c == 0 else (core + 1) * (leaves // 8)

        @pl.loop(lower, upper)
        def _(g, c=c, near_ref=near_ref, far_ref=far_ref):
            for u in range(8):
                j = 8 * g + u
                at = pl.ds(pl.multiple_of(j * 128, 128), 128)
                x = near_weight * jnp.concatenate([near_ref[:, at], far_ref[:, at]], axis=0)
                weights[c * width + j] = stack(x)
                places[c * width + j, 0:3] = spots[c][:, at]

    weights[chunks * width] = jnp.zeros(weights.shape[1:], bf16)
    places[chunks * width] = jnp.zeros(places.shape[1:], f32)
    blank = jnp.zeros((5, 128), f32)

    @pl.loop(0, leaves // 16)
    def _(g):
        rows = []
        for u in range(16):
            at = pl.ds(pl.multiple_of((core * leaves + 16 * g + u) * 128, 128), 128)
            rows += [targets[:, at], blank]
        t = jnp.transpose(jnp.concatenate(rows, axis=0))
        for u in range(16):
            for c in range(3):
                columns_of[16 * g + u, c] = jnp.broadcast_to(t[:, 8 * u + c : 8 * u + c + 1], (128, 128))
            total[16 * g + u] = jnp.zeros((128, 128), f32)

    items = lax.fori_loop(
        0, leaves, lambda i, s: s + jnp.maximum((counts[i] + PAIR - 1) // PAIR, 1), jnp.int32(0)
    )

    def block(leaf, slot):
        kernels, parts = [], []
        for u in range(PAIR):
            j = lists[leaf * SLOTS + slot + u]
            s = places[j]
            d = columns_of[leaf, 0] - s[0:1]
            squared = d * d + smoothing
            d = columns_of[leaf, 1] - s[1:2]
            squared = squared + d * d
            d = columns_of[leaf, 2] - s[2:3]
            squared = squared + d * d
            kernels += split(lax.rsqrt(squared))
            x = weights[j]
            parts += [x, x]
        return lax.dot_general(
            jnp.concatenate(kernels, axis=1),
            jnp.concatenate(parts, axis=1),
            NT,
            preferred_element_type=f32,
        )

    def step(b, carry):
        leaf, slot = carry
        made = []
        for u in range(unroll):
            place = jnp.where(b * unroll + u < items, leaf, leaves)
            made.append((place, block(leaf, slot)))
            done = slot + PAIR >= counts[leaf]
            leaf = jnp.where(done, jnp.minimum(leaf + 1, leaves - 1), leaf)
            slot = jnp.where(done, 0, slot + PAIR)
        for place, x in made:
            total[place] += x
        return leaf, slot

    lax.fori_loop(0, (items + unroll - 1) // unroll, step, (jnp.int32(0), jnp.int32(0)))

    @pl.loop(0, leaves, unroll=8)
    def _(leaf):
        at = pl.ds(pl.multiple_of(leaf * 128, 128), 128)
        x = jnp.transpose(both(total[leaf]))
        if begin is None:
            mine[:, at] = x[0:32]
            other[:, at] = x[32:64]
        else:
            mine[:, at] = begin[0][:, at] + x[0:32]
            other[:, at] = begin[1][:, at] + x[32:64]


def near_pass(unroll, lists, counts, targets, sources, begin=(), spots=()):
    leaves = lists.shape[0] // SLOTS
    chunks = len(sources) // 2
    held = chunks * (sources[0].shape[1] // 128) + 1
    side = jax.ShapeDtypeStruct((32, leaves * 128), f32)
    arrays = (targets, *sources, *begin, *spots)
    return pl.pallas_call(
        functools.partial(near_body, unroll, chunks),
        out_shape=(side, side),
        in_specs=[SM, SM] + [VM] * len(arrays),
        out_specs=(VM, VM),
        scratch_shapes=[
            pltpu.VMEM((leaves, 3, 128, 128), f32),
            pltpu.VMEM((leaves + 1, 128, 128), f32),
            pltpu.VMEM((held, 128, 128), bf16),
            pltpu.VMEM((held, 8, 128), f32),
        ],
        compiler_params=pltpu.CompilerParams(vmem_limit_bytes=24 << 20),
        cost_estimate=pl.CostEstimate(flops=1_000, bytes_accessed=1_000, transcendentals=0),
        name="near_pass",
    )(lists, counts, *arrays)


def arranged(picked, leaf_ids, empty):
    slots = picked.shape[1]
    before = jnp.arange(slots)[:, None] < jnp.arange(slots)[None, :]
    rank = jnp.sum(jnp.where(picked[:, :, None] & before[None], 1, 0), axis=1)
    to = jnp.arange(SLOTS)[None, None, :]
    here = picked[:, :, None] & (rank[:, :, None] == to)
    found = jnp.sum(jnp.where(here, leaf_ids[:, :, None], 0), axis=1)
    count = jnp.sum(picked.astype(jnp.int32), axis=1)
    lists = jnp.where(jnp.arange(SLOTS)[None, :] < count[:, None], found, empty)
    return lists.astype(jnp.int32).reshape(-1), count


def partner_codes(partners, position, leaves):
    spans, starts = [], []
    width, tile = leaves, 0
    while width >= 1:
        spans += [width] * width
        starts += [2 * tile] * width
        tile, width = tile + max(1, width // 2), width // 2
    spans = jnp.array(spans, jnp.int32)[:, None]
    starts = jnp.array(starts, jnp.int32)[:, None]
    local = partners - position * spans
    side = jnp.where(local < 0, 0, jnp.where(local < spans, 1, 2))
    return (side * (2 * leaves) + starts + local - (side - 1) * spans).reshape(-1)


def local(
    points,
    values,
    near_list,
    near_count,
    basis,
    transfer,
    coupling,
    partners,
    transfer_top,
    coupling_top,
    partners_top,
):
    leaves = basis.shape[0]
    position = lax.axis_index("leaf")
    core = lax.axis_index("rhs")
    count = lax.axis_size("leaf")
    forward = [(i, i + 1) for i in range(count - 1)]
    backward = [(target, source) for source, target in forward]
    swap = [(0, 1), (1, 0)]
    low = lax.ppermute(values, "leaf", forward)
    high = lax.ppermute(values, "leaf", backward)
    across = lax.ppermute(values, "rhs", swap)

    half = leaves // 2
    chosen = lax.dynamic_slice_in_dim(near_list, core * half, half, 0) - position * leaves
    live = lax.dynamic_slice_in_dim(near_count, core * half, half, 0)
    alive = jnp.arange(chosen.shape[1])[None, :] < live[:, None]
    inside = (chosen >= 0) & (chosen < leaves)
    near_ids, near_live = arranged(alive & inside, chosen, leaves)
    outside_ids = jnp.where(chosen < 0, chosen + leaves, chosen)
    far_ids, far_live = arranged(alive & ~inside, outside_ids, 2 * leaves)
    near_live = jnp.concatenate([near_live, core[None]]).astype(jnp.int32)
    far_live = jnp.concatenate([far_live, core[None]]).astype(jnp.int32)
    codes = partner_codes(partners, position, leaves)

    def ring(x, stride):
        spot = (position // stride) % 4
        turned = []
        for shift in range(3, 0, -1):
            to = [(i, i + stride * ((i // stride + shift) % 4 - i // stride % 4)) for i in range(count)]
            turned.append(lax.ppermute(x, "leaf", to))
        return turned, spot

    def in_order(turned, x, spot):
        both_rounds = jnp.concatenate([*turned, x, *turned, x], axis=0)
        return lax.dynamic_slice_in_dim(both_rounds, (3 - spot) * x.shape[0], 4 * x.shape[0], 0)

    after = lax.optimization_barrier
    up, trans = up_pass(basis, values, transfer.transpose(1, 2, 0))
    up_low = lax.ppermute(up, "leaf", forward)
    up_high = lax.ppermute(up, "leaf", backward)
    spots = (lax.ppermute(points, "leaf", forward), lax.ppermute(points, "leaf", backward))
    near_ids, up = after((near_ids, up))
    begin = near_pass(8, near_ids, near_live, points, (values, across))
    low, high, coupling, begin = after((low, high, coupling, begin))
    low_across = lax.ppermute(low, "rhs", swap)
    high_across = lax.ppermute(high, "rhs", swap)
    coupling = coupling.transpose(1, 2, 3, 0)
    first = unbatch(coupling, 0)
    far_ids, up_low, up_high, first = after((far_ids, up_low, up_high, first))
    sibling = jnp.where(position % 2 == 0, up_high[leaves - 1, :, 64:], up_low[leaves - 1, :, 64:])
    level = up[leaves - 1, :, 64:] + sibling
    pair = lax.ppermute(level, "leaf", [(i, i ^ 2) for i in range(count)])
    mine, other = near_pass(
        8, far_ids, far_live, points, (low, low_across, high, high_across), begin, spots
    )
    pair, mine, other, coupling = after((pair, mine, other, coupling))
    given = lax.ppermute(other, "rhs", swap)
    level = jnp.where(
        position & 2 == 0,
        jnp.concatenate([level, pair], axis=1),
        jnp.concatenate([pair, level], axis=1),
    )[None]
    turned, spot = ring(level, 4)
    second = unbatch(coupling, 1)
    turned, codes, second = after((turned, codes, second))
    level = in_order(turned, level, spot)
    turned, spot = ring(level, 16)
    far = couple_pass(codes, up_low, up, up_high, first, second)
    turned, far = after((turned, far))
    level = in_order(turned, level, spot)
    parent = top_pass(
        position[None].astype(jnp.int32), partners_top.reshape(-1), level, transfer_top, coupling_top
    )
    return down_pass(core[None].astype(jnp.int32), parent, far, trans, basis, mine, given)


def solution(mesh):
    placed = (
        P(None, "leaf"),
        P("rhs", "leaf"),
        P("leaf", None),
        P("leaf"),
        P("leaf", None, None),
        P("leaf", None, None),
        P("leaf", None, None, None),
        P("leaf", None),
        P(),
        P(),
        P(),
    )
    return jax.shard_map(
        local, mesh=mesh, in_specs=placed, out_specs=P("rhs", "leaf"), check_vma=False
    )
```

```python
import jax, jax.numpy as jnp, functools
from jax import lax
from jax.sharding import PartitionSpec as P
from jax.experimental import pallas as pl
from jax.experimental.pallas import tpu as pltpu
NT = (((1,), (1,)), ((), ()))
SM = pl.BlockSpec(memory_space=pltpu.SMEM)
VM = pl.BlockSpec(memory_space=pltpu.VMEM)
HBM = pl.BlockSpec(memory_space=pltpu.HBM)
PITCH = 136
VMEM_BYTES = 58 << 20
f32 = jnp.float32
bf16 = jnp.bfloat16

def split(x):
    hi = x.astype(bf16)
    return hi, (x - hi.astype(f32)).astype(bf16)

def stack(x):
    hi, lo = split(x)
    return jnp.concatenate([hi, lo], axis=0)

def fold(x):
    half = x.shape[0] // 2
    return x[:half] + x[half:]

def both(x):
    return x + pltpu.roll(x, 64, 1)

def low_lanes(shape):
    return lax.broadcasted_iota(jnp.int32, shape, 1) < 64

def up_body(points, basis_hbm, values_hbm, moves_hbm, up, trans, packed, rows, basis, values, moves, sem):
    leaves = basis.shape[0]
    columns = values.shape[0]
    nodes = moves.shape[2]
    reads = []
    for i in range(4):
        at = pl.ds(16 * i, 16)
        reads.append(pltpu.make_async_copy(moves_hbm.at[at], moves.at[at], sem.at[i]))
    reads.append(pltpu.make_async_copy(values_hbm, values, sem.at[4]))
    reads.append(pltpu.make_async_copy(basis_hbm, basis, sem.at[5]))
    for read in reads:
        read.start()
    for i in range(4):
        reads[i].wait()

        @pl.loop(16 * i, 16 * i + 16, unroll=4)
        def _(r):
            block = jnp.transpose(moves[r])
            rows[pl.ds(pl.multiple_of(r * PITCH, 8), nodes)] = jnp.concatenate([block, block], axis=1)

    left = low_lanes((64, 128))

    @pl.loop(0, nodes, unroll=4)
    def _(n):
        x = rows[pl.ds(n, 64, stride=PITCH), :]
        hi = x.astype(bf16).astype(f32)
        trans[n] = jnp.where(left, hi, x - hi).astype(bf16)

    half = low_lanes((columns, 128))

    for read in reads[4:]:
        read.wait()
    packed[0:columns] = values[...]
    packed[columns:] = points[...]

    def leaf_up(i):
        v = stack(values[:, pl.ds(pl.multiple_of(i * 128, 128), 128)])
        return both(fold(lax.dot_general(v, stack(basis[i]), NT, preferred_element_type=f32)))

    @pl.loop(0, leaves // 2, unroll=4)
    def _(p):
        up[p] = jnp.where(half, leaf_up(2 * p), leaf_up(2 * p + 1))

    def lift(tile, row):
        t = jnp.concatenate([trans[row], trans[row + 1]], axis=0)
        return both(fold(jnp.dot(stack(tile), t, preferred_element_type=f32)))

    def pair(tile_a, tile_b, row):
        return jnp.where(half, lift(tile_a, row), lift(tile_b, row + 2))

    start, row, width = 0, 0, leaves
    while width > 16:
        after = start + width // 2

        @pl.loop(0, width // 16)
        def _(g, start=start, row=row, after=after):
            made = []
            for p in range(4):
                q = 4 * g + p
                made.append(pair(up[start + 2 * q], up[start + 2 * q + 1], row + 4 * q))
            for p in range(4):
                up[after + 4 * g + p] = made[p]

        start, row, width = after, row + width, width // 2
    tiles = [up[start + p] for p in range(width // 2)]
    while width > 1:
        after = start + width // 2
        if width >= 4:
            tiles = [pair(tiles[2 * p], tiles[2 * p + 1], row + 4 * p) for p in range(width // 4)]
        else:
            tiles = [lift(tiles[0], row)]
        if after < leaves - 1:
            for p, tile in enumerate(tiles):
                up[after + p] = tile
        start, row, width = after, row + width, width // 2
    share = both(fold(jnp.dot(stack(tiles[0])[:, 0:64], trans[row], preferred_element_type=f32)))
    up[leaves - 1] = jnp.where(half, tiles[0], share)


def up_pass(points, basis, values, moves):
    leaves = basis.shape[0]
    columns = values.shape[0]
    nodes = moves.shape[2]
    return pl.pallas_call(
        up_body,
        out_shape=(
            jax.ShapeDtypeStruct((leaves, columns, 128), f32),
            jax.ShapeDtypeStruct((nodes + 1, 64, 128), bf16),
            jax.ShapeDtypeStruct((columns + 3, values.shape[1]), f32),
        ),
        in_specs=[VM, HBM, HBM, HBM],
        out_specs=(VM, VM, VM),
        scratch_shapes=[
            pltpu.VMEM((64 * PITCH, 128), f32),
            pltpu.VMEM(basis.shape, f32),
            pltpu.VMEM(values.shape, f32),
            pltpu.VMEM(moves.shape, f32),
            pltpu.SemaphoreType.DMA((6,)),
        ],
        compiler_params=pltpu.CompilerParams(vmem_limit_bytes=VMEM_BYTES),
        cost_estimate=pl.CostEstimate(flops=400_000_000, bytes_accessed=8_000_000, transcendentals=0),
        name="up_pass",
    )(points, basis, values, moves)


CHUNK = 32


def unbatch_body(matrices, out, held, rows, made, in_sem, out_sem):
    nodes = matrices.shape[3]
    pieces = 4
    step = matrices.shape[1] // pieces
    reads = []
    for h in range(2):
        for i in range(pieces):
            at = pl.ds(i * step, step)
            pair = pl.ds(2 * h, 2)
            reads.append(
                pltpu.make_async_copy(
                    matrices.at[pair, at], held.at[pair, at], in_sem.at[pieces * h + i]
                )
            )
    for read in reads:
        read.start()
    writes = []
    for h in range(2):
        for i in range(pieces):
            reads[pieces * h + i].wait()

            @pl.loop(i * step, (i + 1) * step, unroll=4)
            def _(r, h=h):
                x = jnp.concatenate([held[2 * h, r], held[2 * h + 1, r]], axis=0)
                rows[pl.ds(pl.multiple_of((h * 64 + r) * PITCH, 8), nodes)] = jnp.transpose(x)

        def one(n, h=h):
            hi, lo = split(rows[pl.ds(h * 64 * PITCH + n, 64, stride=PITCH), :])
            made[h, n, 0:64] = hi
            made[h, n, 64:128] = lo

        for c, begin in enumerate(range(0, nodes, CHUNK)):
            size = min(CHUNK, nodes - begin)
            whole = begin + size // 8 * 8
            pl.loop(begin, whole, unroll=8)(one)
            for n in range(whole, begin + size):
                one(n)
            at = pl.ds(begin, size)
            writes.append(
                pltpu.make_async_copy(made.at[h, at], out.at[h, at], out_sem.at[h, c])
            )
            writes[-1].start()
    for write in writes:
        write.wait()


def unbatch(matrices):
    nodes = matrices.shape[3]
    return pl.pallas_call(
        unbatch_body,
        out_shape=jax.ShapeDtypeStruct((2, nodes, 128, 128), bf16),
        in_specs=[HBM],
        out_specs=HBM,
        scratch_shapes=[
            pltpu.VMEM(matrices.shape, f32),
            pltpu.VMEM((2 * 64 * PITCH, 128), f32),
            pltpu.VMEM((2, nodes, 128, 128), bf16),
            pltpu.SemaphoreType.DMA((8,)),
            pltpu.SemaphoreType.DMA((2, -(-nodes // CHUNK))),
        ],
        compiler_params=pltpu.CompilerParams(vmem_limit_bytes=VMEM_BYTES),
        cost_estimate=pl.CostEstimate(flops=100_000_000, bytes_accessed=17_000_000, transcendentals=0),
        name="unbatch",
    )(matrices)


def top_body(place, partners, first, moves, matrices, parent, up, block, sem):
    spot = place[0]
    columns = first.shape[1]
    copies = []
    width, row = 32, 0
    for level in range(4):
        index = row + spot // (2 << level)
        copies.append(pltpu.make_async_copy(matrices.at[index], block.at[level], sem.at[level]))
        copies[-1].start()
        row, width = row + width, width // 2
    half = low_lanes((columns, 128))
    up[0:16] = first[...]
    def lift(tile, r):
        t = jnp.concatenate([moves[r], moves[r + 1]], axis=0)
        hi, lo = split(t)
        x = stack(up[tile])
        z = fold(jnp.dot(x, hi, preferred_element_type=f32)) + jnp.dot(x[:columns], lo, preferred_element_type=f32)
        return jnp.concatenate([z, z], axis=1)
    tile0, row, width = 0, 0, 32
    tiles, rows = [], []
    while width >= 4:
        tiles.append(tile0)
        rows.append(row)
        nxt = tile0 + width // 2
        if width > 4:
            for p in range(width // 4):
                up[nxt + p] = jnp.where(half, lift(tile0 + 2 * p, row + 4 * p), lift(tile0 + 2 * p + 1, row + 4 * p + 2))
        tile0, row, width = nxt, row + width, width // 2
    def push(d, r):
        hi, lo = split(moves[r])
        x = stack(d)
        return fold(lax.dot_general(x, hi, NT, preferred_element_type=f32)) + lax.dot_general(x[:columns], lo, NT, preferred_element_type=f32)
    down = jnp.zeros((columns, 64), f32)
    down = push(down, row + spot // 32)
    for level in range(3, -1, -1):
        index = rows[level] + spot // (2 << level)
        down = push(down, index)
        copies[level].wait()
        for k in range(4):
            p = partners[index * 4 + k]
            tile = up[tiles[level] + p // 2]
            x = stack(jnp.where(p % 2 == 0, tile, pltpu.roll(tile, 64, 1))[:, 0:64])
            hi, lo = split(block[level, k])
            down = down + fold(lax.dot_general(x, hi, NT, preferred_element_type=f32)) + lax.dot_general(x[:columns], lo, NT, preferred_element_type=f32)
    parent[...] = jnp.concatenate([down, down], axis=1)

def top_pass(place, partners, first, moves, matrices):
    columns = first.shape[1]
    return pl.pallas_call(
        top_body,
        out_shape=jax.ShapeDtypeStruct((columns, 128), f32),
        in_specs=[SM, SM, VM, VM, HBM],
        out_specs=VM,
        scratch_shapes=[pltpu.VMEM((32, columns, 128), f32), pltpu.VMEM((4, 4, 64, 64), f32), pltpu.SemaphoreType.DMA((4,))],
        compiler_params=pltpu.CompilerParams(vmem_limit_bytes=VMEM_BYTES),
        cost_estimate=pl.CostEstimate(flops=50_000_000, bytes_accessed=2_000_000, transcendentals=0),
        name="top_pass",
    )(place, partners, first, moves, matrices)


def couple_body(codes, low, own, high, matrices, far, gather, held, sem):
    leaves = own.shape[0]
    columns = own.shape[1]
    nodes = matrices.shape[1]
    reads = []
    for i in range(3):
        begin = 42 * i
        at = pl.ds(begin, nodes - begin if i == 2 else 42)
        reads.append(pltpu.make_async_copy(matrices.at[:, at], held.at[:, at], sem.at[i]))
        reads[-1].start()
    half = low_lanes((columns, 128))
    left = low_lanes((2 * columns, 128))
    for side, ref in enumerate((low, own, high)):

        @pl.loop(0, leaves, unroll=16)
        def _(t, side=side, ref=ref):
            x = ref[t]
            gather[0, side * leaves + t] = stack(x)
            gather[1, side * leaves + t] = stack(pltpu.roll(x, 64, 1))

    def pick(n, k, side):
        code = codes[4 * n + k]
        return gather[(code & 1) ^ side, code >> 1]

    def one(n):
        x = jnp.concatenate(
            [
                jnp.where(left, pick(n, 0, 0), pick(n, 1, 1)),
                jnp.where(left, pick(n, 2, 0), pick(n, 3, 1)),
            ],
            axis=1,
        )
        m = jnp.concatenate([held[0, n], held[1, n]], axis=1)
        return both(fold(lax.dot_general(x, m, NT, preferred_element_type=f32)))

    for i in range(3):
        reads[i].wait()

        @pl.loop(21 * i, 21 * i + 21, unroll=7)
        def _(t):
            far[t] = jnp.where(half, one(2 * t), one(2 * t + 1))

    far[leaves - 1] = one(nodes - 1)


def couple_pass(codes, low, own, high, matrices):
    leaves, columns, _ = own.shape
    return pl.pallas_call(
        couple_body,
        out_shape=jax.ShapeDtypeStruct((leaves, columns, 128), f32),
        in_specs=[SM] + [VM] * 3 + [HBM],
        out_specs=VM,
        scratch_shapes=[
            pltpu.VMEM((2, 3 * leaves, 2 * columns, 128), bf16),
            pltpu.VMEM(matrices.shape, bf16),
            pltpu.SemaphoreType.DMA((3,)),
        ],
        compiler_params=pltpu.CompilerParams(vmem_limit_bytes=VMEM_BYTES),
        cost_estimate=pl.CostEstimate(flops=400_000_000, bytes_accessed=12_000_000, transcendentals=0),
        name="couple_pass",
    )(codes, low, own, high, matrices)


def down_body(core, parent, far, trans, basis, mine, given, out, held):
    leaves = basis.shape[0]
    columns = out.shape[0]
    half = low_lanes((columns, 128))

    def push(d, row, tile):
        t = jnp.concatenate([trans[row], trans[row + 1]], axis=0)
        return fold(lax.dot_general(stack(d), t, NT, preferred_element_type=f32)) + far[tile]

    def spread(tile):
        turned = pltpu.roll(tile, 64, 1)
        return jnp.where(half, tile, turned), jnp.where(half, turned, tile)

    last = leaves - 1
    t = trans[2 * last]
    d = fold(
        lax.dot_general(
            stack(parent[...]), jnp.concatenate([t, t], axis=0), NT, preferred_element_type=f32
        )
    )
    sources = [d + far[last]]
    start, width = last, 1
    while width < 16:
        start = start - max(1, width)
        made = [push(d, 2 * (start + i), start + i) for i, d in enumerate(sources)]
        sources = [d for tile in made for d in spread(tile)]
        width = 2 * width
    for i, tile in enumerate(made):
        held[i] = tile
    first = start - width

    @pl.loop(0, len(made), unroll=2)
    def _(i):
        results = []
        for j, d in enumerate(spread(held[i])):
            above = 2 * i + j
            for u, e in enumerate(spread(push(d, 2 * (first + above), first + above))):
                tile = 2 * above + u
                for w, x in enumerate(spread(push(e, 2 * tile, tile))):
                    leaf = 2 * tile + w
                    results.append(
                        (leaf, fold(jnp.dot(stack(x), stack(basis[leaf]), preferred_element_type=f32)))
                    )
        for leaf, x in results:
            out[:, pl.ds(pl.multiple_of(leaf * 128, 128), 128)] = x

    size = mine.shape[1]
    out[:, pl.ds(pl.multiple_of(core[0] * size, size), size)] += mine[...]
    out[:, pl.ds(pl.multiple_of((1 - core[0]) * size, size), size)] += given[...]


def down_pass(core, parent, far, trans, basis, mine, given):
    leaves = basis.shape[0]
    columns = parent.shape[0]
    return pl.pallas_call(
        down_body,
        out_shape=jax.ShapeDtypeStruct((columns, leaves * 128), f32),
        in_specs=[SM] + [VM] * 6,
        out_specs=VM,
        scratch_shapes=[pltpu.VMEM((8, columns, 128), f32)],
        compiler_params=pltpu.CompilerParams(vmem_limit_bytes=VMEM_BYTES),
        cost_estimate=pl.CostEstimate(flops=200_000_000, bytes_accessed=7_000_000, transcendentals=0),
        name="down_pass",
    )(core, parent, far, trans, basis, mine, given)


near_weight = 0.1
smoothing = 0.0025
SLOTS = 28
PAIR = 2

def near_body(unroll, chunks, lists, counts, targets, *refs):
    sources, refs = refs[: 2 * chunks], refs[2 * chunks :]
    begin = None
    if chunks == 2:
        begin, refs = refs[0:2], refs[2:]
    mine, other, columns_of, total, weights, places = refs
    leaves = mine.shape[1] // 128
    width = sources[0].shape[1] // 128
    core = counts[leaves]
    for c in range(chunks):
        near_ref, far_ref = sources[2 * c], sources[2 * c + 1]
        lower = 0 if chunks == 1 or c == 1 else core * (leaves // 8)
        upper = width // 8 if chunks == 1 or c == 0 else (core + 1) * (leaves // 8)

        @pl.loop(lower, upper)
        def _(g, c=c, near_ref=near_ref, far_ref=far_ref):
            for u in range(8):
                j = 8 * g + u
                at = pl.ds(pl.multiple_of(j * 128, 128), 128)
                x = near_weight * jnp.concatenate([near_ref[0:32, at], far_ref[0:32, at]], axis=0)
                weights[c * width + j] = stack(x)
                places[c * width + j, 0:3] = near_ref[32:35, at]

    weights[chunks * width] = jnp.zeros(weights.shape[1:], bf16)
    places[chunks * width] = jnp.zeros(places.shape[1:], f32)
    blank = jnp.zeros((5, 128), f32)

    @pl.loop(0, leaves // 16)
    def _(g):
        rows = []
        for u in range(16):
            at = pl.ds(pl.multiple_of((core * leaves + 16 * g + u) * 128, 128), 128)
            rows += [targets[:, at], blank]
        t = jnp.transpose(jnp.concatenate(rows, axis=0))
        for u in range(16):
            for c in range(3):
                columns_of[16 * g + u, c] = jnp.broadcast_to(t[:, 8 * u + c : 8 * u + c + 1], (128, 128))
            total[16 * g + u] = jnp.zeros((128, 128), f32)

    items = lax.fori_loop(
        0, leaves, lambda i, s: s + jnp.maximum((counts[i] + PAIR - 1) // PAIR, 1), jnp.int32(0)
    )

    def block(leaf, slot):
        kernels, parts = [], []
        for u in range(PAIR):
            j = lists[leaf * SLOTS + slot + u]
            s = places[j]
            d = columns_of[leaf, 0] - s[0:1]
            squared = d * d + smoothing
            d = columns_of[leaf, 1] - s[1:2]
            squared = squared + d * d
            d = columns_of[leaf, 2] - s[2:3]
            squared = squared + d * d
            kernels += split(lax.rsqrt(squared))
            x = weights[j]
            parts += [x, x]
        return lax.dot_general(
            jnp.concatenate(kernels, axis=1),
            jnp.concatenate(parts, axis=1),
            NT,
            preferred_element_type=f32,
        )

    def step(b, carry):
        leaf, slot = carry
        made = []
        for u in range(unroll):
            place = jnp.where(b * unroll + u < items, leaf, leaves)
            made.append((place, block(leaf, slot)))
            done = slot + PAIR >= counts[leaf]
            leaf = jnp.where(done, jnp.minimum(leaf + 1, leaves - 1), leaf)
            slot = jnp.where(done, 0, slot + PAIR)
        for place, x in made:
            total[place] += x
        return leaf, slot

    lax.fori_loop(0, (items + unroll - 1) // unroll, step, (jnp.int32(0), jnp.int32(0)))

    @pl.loop(0, leaves, unroll=8)
    def _(leaf):
        at = pl.ds(pl.multiple_of(leaf * 128, 128), 128)
        x = jnp.transpose(both(total[leaf]))
        if begin is None:
            mine[:, at] = x[0:32]
            other[:, at] = x[32:64]
        else:
            mine[:, at] = begin[0][:, at] + x[0:32]
            other[:, at] = begin[1][:, at] + x[32:64]


def near_pass(unroll, lists, counts, targets, sources, begin=()):
    leaves = lists.shape[0] // SLOTS
    chunks = len(sources) // 2
    held = chunks * (sources[0].shape[1] // 128) + 1
    side = jax.ShapeDtypeStruct((32, leaves * 128), f32)
    arrays = (targets, *sources, *begin)
    return pl.pallas_call(
        functools.partial(near_body, unroll, chunks),
        out_shape=(side, side),
        in_specs=[SM, SM] + [VM] * len(arrays),
        out_specs=(VM, VM),
        scratch_shapes=[
            pltpu.VMEM((leaves, 3, 128, 128), f32),
            pltpu.VMEM((leaves + 1, 128, 128), f32),
            pltpu.VMEM((held, 128, 128), bf16),
            pltpu.VMEM((held, 8, 128), f32),
        ],
        compiler_params=pltpu.CompilerParams(vmem_limit_bytes=VMEM_BYTES),
        cost_estimate=pl.CostEstimate(flops=1_000, bytes_accessed=1_000, transcendentals=0),
        name="near_pass",
    )(lists, counts, *arrays)


def arranged(picked, leaf_ids, empty):
    slots = picked.shape[1]
    before = jnp.arange(slots)[:, None] < jnp.arange(slots)[None, :]
    rank = jnp.sum(jnp.where(picked[:, :, None] & before[None], 1, 0), axis=1)
    to = jnp.arange(SLOTS)[None, None, :]
    here = picked[:, :, None] & (rank[:, :, None] == to)
    found = jnp.sum(jnp.where(here, leaf_ids[:, :, None], 0), axis=1)
    count = jnp.sum(picked.astype(jnp.int32), axis=1)
    lists = jnp.where(jnp.arange(SLOTS)[None, :] < count[:, None], found, empty)
    return lists.astype(jnp.int32).reshape(-1), count


def partner_codes(partners, position, leaves):
    spans, starts = [], []
    width, tile = leaves, 0
    while width >= 1:
        spans += [width] * width
        starts += [2 * tile] * width
        tile, width = tile + max(1, width // 2), width // 2
    spans = jnp.array(spans, jnp.int32)[:, None]
    starts = jnp.array(starts, jnp.int32)[:, None]
    local = partners - position * spans
    side = jnp.where(local < 0, 0, jnp.where(local < spans, 1, 2))
    return (side * (2 * leaves) + starts + local - (side - 1) * spans).reshape(-1)


def local(
    points,
    values,
    near_list,
    near_count,
    basis,
    transfer,
    coupling,
    partners,
    transfer_top,
    coupling_top,
    partners_top,
):
    leaves = basis.shape[0]
    position = lax.axis_index("leaf")
    core = lax.axis_index("rhs")
    count = lax.axis_size("leaf")
    forward = [(i, i + 1) for i in range(count - 1)]
    backward = [(target, source) for source, target in forward]
    swap = [(0, 1), (1, 0)]
    across = lax.ppermute(values, "rhs", swap)
    half = leaves // 2
    chosen = lax.dynamic_slice_in_dim(near_list, core * half, half, 0) - position * leaves
    live = lax.dynamic_slice_in_dim(near_count, core * half, half, 0)
    alive = jnp.arange(chosen.shape[1])[None, :] < live[:, None]
    inside = (chosen >= 0) & (chosen < leaves)
    near_ids, near_live = arranged(alive & inside, chosen, leaves)
    outside_ids = jnp.where(chosen < 0, chosen + leaves, chosen)
    far_ids, far_live = arranged(alive & ~inside, outside_ids, 2 * leaves)
    near_live = jnp.concatenate([near_live, core[None]]).astype(jnp.int32)
    far_live = jnp.concatenate([far_live, core[None]]).astype(jnp.int32)
    codes = partner_codes(partners, position, leaves)

    def ring(x, stride):
        spot = (position // stride) % 4
        turned = []
        for shift in range(3, 0, -1):
            to = [(i, i + stride * ((i // stride + shift) % 4 - i // stride % 4)) for i in range(count)]
            turned.append(lax.ppermute(x, "leaf", to))
        return turned, spot

    def in_order(turned, x, spot):
        both_rounds = jnp.concatenate([*turned, x, *turned, x], axis=0)
        return lax.dynamic_slice_in_dim(both_rounds, (3 - spot) * x.shape[0], 4 * x.shape[0], 0)

    after = lax.optimization_barrier
    up, trans, packed = up_pass(points, basis, values, transfer.transpose(1, 2, 0))
    share = up[leaves - 1, :, 64:]
    shares, spot = ring(share[None], 1)
    low = lax.ppermute(packed, "leaf", forward)
    high = lax.ppermute(packed, "leaf", backward)
    up_low = lax.ppermute(up, "leaf", forward)
    up_high = lax.ppermute(up, "leaf", backward)
    near_ids, far_ids, codes, up = after((near_ids, far_ids, codes, up))
    begin = near_pass(8, near_ids, near_live, points, (packed, across))
    shares, low, high, coupling, begin = after((shares, low, high, coupling, begin))
    level = in_order(shares, share[None], spot)
    level = jnp.concatenate([level[0] + level[1], level[2] + level[3]], axis=1)[None]
    low_across = lax.ppermute(low, "rhs", swap)
    high_across = lax.ppermute(high, "rhs", swap)
    turned, spot = ring(level, 4)
    matrices = unbatch(coupling.transpose(1, 2, 3, 0))
    turned, far_ids, matrices = after((turned, far_ids, matrices))
    level = in_order(turned, level, spot)
    turned, spot = ring(level, 16)
    mine, other = near_pass(
        8, far_ids, far_live, points, (low, low_across, high, high_across), begin
    )
    turned, mine, other = after((turned, mine, other))
    given = lax.ppermute(other, "rhs", swap)
    level = in_order(turned, level, spot)
    parent = top_pass(
        position[None].astype(jnp.int32), partners_top.reshape(-1), level, transfer_top, coupling_top
    )
    up_low, up_high, parent = after((up_low, up_high, parent))
    far = couple_pass(codes, up_low, up, up_high, matrices)
    return down_pass(core[None].astype(jnp.int32), parent, far, trans, basis, mine, given)


def solution(mesh):
    placed = (
        P(None, "leaf"),
        P("rhs", "leaf"),
        P("leaf", None),
        P("leaf"),
        P("leaf", None, None),
        P("leaf", None, None),
        P("leaf", None, None, None),
        P("leaf", None),
        P(),
        P(),
        P(),
    )
    return jax.shard_map(
        local, mesh=mesh, in_specs=placed, out_specs=P("rhs", "leaf"), check_vma=False
    )
```

```python
import jax, jax.numpy as jnp, functools
from jax import lax
from jax.sharding import PartitionSpec as P
from jax.experimental import pallas as pl
from jax.experimental.pallas import tpu as pltpu
NT = (((1,), (1,)), ((), ()))
SM = pl.BlockSpec(memory_space=pltpu.SMEM)
VM = pl.BlockSpec(memory_space=pltpu.VMEM)
HBM = pl.BlockSpec(memory_space=pltpu.HBM)
PITCH = 136
VMEM_BYTES = 58 << 20
f32 = jnp.float32
bf16 = jnp.bfloat16

def split(x):
    hi = x.astype(bf16)
    return hi, (x - hi.astype(f32)).astype(bf16)

def stack(x):
    hi, lo = split(x)
    return jnp.concatenate([hi, lo], axis=0)

def fold(x):
    half = x.shape[0] // 2
    return x[:half] + x[half:]

def both(x):
    return x + pltpu.roll(x, 64, 1)

def low_lanes(shape):
    return lax.broadcasted_iota(jnp.int32, shape, 1) < 64

def up_body(
    points, basis_hbm, values_hbm, moves_hbm, up, trans_hbm, packed_hbm, rows, basis, values, moves, trans, packed, sem
):
    leaves = basis.shape[0]
    columns = values.shape[0]
    nodes = moves.shape[2]
    reads = []
    for i in range(4):
        at = pl.ds(16 * i, 16)
        reads.append(pltpu.make_async_copy(moves_hbm.at[at], moves.at[at], sem.at[i]))
    reads.append(pltpu.make_async_copy(values_hbm, values, sem.at[4]))
    reads.append(pltpu.make_async_copy(basis_hbm, basis, sem.at[5]))
    for read in reads:
        read.start()
    for i in range(4):
        reads[i].wait()

        @pl.loop(16 * i, 16 * i + 16, unroll=8)
        def _(r):
            block = jnp.transpose(moves[r])
            rows[pl.ds(pl.multiple_of(r * PITCH, 8), nodes)] = jnp.concatenate([block, block], axis=1)

    left = low_lanes((64, 128))

    def node(n):
        x = rows[pl.ds(n, 64, stride=PITCH), :]
        hi = x.astype(bf16).astype(f32)
        trans[n] = jnp.where(left, hi, x - hi).astype(bf16)

    whole = nodes // 8 * 8
    pl.loop(0, whole, unroll=8)(node)
    for n in range(whole, nodes):
        node(n)
    trans[nodes] = jnp.zeros(trans.shape[1:], bf16)
    writes = [pltpu.make_async_copy(trans, trans_hbm, sem.at[6])]
    writes[0].start()

    half = low_lanes((columns, 128))

    for read in reads[4:]:
        read.wait()
    packed[0:columns] = values[...]
    packed[columns : columns + 3] = points[...]
    packed[columns + 4 :] = jnp.zeros((4, packed.shape[1]), f32)

    def leaf_up(i):
        v = stack(values[:, pl.ds(pl.multiple_of(i * 128, 128), 128)])
        return both(fold(lax.dot_general(v, stack(basis[i]), NT, preferred_element_type=f32)))

    @pl.loop(0, leaves // 2, unroll=8)
    def _(p):
        up[p] = jnp.where(half, leaf_up(2 * p), leaf_up(2 * p + 1))

    def lift(tile, row):
        t = jnp.concatenate([trans[row], trans[row + 1]], axis=0)
        return both(fold(jnp.dot(stack(tile), t, preferred_element_type=f32)))

    def pair(tile_a, tile_b, row):
        return jnp.where(half, lift(tile_a, row), lift(tile_b, row + 2))

    start, row, width = 0, 0, leaves
    while width > 16:
        after = start + width // 2

        @pl.loop(0, width // 16)
        def _(g, start=start, row=row, after=after):
            made = []
            for p in range(4):
                q = 4 * g + p
                made.append(pair(up[start + 2 * q], up[start + 2 * q + 1], row + 4 * q))
            for p in range(4):
                up[after + 4 * g + p] = made[p]

        start, row, width = after, row + width, width // 2
    tiles = [up[start + p] for p in range(width // 2)]
    while width > 1:
        after = start + width // 2
        if width >= 4:
            tiles = [pair(tiles[2 * p], tiles[2 * p + 1], row + 4 * p) for p in range(width // 4)]
        else:
            tiles = [lift(tiles[0], row)]
        if after < leaves - 1:
            for p, tile in enumerate(tiles):
                up[after + p] = tile
        start, row, width = after, row + width, width // 2
    up[leaves - 1] = tiles[0]
    share = both(fold(jnp.dot(stack(tiles[0])[:, 0:64], trans[row], preferred_element_type=f32)))
    for c in range(columns):
        packed[columns + 3 : columns + 4, 128 * c : 128 * c + 128] = share[c : c + 1]
    packed[columns + 3 : columns + 4, 128 * columns :] = jnp.zeros(
        (1, packed.shape[1] - 128 * columns), f32
    )
    writes.append(pltpu.make_async_copy(packed, packed_hbm, sem.at[7]))
    writes[1].start()
    for write in writes:
        write.wait()


def up_pass(points, basis, values, moves):
    leaves = basis.shape[0]
    columns = values.shape[0]
    nodes = moves.shape[2]
    return pl.pallas_call(
        up_body,
        out_shape=(
            jax.ShapeDtypeStruct((leaves, columns, 128), f32),
            jax.ShapeDtypeStruct((nodes + 1, 64, 128), bf16),
            jax.ShapeDtypeStruct((columns + 8, values.shape[1]), f32),
        ),
        in_specs=[VM, HBM, HBM, HBM],
        out_specs=(VM, HBM, HBM),
        scratch_shapes=[
            pltpu.VMEM((64 * PITCH, 128), f32),
            pltpu.VMEM(basis.shape, f32),
            pltpu.VMEM(values.shape, f32),
            pltpu.VMEM(moves.shape, f32),
            pltpu.VMEM((nodes + 1, 64, 128), bf16),
            pltpu.VMEM((columns + 8, values.shape[1]), f32),
            pltpu.SemaphoreType.DMA((8,)),
        ],
        compiler_params=pltpu.CompilerParams(vmem_limit_bytes=VMEM_BYTES),
        cost_estimate=pl.CostEstimate(flops=400_000_000, bytes_accessed=8_000_000, transcendentals=0),
        name="up_pass",
    )(points, basis, values, moves)


CHUNK = 32


def unbatch_body(matrices, out, held, rows, made, in_sem, out_sem):
    nodes = matrices.shape[3]
    pieces = 4
    step = matrices.shape[1] // pieces
    reads = []
    for h in range(2):
        for i in range(pieces):
            at = pl.ds(i * step, step)
            pair = pl.ds(2 * h, 2)
            reads.append(
                pltpu.make_async_copy(
                    matrices.at[pair, at], held.at[pair, at], in_sem.at[pieces * h + i]
                )
            )
    for read in reads:
        read.start()
    writes = []
    for h in range(2):
        for i in range(pieces):
            reads[pieces * h + i].wait()

            @pl.loop(i * step, (i + 1) * step, unroll=4)
            def _(r, h=h):
                x = jnp.concatenate([held[2 * h, r], held[2 * h + 1, r]], axis=0)
                rows[pl.ds(pl.multiple_of((h * 64 + r) * PITCH, 8), nodes)] = jnp.transpose(x)

        def one(n, h=h):
            hi, lo = split(rows[pl.ds(h * 64 * PITCH + n, 64, stride=PITCH), :])
            made[h, n, 0:64] = hi
            made[h, n, 64:128] = lo

        for c, begin in enumerate(range(0, nodes, CHUNK)):
            size = min(CHUNK, nodes - begin)
            whole = begin + size // 8 * 8
            pl.loop(begin, whole, unroll=8)(one)
            for n in range(whole, begin + size):
                one(n)
            at = pl.ds(begin, size)
            writes.append(
                pltpu.make_async_copy(made.at[h, at], out.at[h, at], out_sem.at[h, c])
            )
            writes[-1].start()
    for write in writes:
        write.wait()


def unbatch(matrices):
    nodes = matrices.shape[3]
    return pl.pallas_call(
        unbatch_body,
        out_shape=jax.ShapeDtypeStruct((2, nodes, 128, 128), bf16),
        in_specs=[HBM],
        out_specs=HBM,
        scratch_shapes=[
            pltpu.VMEM(matrices.shape, f32),
            pltpu.VMEM((2 * 64 * PITCH, 128), f32),
            pltpu.VMEM((2, nodes, 128, 128), bf16),
            pltpu.SemaphoreType.DMA((8,)),
            pltpu.SemaphoreType.DMA((2, -(-nodes // CHUNK))),
        ],
        compiler_params=pltpu.CompilerParams(vmem_limit_bytes=VMEM_BYTES),
        cost_estimate=pl.CostEstimate(flops=1_000, bytes_accessed=1_000, transcendentals=0),
        name="unbatch",
    )(matrices)


def top_body(place, partners, far_three, far_two, far_one, own, moves, matrices, parent, up, block, sem):
    spot = place[0]
    columns = own.shape[1]
    copies = []
    width, row = 32, 0
    for level in range(4):
        index = row + spot // (2 << level)
        copies.append(pltpu.make_async_copy(matrices.at[index], block.at[level], sem.at[level]))
        copies[-1].start()
        row, width = row + width, width // 2
    half = low_lanes((columns, 128))
    for j, ref in enumerate((far_three, far_two, far_one, own)):
        up[pl.ds(4 * ((spot // 16 + 1 + j) % 4), 4)] = ref[...]
    def lift(tile, r):
        t = jnp.concatenate([moves[r], moves[r + 1]], axis=0)
        hi, lo = split(t)
        x = stack(up[tile])
        z = fold(jnp.dot(x, hi, preferred_element_type=f32)) + jnp.dot(x[:columns], lo, preferred_element_type=f32)
        return jnp.concatenate([z, z], axis=1)
    tile0, row, width = 0, 0, 32
    tiles, rows = [], []
    while width >= 4:
        tiles.append(tile0)
        rows.append(row)
        nxt = tile0 + width // 2
        if width > 4:
            for p in range(width // 4):
                up[nxt + p] = jnp.where(half, lift(tile0 + 2 * p, row + 4 * p), lift(tile0 + 2 * p + 1, row + 4 * p + 2))
        tile0, row, width = nxt, row + width, width // 2
    def push(d, r):
        hi, lo = split(moves[r])
        x = stack(d)
        return fold(lax.dot_general(x, hi, NT, preferred_element_type=f32)) + lax.dot_general(x[:columns], lo, NT, preferred_element_type=f32)
    for copy in copies:
        copy.wait()
    fars = []
    for level in range(4):
        index = rows[level] + spot // (2 << level)
        far = jnp.zeros((columns, 64), f32)
        for k in range(4):
            p = partners[index, k]
            tile = up[tiles[level] + p // 2]
            x = stack(jnp.where(p % 2 == 0, tile, pltpu.roll(tile, 64, 1))[:, 0:64])
            hi, lo = split(block[level, k])
            far = far + fold(lax.dot_general(x, hi, NT, preferred_element_type=f32))
            far = far + lax.dot_general(x[:columns], lo, NT, preferred_element_type=f32)
        fars.append(far)
    down = jnp.zeros((columns, 64), f32)
    down = push(down, row + spot // 32)
    for level in range(3, -1, -1):
        down = push(down, rows[level] + spot // (2 << level)) + fars[level]
    parent[...] = jnp.concatenate([down, down], axis=1)

def top_pass(place, partners, gathered, moves, matrices):
    columns = gathered[0].shape[1]
    return pl.pallas_call(
        top_body,
        out_shape=jax.ShapeDtypeStruct((columns, 128), f32),
        in_specs=[SM, SM] + [VM] * 5 + [HBM],
        out_specs=VM,
        scratch_shapes=[pltpu.VMEM((32, columns, 128), f32), pltpu.VMEM((4, 4, 64, 64), f32), pltpu.SemaphoreType.DMA((4,))],
        compiler_params=pltpu.CompilerParams(vmem_limit_bytes=VMEM_BYTES),
        cost_estimate=pl.CostEstimate(flops=50_000_000, bytes_accessed=2_000_000, transcendentals=0),
        name="top_pass",
    )(place, partners, *gathered, moves, matrices)


def couple_body(codes, low, own, high, matrices, far, gather, tiles, held, sem):
    leaves, columns, _ = own.shape
    nodes = matrices.shape[1]
    takes = []
    for side, ref in enumerate((low, own, high)):
        takes.append(pltpu.make_async_copy(ref, tiles.at[side], sem.at[3 + side]))
        takes[-1].start()
    reads = []
    for i in range(3):
        begin = 42 * i
        at = pl.ds(begin, nodes - begin if i == 2 else 42)
        reads.append(pltpu.make_async_copy(matrices.at[:, at], held.at[:, at], sem.at[i]))
        reads[-1].start()
    half = low_lanes((columns, 128))
    left = low_lanes((2 * columns, 128))
    for side in range(3):
        takes[side].wait()

        @pl.loop(0, leaves, unroll=16)
        def _(t, side=side):
            x = tiles[side, t]
            gather[0, side * leaves + t] = stack(x)
            gather[1, side * leaves + t] = stack(pltpu.roll(x, 64, 1))

    def pick(n, k, side):
        code = codes[n, k]
        return gather[(code & 1) ^ side, code >> 1]

    def one(n):
        x = jnp.concatenate(
            [
                jnp.where(left, pick(n, 0, 0), pick(n, 1, 1)),
                jnp.where(left, pick(n, 2, 0), pick(n, 3, 1)),
            ],
            axis=1,
        )
        m = jnp.concatenate([held[0, n], held[1, n]], axis=1)
        return both(fold(lax.dot_general(x, m, NT, preferred_element_type=f32)))

    for i in range(3):
        reads[i].wait()

        @pl.loop(21 * i, 21 * i + 21, unroll=7)
        def _(t):
            far[t] = jnp.where(half, one(2 * t), one(2 * t + 1))

    far[leaves - 1] = one(nodes - 1)


def couple_pass(codes, low, own, high, matrices):
    leaves, columns, _ = own.shape
    return pl.pallas_call(
        couple_body,
        out_shape=jax.ShapeDtypeStruct((leaves, columns, 128), f32),
        in_specs=[SM] + [HBM] * 4,
        out_specs=VM,
        scratch_shapes=[
            pltpu.VMEM((2, 3 * leaves, 2 * columns, 128), bf16),
            pltpu.VMEM((3, leaves, columns, 128), f32),
            pltpu.VMEM(matrices.shape, bf16),
            pltpu.SemaphoreType.DMA((6,)),
        ],
        compiler_params=pltpu.CompilerParams(vmem_limit_bytes=VMEM_BYTES),
        cost_estimate=pl.CostEstimate(flops=400_000_000, bytes_accessed=12_000_000, transcendentals=0),
        name="couple_pass",
    )(codes, low, own, high, matrices)


def down_body(core, parent, far_hbm, trans_hbm, basis_hbm, mine, given, out, far, trans, basis, ones, twos, sem):
    leaves = basis.shape[0]
    columns = out.shape[0]
    reads = []
    for i, (source, dest) in enumerate(((far_hbm, far), (trans_hbm, trans), (basis_hbm, basis))):
        reads.append(pltpu.make_async_copy(source, dest, sem.at[i]))
        reads[-1].start()
    half = low_lanes((columns, 128))

    def push(d, tile):
        t = jnp.concatenate([trans[2 * tile], trans[2 * tile + 1]], axis=0)
        return fold(lax.dot_general(stack(d), t, NT, preferred_element_type=f32)) + far[tile]

    def spread(tile):
        turned = pltpu.roll(tile, 64, 1)
        return jnp.where(half, tile, turned), jnp.where(half, turned, tile)

    last = leaves - 1
    above = stack(parent[...])
    reads[0].wait()
    reads[1].wait()
    t = trans[2 * last]
    t = jnp.concatenate([t, t], axis=0)
    sources = [fold(lax.dot_general(above, t, NT, preferred_element_type=f32)) + far[last]]
    start, width = last, 1
    while width < 16:
        start = start - width
        made = [push(d, start + i) for i, d in enumerate(sources)]
        sources = [d for tile in made for d in spread(tile)]
        width = 2 * width
    start = start - width
    for i, d in enumerate(sources):
        ones[i] = push(d, start + i)

    @pl.loop(0, width, unroll=8)
    def _(i):
        for u, d in enumerate(spread(ones[i])):
            twos[2 * i + u] = push(d, 2 * i + u)

    reads[2].wait()

    @pl.loop(0, leaves // 2, unroll=4)
    def _(i):
        for u, d in enumerate(spread(twos[i])):
            leaf = 2 * i + u
            out[:, pl.ds(pl.multiple_of(leaf * 128, 128), 128)] = fold(
                jnp.dot(stack(d), stack(basis[leaf]), preferred_element_type=f32)
            )

    size = mine.shape[1]
    out[:, pl.ds(pl.multiple_of(core[0] * size, size), size)] += mine[...]
    out[:, pl.ds(pl.multiple_of((1 - core[0]) * size, size), size)] += given[...]


def down_pass(core, parent, far, trans, basis, mine, given):
    leaves = basis.shape[0]
    columns = parent.shape[0]
    return pl.pallas_call(
        down_body,
        out_shape=jax.ShapeDtypeStruct((columns, leaves * 128), f32),
        in_specs=[SM, VM, HBM, HBM, HBM, VM, VM],
        out_specs=VM,
        scratch_shapes=[
            pltpu.VMEM(far.shape, f32),
            pltpu.VMEM(trans.shape, bf16),
            pltpu.VMEM(basis.shape, f32),
            pltpu.VMEM((leaves // 4, columns, 128), f32),
            pltpu.VMEM((leaves // 2, columns, 128), f32),
            pltpu.SemaphoreType.DMA((3,)),
        ],
        compiler_params=pltpu.CompilerParams(vmem_limit_bytes=VMEM_BYTES),
        cost_estimate=pl.CostEstimate(flops=200_000_000, bytes_accessed=7_000_000, transcendentals=0),
        name="down_pass",
    )(core, parent, far, trans, basis, mine, given)


near_weight = 0.1
smoothing = 0.0025
SLOTS = 28
PAIR = 2

def near_body(unroll, chunks, core, lists, counts, targets, *refs):
    origins, refs = refs[: 2 * chunks], refs[2 * chunks :]
    begin = None
    if chunks == 2:
        begin, refs = refs[0:2], refs[2:]
    mine, other, columns_of, total, weights, places, sem, *sources = refs
    leaves = mine.shape[1] // 128
    width = sources[0].shape[1] // 128
    core = core[0]
    reads = []
    for i, (origin, source) in enumerate(zip(origins, sources)):
        reads.append(pltpu.make_async_copy(origin, source, sem.at[i]))
        reads[-1].start()
    weights[chunks * width] = jnp.zeros(weights.shape[1:], bf16)
    places[chunks * width] = jnp.zeros(places.shape[1:], f32)
    blank = jnp.zeros((5, 128), f32)

    @pl.loop(0, leaves // 16)
    def _(g):
        rows = []
        for u in range(16):
            at = pl.ds(pl.multiple_of((core * leaves + 16 * g + u) * 128, 128), 128)
            rows += [targets[:, at], blank]
        t = jnp.transpose(jnp.concatenate(rows, axis=0))
        for u in range(16):
            for c in range(3):
                columns_of[16 * g + u, c] = jnp.broadcast_to(t[:, 8 * u + c : 8 * u + c + 1], (128, 128))
            total[16 * g + u] = jnp.zeros((128, 128), f32)

    for read in reads:
        read.wait()
    for c in range(chunks):
        near_ref, far_ref = sources[2 * c], sources[2 * c + 1]
        lower = 0 if chunks == 1 or c == 1 else core * (leaves // 8)
        upper = width // 8 if chunks == 1 or c == 0 else (core + 1) * (leaves // 8)

        @pl.loop(lower, upper)
        def _(g, c=c, near_ref=near_ref, far_ref=far_ref):
            for u in range(8):
                j = 8 * g + u
                at = pl.ds(pl.multiple_of(j * 128, 128), 128)
                x = near_weight * jnp.concatenate([near_ref[0:32, at], far_ref[0:32, at]], axis=0)
                weights[c * width + j] = stack(x)
                places[c * width + j, 0:3] = near_ref[32:35, at]

    items = lax.fori_loop(
        0, leaves, lambda i, s: s + jnp.maximum((counts[i] + PAIR - 1) // PAIR, 1), jnp.int32(0)
    )

    def block(leaf, slot):
        kernels, parts = [], []
        for u in range(PAIR):
            j = lists[leaf, slot + u]
            s = places[j]
            d = columns_of[leaf, 0] - s[0:1]
            squared = d * d + smoothing
            d = columns_of[leaf, 1] - s[1:2]
            squared = squared + d * d
            d = columns_of[leaf, 2] - s[2:3]
            squared = squared + d * d
            kernels += split(lax.rsqrt(squared))
            x = weights[j]
            parts += [x, x]
        return lax.dot_general(
            jnp.concatenate(kernels, axis=1),
            jnp.concatenate(parts, axis=1),
            NT,
            preferred_element_type=f32,
        )

    def step(b, carry):
        leaf, slot = carry
        made = []
        for u in range(unroll):
            place = jnp.where(b * unroll + u < items, leaf, leaves)
            made.append((place, block(leaf, slot)))
            done = slot + PAIR >= counts[leaf]
            leaf = jnp.where(done, jnp.minimum(leaf + 1, leaves - 1), leaf)
            slot = jnp.where(done, 0, slot + PAIR)
        for place, x in made:
            total[place] += x
        return leaf, slot

    lax.fori_loop(0, (items + unroll - 1) // unroll, step, (jnp.int32(0), jnp.int32(0)))

    @pl.loop(0, leaves, unroll=8)
    def _(leaf):
        at = pl.ds(pl.multiple_of(leaf * 128, 128), 128)
        x = jnp.transpose(both(total[leaf]))
        if begin is None:
            mine[:, at] = x[0:32]
            other[:, at] = x[32:64]
        else:
            mine[:, at] = begin[0][:, at] + x[0:32]
            other[:, at] = begin[1][:, at] + x[32:64]


def near_pass(unroll, core, lists, counts, targets, sources, begin=()):
    leaves = lists.shape[0]
    chunks = len(sources) // 2
    held = chunks * (sources[0].shape[1] // 128) + 1
    side = jax.ShapeDtypeStruct((32, leaves * 128), f32)
    arrays = (targets, *sources, *begin)
    return pl.pallas_call(
        functools.partial(near_body, unroll, chunks),
        out_shape=(side, side),
        in_specs=[SM, SM, SM, VM] + [HBM] * len(sources) + [VM] * len(begin),
        out_specs=(VM, VM),
        scratch_shapes=[
            pltpu.VMEM((leaves, 3, 128, 128), f32),
            pltpu.VMEM((leaves + 1, 128, 128), f32),
            pltpu.VMEM((held, 128, 128), bf16),
            pltpu.VMEM((held, 8, 128), f32),
            pltpu.SemaphoreType.DMA((len(sources),)),
            *[pltpu.VMEM(x.shape, f32) for x in sources],
        ],
        compiler_params=pltpu.CompilerParams(vmem_limit_bytes=VMEM_BYTES),
        cost_estimate=pl.CostEstimate(flops=1_000, bytes_accessed=1_000, transcendentals=0),
        name="near_pass",
    )(core, lists, counts, *arrays)


def arranged(picked, leaf_ids, empty):
    slots = picked.shape[1]
    before = jnp.arange(slots)[:, None] < jnp.arange(slots)[None, :]
    rank = jnp.sum(jnp.where(picked[:, :, None] & before[None], 1, 0), axis=1)
    to = jnp.arange(SLOTS)[None, None, :]
    here = picked[:, :, None] & (rank[:, :, None] == to)
    found = jnp.sum(jnp.where(here, leaf_ids[:, :, None], 0), axis=1)
    count = jnp.sum(picked.astype(jnp.int32), axis=1)
    lists = jnp.where(jnp.arange(SLOTS)[None, :] < count[:, None], found, empty)
    return lists.astype(jnp.int32), count


def partner_codes(partners, position, leaves):
    spans, starts = [], []
    width, tile = leaves, 0
    while width >= 1:
        spans += [width] * width
        starts += [2 * tile] * width
        tile, width = tile + max(1, width // 2), width // 2
    spans = jnp.array(spans, jnp.int32)[:, None]
    starts = jnp.array(starts, jnp.int32)[:, None]
    local = partners - position * spans
    side = jnp.where(local < 0, 0, jnp.where(local < spans, 1, 2))
    return (side * (2 * leaves) + starts + local - (side - 1) * spans)


def local(
    points,
    values,
    near_list,
    near_count,
    basis,
    transfer,
    coupling,
    partners,
    transfer_top,
    coupling_top,
    partners_top,
):
    leaves = basis.shape[0]
    position = lax.axis_index("leaf")
    core = lax.axis_index("rhs")
    count = lax.axis_size("leaf")
    forward = [(i, i + 1) for i in range(count - 1)]
    backward = [(target, source) for source, target in forward]
    swap = [(0, 1), (1, 0)]
    across = lax.ppermute(values, "rhs", swap)
    half = leaves // 2
    chosen = lax.dynamic_slice_in_dim(near_list, core * half, half, 0) - position * leaves
    live = lax.dynamic_slice_in_dim(near_count, core * half, half, 0)
    alive = jnp.arange(chosen.shape[1])[None, :] < live[:, None]
    inside = (chosen >= 0) & (chosen < leaves)
    near_ids, near_live = arranged(alive & inside, chosen, leaves)
    outside_ids = jnp.where(chosen < 0, chosen + leaves, chosen)
    far_ids, far_live = arranged(alive & ~inside, outside_ids, 2 * leaves)
    codes = partner_codes(partners, position, leaves)

    def ring(x, stride):
        spot = (position // stride) % 4
        turned = []
        for shift in range(3, 0, -1):
            to = [(i, i + stride * ((i // stride + shift) % 4 - i // stride % 4)) for i in range(count)]
            turned.append(lax.ppermute(x, "leaf", to))
        return turned, spot

    def in_order(turned, x, spot):
        blocks = [*turned, x]
        ordered = []
        for k in range(4):
            block = blocks[3]
            for j in range(3):
                block = jnp.where(spot == (k - j - 1) % 4, blocks[j], block)
            ordered.append(block)
        return jnp.concatenate(ordered, axis=0)

    after = lax.optimization_barrier
    core = core[None].astype(jnp.int32)
    columns = values.shape[0]
    up, trans, packed = up_pass(points, basis, values, transfer.transpose(1, 2, 0))
    low = lax.ppermute(packed, "leaf", forward)
    high = lax.ppermute(packed, "leaf", backward)
    near_ids, far_ids, codes, up = after((near_ids, far_ids, codes, up))
    begin = near_pass(12, core, near_ids, near_live, points, (packed, across))
    low, high, coupling, begin = after((low, high, coupling, begin))
    row = slice(columns + 3, columns + 4)
    lanes = 128 * columns
    sibling = jnp.where(position % 2 == 0, high[row, 0:lanes], low[row, 0:lanes])
    level = (packed[row, 0:lanes] + sibling).reshape(columns, 128)
    pair = lax.ppermute(level, "leaf", [(i, i ^ 2) for i in range(count)])
    low_across = lax.ppermute(low, "rhs", swap)
    high_across = lax.ppermute(high, "rhs", swap)
    pair, up, coupling = after((pair, up, coupling))
    up_low = lax.ppermute(up, "leaf", forward)
    up_high = lax.ppermute(up, "leaf", backward)
    matrices = unbatch(coupling.transpose(1, 2, 3, 0))
    pair, far_ids, matrices = after((pair, far_ids, matrices))
    lower = jnp.arange(128) < 64
    level = jnp.where(lower == (position & 2 == 0), level, pair)[None]
    turned, spot = ring(level, 4)
    mine, other = near_pass(
        12, core, far_ids, far_live, points, (low, low_across, high, high_across), begin
    )
    turned, mine, other = after((turned, mine, other))
    given = lax.ppermute(other, "rhs", swap)
    level = in_order(turned, level, spot)
    turned, spot = ring(level, 16)
    codes, mine = after((codes, mine))
    far = couple_pass(codes, up_low, up, up_high, matrices)
    turned, far = after((turned, far))
    parent = top_pass(
        position[None].astype(jnp.int32), partners_top, (*turned, level), transfer_top, coupling_top
    )
    return down_pass(core, parent, far, trans, basis, mine, given)


def solution(mesh):
    placed = (
        P(None, "leaf"),
        P("rhs", "leaf"),
        P("leaf", None),
        P("leaf"),
        P("leaf", None, None),
        P("leaf", None, None),
        P("leaf", None, None, None),
        P("leaf", None),
        P(),
        P(),
        P(),
    )
    return jax.shard_map(
        local, mesh=mesh, in_specs=placed, out_specs=P("rhs", "leaf"), check_vma=False
    )
```

```python
import jax, jax.numpy as jnp, functools
from jax import lax
from jax.sharding import PartitionSpec as P
from jax.experimental import pallas as pl
from jax.experimental.pallas import tpu as pltpu
NT = (((1,), (1,)), ((), ()))
SM = pl.BlockSpec(memory_space=pltpu.SMEM)
VM = pl.BlockSpec(memory_space=pltpu.VMEM)
HBM = pl.BlockSpec(memory_space=pltpu.HBM)
PITCH = 136
VMEM_BYTES = 58 << 20
f32 = jnp.float32
bf16 = jnp.bfloat16

def split(x):
    hi = x.astype(bf16)
    return hi, (x - hi.astype(f32)).astype(bf16)

def stack(x):
    hi, lo = split(x)
    return jnp.concatenate([hi, lo], axis=0)

def fold(x):
    half = x.shape[0] // 2
    return x[:half] + x[half:]

def both(x):
    return x + pltpu.roll(x, 64, 1)

def low_lanes(shape):
    return lax.broadcasted_iota(jnp.int32, shape, 1) < 64

def up_body(basis_hbm, values_hbm, moves_hbm, up, share, trans_hbm, rows, basis, values, moves, trans, sem):
    leaves = basis.shape[0]
    columns = values.shape[0]
    nodes = moves.shape[2]
    reads = []
    for i in range(4):
        at = pl.ds(16 * i, 16)
        reads.append(pltpu.make_async_copy(moves_hbm.at[at], moves.at[at], sem.at[i]))
    reads.append(pltpu.make_async_copy(values_hbm, values, sem.at[4]))
    reads.append(pltpu.make_async_copy(basis_hbm, basis, sem.at[5]))
    for read in reads:
        read.start()
    for i in range(4):
        reads[i].wait()

        @pl.loop(16 * i, 16 * i + 16, unroll=8)
        def _(r):
            block = jnp.transpose(moves[r])
            rows[pl.ds(pl.multiple_of(r * PITCH, 8), nodes)] = jnp.concatenate([block, block], axis=1)

    left = low_lanes((64, 128))

    def node(n):
        x = rows[pl.ds(n, 64, stride=PITCH), :]
        hi = x.astype(bf16).astype(f32)
        trans[n] = jnp.where(left, hi, x - hi).astype(bf16)

    whole = nodes // 8 * 8
    pl.loop(0, whole, unroll=8)(node)
    for n in range(whole, nodes):
        node(n)
    trans[nodes] = jnp.zeros(trans.shape[1:], bf16)
    write = pltpu.make_async_copy(trans, trans_hbm, sem.at[6])
    write.start()

    half = low_lanes((columns, 128))

    for read in reads[4:]:
        read.wait()

    def leaf_up(i):
        v = stack(values[:, pl.ds(pl.multiple_of(i * 128, 128), 128)])
        return both(fold(lax.dot_general(v, stack(basis[i]), NT, preferred_element_type=f32)))

    @pl.loop(0, leaves // 2, unroll=8)
    def _(p):
        up[p] = jnp.where(half, leaf_up(2 * p), leaf_up(2 * p + 1))

    def lift(tile, row):
        t = jnp.concatenate([trans[row], trans[row + 1]], axis=0)
        return both(fold(jnp.dot(stack(tile), t, preferred_element_type=f32)))

    def pair(tile_a, tile_b, row):
        return jnp.where(half, lift(tile_a, row), lift(tile_b, row + 2))

    start, row, width = 0, 0, leaves
    while width > 16:
        after = start + width // 2

        @pl.loop(0, width // 16)
        def _(g, start=start, row=row, after=after):
            made = []
            for p in range(4):
                q = 4 * g + p
                made.append(pair(up[start + 2 * q], up[start + 2 * q + 1], row + 4 * q))
            for p in range(4):
                up[after + 4 * g + p] = made[p]

        start, row, width = after, row + width, width // 2
    tiles = [up[start + p] for p in range(width // 2)]
    while width > 1:
        after = start + width // 2
        if width >= 4:
            tiles = [pair(tiles[2 * p], tiles[2 * p + 1], row + 4 * p) for p in range(width // 4)]
        else:
            tiles = [lift(tiles[0], row)]
        if after < leaves - 1:
            for p, tile in enumerate(tiles):
                up[after + p] = tile
        start, row, width = after, row + width, width // 2
    up[leaves - 1] = tiles[0]
    share[...] = both(fold(jnp.dot(stack(tiles[0])[:, 0:64], trans[row], preferred_element_type=f32)))
    write.wait()


def up_pass(basis, values, moves):
    leaves = basis.shape[0]
    columns = values.shape[0]
    nodes = moves.shape[2]
    return pl.pallas_call(
        up_body,
        out_shape=(
            jax.ShapeDtypeStruct((leaves, columns, 128), f32),
            jax.ShapeDtypeStruct((columns, 128), f32),
            jax.ShapeDtypeStruct((nodes + 1, 64, 128), bf16),
        ),
        in_specs=[HBM, HBM, HBM],
        out_specs=(VM, VM, HBM),
        scratch_shapes=[
            pltpu.VMEM((64 * PITCH, 128), f32),
            pltpu.VMEM(basis.shape, f32),
            pltpu.VMEM(values.shape, f32),
            pltpu.VMEM(moves.shape, f32),
            pltpu.VMEM((nodes + 1, 64, 128), bf16),
            pltpu.SemaphoreType.DMA((7,)),
        ],
        compiler_params=pltpu.CompilerParams(vmem_limit_bytes=VMEM_BYTES),
        cost_estimate=pl.CostEstimate(flops=400_000_000, bytes_accessed=8_000_000, transcendentals=0),
        name="up_pass",
    )(basis, values, moves)


CHUNK = 32


def unbatch_body(part, matrices, out, held, rows, made, in_sem, out_sem):
    nodes = matrices.shape[3]
    pieces = 4
    step = matrices.shape[1] // pieces
    reads = []
    for i in range(pieces):
        at = pl.ds(i * step, step)
        reads.append(
            pltpu.make_async_copy(matrices.at[pl.ds(2 * part, 2), at], held.at[:, at], in_sem.at[i])
        )
        reads[-1].start()
    for i in range(pieces):
        reads[i].wait()

        @pl.loop(i * step, (i + 1) * step, unroll=8)
        def _(r):
            x = jnp.concatenate([held[0, r], held[1, r]], axis=0)
            rows[pl.ds(pl.multiple_of(r * PITCH, 8), nodes)] = jnp.transpose(x)

    def one(n):
        hi, lo = split(rows[pl.ds(n, 64, stride=PITCH), :])
        made[n, 0:64] = hi
        made[n, 64:128] = lo

    writes = []
    for c, begin in enumerate(range(0, nodes, CHUNK)):
        size = min(CHUNK, nodes - begin)
        whole = begin + size // 8 * 8
        pl.loop(begin, whole, unroll=8)(one)
        for n in range(whole, begin + size):
            one(n)
        at = pl.ds(begin, size)
        writes.append(pltpu.make_async_copy(made.at[at], out.at[at], out_sem.at[c]))
        writes[-1].start()
    for write in writes:
        write.wait()


def unbatch(matrices, part):
    nodes = matrices.shape[3]
    return pl.pallas_call(
        functools.partial(unbatch_body, part),
        out_shape=jax.ShapeDtypeStruct((nodes, 128, 128), bf16),
        in_specs=[HBM],
        out_specs=HBM,
        scratch_shapes=[
            pltpu.VMEM((2, *matrices.shape[1:]), f32),
            pltpu.VMEM((64 * PITCH, 128), f32),
            pltpu.VMEM((nodes, 128, 128), bf16),
            pltpu.SemaphoreType.DMA((4,)),
            pltpu.SemaphoreType.DMA((-(-nodes // CHUNK),)),
        ],
        compiler_params=pltpu.CompilerParams(vmem_limit_bytes=VMEM_BYTES),
        cost_estimate=pl.CostEstimate(flops=1_000, bytes_accessed=1_000, transcendentals=0),
        name="unbatch",
    )(matrices)


def top_body(place, partners, far_three, far_two, far_one, own, moves, matrices, parent, up, block, sem):
    spot = place[0]
    columns = own.shape[1]
    copies = []
    width, row = 32, 0
    for level in range(4):
        index = row + spot // (2 << level)
        copies.append(pltpu.make_async_copy(matrices.at[index], block.at[level], sem.at[level]))
        copies[-1].start()
        row, width = row + width, width // 2
    half = low_lanes((columns, 128))
    for j, ref in enumerate((far_three, far_two, far_one, own)):
        up[pl.ds(4 * ((spot // 16 + 1 + j) % 4), 4)] = ref[...]
    def lift(tile, r):
        t = jnp.concatenate([moves[r], moves[r + 1]], axis=0)
        hi, lo = split(t)
        x = stack(up[tile])
        z = fold(jnp.dot(x, hi, preferred_element_type=f32)) + jnp.dot(x[:columns], lo, preferred_element_type=f32)
        return jnp.concatenate([z, z], axis=1)
    tile0, row, width = 0, 0, 32
    tiles, rows = [], []
    while width >= 4:
        tiles.append(tile0)
        rows.append(row)
        nxt = tile0 + width // 2
        if width > 4:
            for p in range(width // 4):
                up[nxt + p] = jnp.where(half, lift(tile0 + 2 * p, row + 4 * p), lift(tile0 + 2 * p + 1, row + 4 * p + 2))
        tile0, row, width = nxt, row + width, width // 2
    def push(d, r):
        hi, lo = split(moves[r])
        x = stack(d)
        return fold(lax.dot_general(x, hi, NT, preferred_element_type=f32)) + lax.dot_general(x[:columns], lo, NT, preferred_element_type=f32)
    for copy in copies:
        copy.wait()
    fars = []
    for level in range(4):
        index = rows[level] + spot // (2 << level)
        far = jnp.zeros((columns, 64), f32)
        for k in range(4):
            p = partners[index, k]
            tile = up[tiles[level] + p // 2]
            x = stack(jnp.where(p % 2 == 0, tile, pltpu.roll(tile, 64, 1))[:, 0:64])
            hi, lo = split(block[level, k])
            far = far + fold(lax.dot_general(x, hi, NT, preferred_element_type=f32))
            far = far + lax.dot_general(x[:columns], lo, NT, preferred_element_type=f32)
        fars.append(far)
    down = jnp.zeros((columns, 64), f32)
    down = push(down, row + spot // 32)
    for level in range(3, -1, -1):
        down = push(down, rows[level] + spot // (2 << level)) + fars[level]
    parent[...] = jnp.concatenate([down, down], axis=1)

def top_pass(place, partners, gathered, moves, matrices):
    columns = gathered[0].shape[1]
    return pl.pallas_call(
        top_body,
        out_shape=jax.ShapeDtypeStruct((columns, 128), f32),
        in_specs=[SM, SM] + [VM] * 5 + [HBM],
        out_specs=VM,
        scratch_shapes=[pltpu.VMEM((32, columns, 128), f32), pltpu.VMEM((4, 4, 64, 64), f32), pltpu.SemaphoreType.DMA((4,))],
        compiler_params=pltpu.CompilerParams(vmem_limit_bytes=VMEM_BYTES),
        cost_estimate=pl.CostEstimate(flops=50_000_000, bytes_accessed=2_000_000, transcendentals=0),
        name="top_pass",
    )(place, partners, *gathered, moves, matrices)


def couple_body(codes, low, own, high, first, second, far, gather, tiles, held, sem):
    leaves, columns, _ = own.shape
    nodes = first.shape[0]
    takes = []
    for side, ref in enumerate((low, own, high)):
        takes.append(pltpu.make_async_copy(ref, tiles.at[side], sem.at[3 + side]))
        takes[-1].start()
    reads = []
    for i in range(3):
        begin = 42 * i
        at = pl.ds(begin, nodes - begin if i == 2 else 42)
        for h, x in enumerate((first, second)):
            reads.append(pltpu.make_async_copy(x.at[at], held.at[h, at], sem.at[6 + 2 * i + h]))
            reads[-1].start()
    half = low_lanes((columns, 128))
    left = low_lanes((2 * columns, 128))
    for side in range(3):
        takes[side].wait()

        @pl.loop(0, leaves, unroll=16)
        def _(t, side=side):
            x = tiles[side, t]
            gather[0, side * leaves + t] = stack(x)
            gather[1, side * leaves + t] = stack(pltpu.roll(x, 64, 1))

    def pick(n, k, side):
        code = codes[n, k]
        return gather[(code & 1) ^ side, code >> 1]

    def one(n):
        x = jnp.concatenate(
            [
                jnp.where(left, pick(n, 0, 0), pick(n, 1, 1)),
                jnp.where(left, pick(n, 2, 0), pick(n, 3, 1)),
            ],
            axis=1,
        )
        m = jnp.concatenate([held[0, n], held[1, n]], axis=1)
        return both(fold(lax.dot_general(x, m, NT, preferred_element_type=f32)))

    for i in range(3):
        reads[2 * i].wait()
        reads[2 * i + 1].wait()

        @pl.loop(21 * i, 21 * i + 21, unroll=7)
        def _(t):
            far[t] = jnp.where(half, one(2 * t), one(2 * t + 1))

    far[leaves - 1] = one(nodes - 1)


def couple_pass(codes, low, own, high, first, second):
    leaves, columns, _ = own.shape
    return pl.pallas_call(
        couple_body,
        out_shape=jax.ShapeDtypeStruct((leaves, columns, 128), f32),
        in_specs=[SM] + [HBM] * 5,
        out_specs=VM,
        scratch_shapes=[
            pltpu.VMEM((2, 3 * leaves, 2 * columns, 128), bf16),
            pltpu.VMEM((3, leaves, columns, 128), f32),
            pltpu.VMEM((2, *first.shape), bf16),
            pltpu.SemaphoreType.DMA((12,)),
        ],
        compiler_params=pltpu.CompilerParams(vmem_limit_bytes=VMEM_BYTES),
        cost_estimate=pl.CostEstimate(flops=400_000_000, bytes_accessed=12_000_000, transcendentals=0),
        name="couple_pass",
    )(codes, low, own, high, first, second)


def down_body(core, parent, far_hbm, trans_hbm, basis_hbm, mine, given, out, far, trans, basis, ones, twos, sem):
    leaves = basis.shape[0]
    columns = out.shape[0]
    reads = []
    for i, (source, dest) in enumerate(((far_hbm, far), (trans_hbm, trans), (basis_hbm, basis))):
        reads.append(pltpu.make_async_copy(source, dest, sem.at[i]))
        reads[-1].start()
    half = low_lanes((columns, 128))

    def push(d, tile):
        t = jnp.concatenate([trans[2 * tile], trans[2 * tile + 1]], axis=0)
        return fold(lax.dot_general(stack(d), t, NT, preferred_element_type=f32)) + far[tile]

    def spread(tile):
        turned = pltpu.roll(tile, 64, 1)
        return jnp.where(half, tile, turned), jnp.where(half, turned, tile)

    last = leaves - 1
    above = stack(parent[...])
    reads[0].wait()
    reads[1].wait()
    t = trans[2 * last]
    t = jnp.concatenate([t, t], axis=0)
    sources = [fold(lax.dot_general(above, t, NT, preferred_element_type=f32)) + far[last]]
    start, width = last, 1
    while width < 16:
        start = start - width
        made = [push(d, start + i) for i, d in enumerate(sources)]
        sources = [d for tile in made for d in spread(tile)]
        width = 2 * width
    start = start - width
    for i, d in enumerate(sources):
        ones[i] = push(d, start + i)

    @pl.loop(0, width, unroll=8)
    def _(i):
        for u, d in enumerate(spread(ones[i])):
            twos[2 * i + u] = push(d, 2 * i + u)

    reads[2].wait()

    @pl.loop(0, leaves // 2, unroll=4)
    def _(i):
        for u, d in enumerate(spread(twos[i])):
            leaf = 2 * i + u
            out[:, pl.ds(pl.multiple_of(leaf * 128, 128), 128)] = fold(
                jnp.dot(stack(d), stack(basis[leaf]), preferred_element_type=f32)
            )

    size = mine.shape[1]
    out[:, pl.ds(pl.multiple_of(core[0] * size, size), size)] += mine[...]
    out[:, pl.ds(pl.multiple_of((1 - core[0]) * size, size), size)] += given[...]


def down_pass(core, parent, far, trans, basis, mine, given):
    leaves = basis.shape[0]
    columns = parent.shape[0]
    return pl.pallas_call(
        down_body,
        out_shape=jax.ShapeDtypeStruct((columns, leaves * 128), f32),
        in_specs=[SM, VM, HBM, HBM, HBM, VM, VM],
        out_specs=VM,
        scratch_shapes=[
            pltpu.VMEM(far.shape, f32),
            pltpu.VMEM(trans.shape, bf16),
            pltpu.VMEM(basis.shape, f32),
            pltpu.VMEM((leaves // 4, columns, 128), f32),
            pltpu.VMEM((leaves // 2, columns, 128), f32),
            pltpu.SemaphoreType.DMA((3,)),
        ],
        compiler_params=pltpu.CompilerParams(vmem_limit_bytes=VMEM_BYTES),
        cost_estimate=pl.CostEstimate(flops=200_000_000, bytes_accessed=7_000_000, transcendentals=0),
        name="down_pass",
    )(core, parent, far, trans, basis, mine, given)


near_weight = 0.1
smoothing = 0.0025
SLOTS = 28
PAIR = 2

def near_body(unroll, chunks, core, lists, counts, targets, *refs):
    origins, refs = refs[: 2 * chunks], refs[2 * chunks :]
    begin, spots = None, [targets]
    if chunks == 2:
        begin, spots, refs = refs[0:2], refs[2:4], refs[4:]
    mine, other, columns_of, total, weights, places, sem, *sources = refs
    leaves = mine.shape[1] // 128
    width = sources[0].shape[1] // 128
    core = core[0]
    reads = []
    for i, (origin, source) in enumerate(zip(origins, sources)):
        reads.append(pltpu.make_async_copy(origin, source, sem.at[i]))
        reads[-1].start()
    weights[chunks * width] = jnp.zeros(weights.shape[1:], bf16)
    places[chunks * width] = jnp.zeros(places.shape[1:], f32)
    blank = jnp.zeros((5, 128), f32)

    @pl.loop(0, leaves // 16)
    def _(g):
        rows = []
        for u in range(16):
            at = pl.ds(pl.multiple_of((core * leaves + 16 * g + u) * 128, 128), 128)
            rows += [targets[:, at], blank]
        t = jnp.transpose(jnp.concatenate(rows, axis=0))
        for u in range(16):
            for c in range(3):
                columns_of[16 * g + u, c] = jnp.broadcast_to(t[:, 8 * u + c : 8 * u + c + 1], (128, 128))
            total[16 * g + u] = jnp.zeros((128, 128), f32)

    for read in reads:
        read.wait()
    for c in range(chunks):
        near_ref, far_ref = sources[2 * c], sources[2 * c + 1]
        lower = 0 if chunks == 1 or c == 1 else core * (leaves // 8)
        upper = width // 8 if chunks == 1 or c == 0 else (core + 1) * (leaves // 8)

        @pl.loop(lower, upper)
        def _(g, c=c, near_ref=near_ref, far_ref=far_ref):
            for u in range(8):
                j = 8 * g + u
                at = pl.ds(pl.multiple_of(j * 128, 128), 128)
                x = near_weight * jnp.concatenate([near_ref[:, at], far_ref[:, at]], axis=0)
                weights[c * width + j] = stack(x)
                places[c * width + j, 0:3] = spots[c][:, at]

    items = lax.fori_loop(
        0, leaves, lambda i, s: s + jnp.maximum((counts[i] + PAIR - 1) // PAIR, 1), jnp.int32(0)
    )

    def block(leaf, slot):
        kernels, parts = [], []
        for u in range(PAIR):
            j = lists[leaf, slot + u]
            s = places[j]
            d = columns_of[leaf, 0] - s[0:1]
            squared = d * d + smoothing
            d = columns_of[leaf, 1] - s[1:2]
            squared = squared + d * d
            d = columns_of[leaf, 2] - s[2:3]
            squared = squared + d * d
            kernels += split(lax.rsqrt(squared))
            x = weights[j]
            parts += [x, x]
        return lax.dot_general(
            jnp.concatenate(kernels, axis=1),
            jnp.concatenate(parts, axis=1),
            NT,
            preferred_element_type=f32,
        )

    def step(b, carry):
        leaf, slot = carry
        made = []
        for u in range(unroll):
            place = jnp.where(b * unroll + u < items, leaf, leaves)
            made.append((place, block(leaf, slot)))
            done = slot + PAIR >= counts[leaf]
            leaf = jnp.where(done, jnp.minimum(leaf + 1, leaves - 1), leaf)
            slot = jnp.where(done, 0, slot + PAIR)
        for place, x in made:
            total[place] += x
        return leaf, slot

    lax.fori_loop(0, (items + unroll - 1) // unroll, step, (jnp.int32(0), jnp.int32(0)))

    @pl.loop(0, leaves, unroll=8)
    def _(leaf):
        at = pl.ds(pl.multiple_of(leaf * 128, 128), 128)
        x = jnp.transpose(both(total[leaf]))
        if begin is None:
            mine[:, at] = x[0:32]
            other[:, at] = x[32:64]
        else:
            mine[:, at] = begin[0][:, at] + x[0:32]
            other[:, at] = begin[1][:, at] + x[32:64]


def near_pass(unroll, core, lists, counts, targets, sources, begin=(), spots=()):
    leaves = lists.shape[0]
    chunks = len(sources) // 2
    held = chunks * (sources[0].shape[1] // 128) + 1
    side = jax.ShapeDtypeStruct((32, leaves * 128), f32)
    arrays = (targets, *sources, *begin, *spots)
    return pl.pallas_call(
        functools.partial(near_body, unroll, chunks),
        out_shape=(side, side),
        in_specs=[SM, SM, SM, VM] + [HBM] * len(sources) + [VM] * 2 * len(begin),
        out_specs=(VM, VM),
        scratch_shapes=[
            pltpu.VMEM((leaves, 3, 128, 128), f32),
            pltpu.VMEM((leaves + 1, 128, 128), f32),
            pltpu.VMEM((held, 128, 128), bf16),
            pltpu.VMEM((held, 8, 128), f32),
            pltpu.SemaphoreType.DMA((len(sources),)),
            *[pltpu.VMEM(x.shape, f32) for x in sources],
        ],
        compiler_params=pltpu.CompilerParams(vmem_limit_bytes=VMEM_BYTES),
        cost_estimate=pl.CostEstimate(flops=1_000, bytes_accessed=1_000, transcendentals=0),
        name="near_pass",
    )(core, lists, counts, *arrays)


def arranged(picked, leaf_ids, empty):
    slots = picked.shape[1]
    before = jnp.arange(slots)[:, None] < jnp.arange(slots)[None, :]
    rank = jnp.sum(jnp.where(picked[:, :, None] & before[None], 1, 0), axis=1)
    to = jnp.arange(SLOTS)[None, None, :]
    here = picked[:, :, None] & (rank[:, :, None] == to)
    found = jnp.sum(jnp.where(here, leaf_ids[:, :, None], 0), axis=1)
    count = jnp.sum(picked.astype(jnp.int32), axis=1)
    lists = jnp.where(jnp.arange(SLOTS)[None, :] < count[:, None], found, empty)
    return lists.astype(jnp.int32), count


def partner_codes(partners, position, leaves):
    spans, starts = [], []
    width, tile = leaves, 0
    while width >= 1:
        spans += [width] * width
        starts += [2 * tile] * width
        tile, width = tile + max(1, width // 2), width // 2
    spans = jnp.array(spans, jnp.int32)[:, None]
    starts = jnp.array(starts, jnp.int32)[:, None]
    local = partners - position * spans
    side = jnp.where(local < 0, 0, jnp.where(local < spans, 1, 2))
    return (side * (2 * leaves) + starts + local - (side - 1) * spans)


def local(
    points,
    values,
    near_list,
    near_count,
    basis,
    transfer,
    coupling,
    partners,
    transfer_top,
    coupling_top,
    partners_top,
):
    leaves = basis.shape[0]
    position = lax.axis_index("leaf")
    core = lax.axis_index("rhs")
    count = lax.axis_size("leaf")
    forward = [(i, i + 1) for i in range(count - 1)]
    backward = [(target, source) for source, target in forward]
    swap = [(0, 1), (1, 0)]
    low = lax.ppermute(values, "leaf", forward)
    high = lax.ppermute(values, "leaf", backward)
    spots = (lax.ppermute(points, "leaf", forward), lax.ppermute(points, "leaf", backward))
    across = lax.ppermute(values, "rhs", swap)
    half = leaves // 2
    chosen = lax.dynamic_slice_in_dim(near_list, core * half, half, 0) - position * leaves
    live = lax.dynamic_slice_in_dim(near_count, core * half, half, 0)
    alive = jnp.arange(chosen.shape[1])[None, :] < live[:, None]
    inside = (chosen >= 0) & (chosen < leaves)
    near_ids, near_live = arranged(alive & inside, chosen, leaves)
    outside_ids = jnp.where(chosen < 0, chosen + leaves, chosen)
    far_ids, far_live = arranged(alive & ~inside, outside_ids, 2 * leaves)
    codes = partner_codes(partners, position, leaves)

    def ring(x, stride):
        spot = (position // stride) % 4
        turned = []
        for shift in range(3, 0, -1):
            to = [(i, i + stride * ((i // stride + shift) % 4 - i // stride % 4)) for i in range(count)]
            turned.append(lax.ppermute(x, "leaf", to))
        return turned, spot

    def in_order(turned, x, spot):
        blocks = [*turned, x]
        ordered = []
        for k in range(4):
            block = blocks[3]
            for j in range(3):
                block = jnp.where(spot == (k - j - 1) % 4, blocks[j], block)
            ordered.append(block)
        return jnp.concatenate(ordered, axis=0)

    after = lax.optimization_barrier
    core = core[None].astype(jnp.int32)
    up, share, trans = up_pass(basis, values, transfer.transpose(1, 2, 0))
    near_ids, far_ids, codes, up = after((near_ids, far_ids, codes, up))
    begin = near_pass(12, core, near_ids, near_live, points, (values, across))
    low, high, spots, coupling, share, begin = after((low, high, spots, coupling, share, begin))
    turned, spot = ring(share[None], 1)
    low_across = lax.ppermute(low, "rhs", swap)
    high_across = lax.ppermute(high, "rhs", swap)
    coupling = coupling.transpose(1, 2, 3, 0)
    first = unbatch(coupling, 0)
    turned, low_across, high_across, up, coupling, first = after(
        (turned, low_across, high_across, up, coupling, first)
    )
    level = in_order(turned, share[None], spot)
    level = jnp.where(jnp.arange(128) < 64, level[0] + level[1], level[2] + level[3])[None]
    turned, spot = ring(level, 4)
    up_low = lax.ppermute(up, "leaf", forward)
    up_high = lax.ppermute(up, "leaf", backward)
    second = unbatch(coupling, 1)
    turned, far_ids, second = after((turned, far_ids, second))
    level = in_order(turned, level, spot)
    turned, spot = ring(level, 16)
    mine, other = near_pass(
        12, core, far_ids, far_live, points, (low, low_across, high, high_across), begin, spots
    )
    turned, mine, other = after((turned, mine, other))
    given = lax.ppermute(other, "rhs", swap)
    parent = top_pass(
        position[None].astype(jnp.int32), partners_top, (*turned, level), transfer_top, coupling_top
    )
    up_low, up_high, parent = after((up_low, up_high, parent))
    far = couple_pass(codes, up_low, up, up_high, first, second)
    return down_pass(core, parent, far, trans, basis, mine, given)


def solution(mesh):
    placed = (
        P(None, "leaf"),
        P("rhs", "leaf"),
        P("leaf", None),
        P("leaf"),
        P("leaf", None, None),
        P("leaf", None, None),
        P("leaf", None, None, None),
        P("leaf", None),
        P(),
        P(),
        P(),
    )
    return jax.shard_map(
        local, mesh=mesh, in_specs=placed, out_specs=P("rhs", "leaf"), check_vma=False
    )
```

```python
import jax, jax.numpy as jnp, functools
from jax import lax
from jax.sharding import PartitionSpec as P
from jax.experimental import pallas as pl
from jax.experimental.pallas import tpu as pltpu
NT = (((1,), (1,)), ((), ()))
SM = pl.BlockSpec(memory_space=pltpu.SMEM)
VM = pl.BlockSpec(memory_space=pltpu.VMEM)
HBM = pl.BlockSpec(memory_space=pltpu.HBM)
PITCH = 136
VMEM_BYTES = 62 << 20
SLOTS = 28
f32 = jnp.float32
bf16 = jnp.bfloat16

def split(x):
    hi = x.astype(bf16)
    return hi, (x - hi.astype(f32)).astype(bf16)

def stack(x):
    hi, lo = split(x)
    return jnp.concatenate([hi, lo], axis=0)

def fold(x):
    half = x.shape[0] // 2
    return x[:half] + x[half:]

def both(x):
    return x + pltpu.roll(x, 64, 1)

def low_lanes(shape):
    return lax.broadcasted_iota(jnp.int32, shape, 1) < 64

def pack_body(points, values, out, sem):
    columns = values.shape[0]
    read = pltpu.make_async_copy(values, out.at[pl.ds(0, columns)], sem)
    read.start()
    out[columns:] = jnp.concatenate(
        [points[...], jnp.zeros((out.shape[0] - columns - 3, out.shape[1]), f32)], axis=0
    )
    read.wait()


def pack(points, values):
    columns, width = values.shape
    return pl.pallas_call(
        pack_body,
        out_shape=jax.ShapeDtypeStruct((columns + 8, width), f32),
        in_specs=[VM, HBM],
        out_specs=VM,
        scratch_shapes=[pltpu.SemaphoreType.DMA],
        compiler_params=pltpu.CompilerParams(vmem_limit_bytes=VMEM_BYTES),
        name="pack",
    )(points, values)


def plan(place, near_list, near_count, partners, lists, live, codes):
    slots, leaves = near_list.shape
    local = near_list[...] - place * leaves
    count = near_count[...]
    inside = (local >= 0) & (local < leaves)
    row = lax.broadcasted_iota(jnp.int32, (SLOTS, leaves), 0)
    for side in range(2):
        rank = jnp.zeros((1, leaves), jnp.int32)
        found = jnp.full((SLOTS, leaves), (1 + side) * leaves, jnp.int32)
        for s in range(slots):
            here = inside[s : s + 1] if side == 0 else jnp.logical_not(inside[s : s + 1])
            picked = here & (s < count)
            ids = local[s : s + 1]
            if side == 1:
                ids = jnp.where(ids < 0, ids + leaves, ids)
            found = jnp.where((row == rank) & picked, ids, found)
            rank = rank + picked.astype(jnp.int32)
        lists[side] = found
        live[side : side + 1] = rank
    nodes = partners.shape[1]
    node = lax.broadcasted_iota(jnp.int32, (1, nodes), 1)
    span = jnp.full((1, nodes), leaves, jnp.int32)
    start = jnp.zeros((1, nodes), jnp.int32)
    width, tile, first = leaves // 2, leaves // 2, leaves
    while width >= 1:
        span = jnp.where(node >= first, width, span)
        start = jnp.where(node >= first, 2 * tile, start)
        tile, first, width = tile + max(1, width // 2), first + width, width // 2
    shifted = partners[...] - place * span
    side = jnp.where(shifted < 0, 0, jnp.where(shifted < span, 1, 2))
    codes[...] = side * (2 * leaves) + start + shifted - (side - 1) * span


def up_body(
    place, near_list, near_count, partners, basis_hbm, values_hbm, moves_hbm,
    up, share, trans_hbm, lists, live, codes, rows, basis, values, moves, trans, sem,
):
    leaves = basis.shape[0]
    columns = values.shape[0]
    nodes = moves.shape[2]
    reads = []
    for i in range(4):
        at = pl.ds(16 * i, 16)
        reads.append(pltpu.make_async_copy(moves_hbm.at[at], moves.at[at], sem.at[i]))
    reads.append(pltpu.make_async_copy(values_hbm, values, sem.at[4]))
    reads.append(pltpu.make_async_copy(basis_hbm, basis, sem.at[5]))
    for read in reads:
        read.start()
    plan(place[0], near_list, near_count, partners, lists, live, codes)
    for i in range(4):
        reads[i].wait()

        @pl.loop(16 * i, 16 * i + 16, unroll=8)
        def _(r):
            block = jnp.transpose(moves[r])
            rows[pl.ds(pl.multiple_of(r * PITCH, 8), nodes)] = jnp.concatenate([block, block], axis=1)

    left = low_lanes((64, 128))

    def node(n):
        x = rows[pl.ds(n, 64, stride=PITCH), :]
        hi = x.astype(bf16).astype(f32)
        trans[n] = jnp.where(left, hi, x - hi).astype(bf16)

    whole = nodes // 8 * 8
    pl.loop(0, whole, unroll=8)(node)
    for n in range(whole, nodes):
        node(n)
    trans[nodes] = jnp.zeros(trans.shape[1:], bf16)
    write = pltpu.make_async_copy(trans, trans_hbm, sem.at[6])
    write.start()

    half = low_lanes((columns, 128))

    for read in reads[4:]:
        read.wait()

    def leaf_up(i):
        v = stack(values[:, pl.ds(pl.multiple_of(i * 128, 128), 128)])
        return both(fold(lax.dot_general(v, stack(basis[i]), NT, preferred_element_type=f32)))

    @pl.loop(0, leaves // 2, unroll=8)
    def _(p):
        up[p] = jnp.where(half, leaf_up(2 * p), leaf_up(2 * p + 1))

    def lift(tile, row):
        t = jnp.concatenate([trans[row], trans[row + 1]], axis=0)
        return both(fold(jnp.dot(stack(tile), t, preferred_element_type=f32)))

    def pair(tile_a, tile_b, row):
        return jnp.where(half, lift(tile_a, row), lift(tile_b, row + 2))

    start, row, width = 0, 0, leaves
    while width > 16:
        after = start + width // 2

        @pl.loop(0, width // 16)
        def _(g, start=start, row=row, after=after):
            made = []
            for p in range(4):
                q = 4 * g + p
                made.append(pair(up[start + 2 * q], up[start + 2 * q + 1], row + 4 * q))
            for p in range(4):
                up[after + 4 * g + p] = made[p]

        start, row, width = after, row + width, width // 2
    tiles = [up[start + p] for p in range(width // 2)]
    while width > 1:
        after = start + width // 2
        if width >= 4:
            tiles = [pair(tiles[2 * p], tiles[2 * p + 1], row + 4 * p) for p in range(width // 4)]
        else:
            tiles = [lift(tiles[0], row)]
        if after < leaves - 1:
            for p, tile in enumerate(tiles):
                up[after + p] = tile
        start, row, width = after, row + width, width // 2
    up[leaves - 1] = tiles[0]
    share[...] = both(fold(jnp.dot(stack(tiles[0])[:, 0:64], trans[row], preferred_element_type=f32)))
    write.wait()


def up_pass(place, near_list, near_count, partners, basis, values, moves):
    leaves = basis.shape[0]
    columns = values.shape[0]
    nodes = moves.shape[2]
    return pl.pallas_call(
        up_body,
        out_shape=(
            jax.ShapeDtypeStruct((leaves, columns, 128), f32),
            jax.ShapeDtypeStruct((columns, 128), f32),
            jax.ShapeDtypeStruct((nodes + 1, 64, 128), bf16),
            jax.ShapeDtypeStruct((2, SLOTS, leaves), jnp.int32),
            jax.ShapeDtypeStruct((2, leaves), jnp.int32),
            jax.ShapeDtypeStruct(partners.shape, jnp.int32),
        ),
        in_specs=[SM, VM, VM, VM, HBM, HBM, HBM],
        out_specs=(VM, VM, HBM, VM, VM, VM),
        scratch_shapes=[
            pltpu.VMEM((64 * PITCH, 128), f32),
            pltpu.VMEM(basis.shape, f32),
            pltpu.VMEM(values.shape, f32),
            pltpu.VMEM(moves.shape, f32),
            pltpu.VMEM((nodes + 1, 64, 128), bf16),
            pltpu.SemaphoreType.DMA((7,)),
        ],
        compiler_params=pltpu.CompilerParams(vmem_limit_bytes=VMEM_BYTES),
        cost_estimate=pl.CostEstimate(flops=400_000_000, bytes_accessed=8_000_000, transcendentals=0),
        name="up_pass",
    )(place, near_list, near_count, partners, basis, values, moves)


CHUNK = 32


def unbatch_body(part, matrices, out, held, rows, made, in_sem, out_sem):
    nodes = matrices.shape[3]
    pieces = 4
    step = matrices.shape[1] // pieces
    reads = []
    for i in range(pieces):
        at = pl.ds(i * step, step)
        reads.append(
            pltpu.make_async_copy(matrices.at[pl.ds(2 * part, 2), at], held.at[:, at], in_sem.at[i])
        )
        reads[-1].start()
    for i in range(pieces):
        reads[i].wait()

        @pl.loop(i * step, (i + 1) * step, unroll=8)
        def _(r):
            x = jnp.concatenate([held[0, r], held[1, r]], axis=0)
            rows[pl.ds(pl.multiple_of(r * PITCH, 8), nodes)] = jnp.transpose(x)

    def one(n):
        hi, lo = split(rows[pl.ds(n, 64, stride=PITCH), :])
        made[n, 0:64] = hi
        made[n, 64:128] = lo

    writes = []
    for c, begin in enumerate(range(0, nodes, CHUNK)):
        size = min(CHUNK, nodes - begin)
        whole = begin + size // 8 * 8
        pl.loop(begin, whole, unroll=8)(one)
        for n in range(whole, begin + size):
            one(n)
        at = pl.ds(begin, size)
        writes.append(pltpu.make_async_copy(made.at[at], out.at[at], out_sem.at[c]))
        writes[-1].start()
    for write in writes:
        write.wait()


def unbatch(matrices, part):
    nodes = matrices.shape[3]
    return pl.pallas_call(
        functools.partial(unbatch_body, part),
        out_shape=jax.ShapeDtypeStruct((nodes, 128, 128), bf16),
        in_specs=[HBM],
        out_specs=HBM,
        scratch_shapes=[
            pltpu.VMEM((2, *matrices.shape[1:]), f32),
            pltpu.VMEM((64 * PITCH, 128), f32),
            pltpu.VMEM((nodes, 128, 128), bf16),
            pltpu.SemaphoreType.DMA((4,)),
            pltpu.SemaphoreType.DMA((-(-nodes // CHUNK),)),
        ],
        compiler_params=pltpu.CompilerParams(vmem_limit_bytes=VMEM_BYTES),
        cost_estimate=pl.CostEstimate(flops=1_000, bytes_accessed=1_000, transcendentals=0),
        name="unbatch",
    )(matrices)


def top_body(place, partners, far_three, far_two, far_one, own, moves, matrices, parent, up, block, sem):
    spot = place[0]
    columns = own.shape[1]
    copies = []
    width, row = 32, 0
    for level in range(4):
        index = row + spot // (2 << level)
        copies.append(pltpu.make_async_copy(matrices.at[index], block.at[level], sem.at[level]))
        copies[-1].start()
        row, width = row + width, width // 2
    half = low_lanes((columns, 128))
    for j, ref in enumerate((far_three, far_two, far_one, own)):
        up[pl.ds(4 * ((spot // 16 + 1 + j) % 4), 4)] = ref[...]
    def lift(tile, r):
        t = jnp.concatenate([moves[r], moves[r + 1]], axis=0)
        hi, lo = split(t)
        x = stack(up[tile])
        z = fold(jnp.dot(x, hi, preferred_element_type=f32)) + jnp.dot(x[:columns], lo, preferred_element_type=f32)
        return jnp.concatenate([z, z], axis=1)
    tile0, row, width = 0, 0, 32
    tiles, rows = [], []
    while width >= 4:
        tiles.append(tile0)
        rows.append(row)
        nxt = tile0 + width // 2
        if width > 4:
            for p in range(width // 4):
                up[nxt + p] = jnp.where(half, lift(tile0 + 2 * p, row + 4 * p), lift(tile0 + 2 * p + 1, row + 4 * p + 2))
        tile0, row, width = nxt, row + width, width // 2
    def push(d, r):
        hi, lo = split(moves[r])
        x = stack(d)
        return fold(lax.dot_general(x, hi, NT, preferred_element_type=f32)) + lax.dot_general(x[:columns], lo, NT, preferred_element_type=f32)
    for copy in copies:
        copy.wait()
    fars = []
    for level in range(4):
        index = rows[level] + spot // (2 << level)
        far = jnp.zeros((columns, 64), f32)
        for k in range(4):
            p = partners[k, index]
            tile = up[tiles[level] + p // 2]
            x = stack(jnp.where(p % 2 == 0, tile, pltpu.roll(tile, 64, 1))[:, 0:64])
            hi, lo = split(block[level, k])
            far = far + fold(lax.dot_general(x, hi, NT, preferred_element_type=f32))
            far = far + lax.dot_general(x[:columns], lo, NT, preferred_element_type=f32)
        fars.append(far)
    down = jnp.zeros((columns, 64), f32)
    down = push(down, row + spot // 32)
    for level in range(3, -1, -1):
        down = push(down, rows[level] + spot // (2 << level)) + fars[level]
    parent[...] = jnp.concatenate([down, down], axis=1)

def top_pass(place, partners, gathered, moves, matrices):
    columns = gathered[0].shape[1]
    return pl.pallas_call(
        top_body,
        out_shape=jax.ShapeDtypeStruct((columns, 128), f32),
        in_specs=[SM, SM] + [VM] * 5 + [HBM],
        out_specs=VM,
        scratch_shapes=[pltpu.VMEM((32, columns, 128), f32), pltpu.VMEM((4, 4, 64, 64), f32), pltpu.SemaphoreType.DMA((4,))],
        compiler_params=pltpu.CompilerParams(vmem_limit_bytes=VMEM_BYTES),
        cost_estimate=pl.CostEstimate(flops=50_000_000, bytes_accessed=2_000_000, transcendentals=0),
        name="top_pass",
    )(place, partners, *gathered, moves, matrices)


def couple_body(codes, low, own, high, first, second, far, gather, tiles, held, sem):
    leaves, columns, _ = own.shape
    nodes = first.shape[0]
    takes = []
    for side, ref in enumerate((low, own, high)):
        takes.append(pltpu.make_async_copy(ref, tiles.at[side], sem.at[3 + side]))
        takes[-1].start()
    reads = []
    for i in range(3):
        begin = 42 * i
        at = pl.ds(begin, nodes - begin if i == 2 else 42)
        for h, x in enumerate((first, second)):
            reads.append(pltpu.make_async_copy(x.at[at], held.at[h, at], sem.at[6 + 2 * i + h]))
            reads[-1].start()
    half = low_lanes((columns, 128))
    left = low_lanes((2 * columns, 128))
    for side in range(3):
        takes[side].wait()

        @pl.loop(0, leaves, unroll=16)
        def _(t, side=side):
            x = tiles[side, t]
            gather[0, side * leaves + t] = stack(x)
            gather[1, side * leaves + t] = stack(pltpu.roll(x, 64, 1))

    def pick(n, k, side):
        code = codes[k, n]
        return gather[(code & 1) ^ side, code >> 1]

    def one(n):
        x = jnp.concatenate(
            [
                jnp.where(left, pick(n, 0, 0), pick(n, 1, 1)),
                jnp.where(left, pick(n, 2, 0), pick(n, 3, 1)),
            ],
            axis=1,
        )
        m = jnp.concatenate([held[0, n], held[1, n]], axis=1)
        return both(fold(lax.dot_general(x, m, NT, preferred_element_type=f32)))

    for i in range(3):
        reads[2 * i].wait()
        reads[2 * i + 1].wait()

        @pl.loop(21 * i, 21 * i + 21, unroll=7)
        def _(t):
            far[t] = jnp.where(half, one(2 * t), one(2 * t + 1))

    far[leaves - 1] = one(nodes - 1)


def couple_pass(codes, low, own, high, first, second):
    leaves, columns, _ = own.shape
    return pl.pallas_call(
        couple_body,
        out_shape=jax.ShapeDtypeStruct((leaves, columns, 128), f32),
        in_specs=[SM] + [HBM] * 5,
        out_specs=VM,
        scratch_shapes=[
            pltpu.VMEM((2, 3 * leaves, 2 * columns, 128), bf16),
            pltpu.VMEM((3, leaves, columns, 128), f32),
            pltpu.VMEM((2, *first.shape), bf16),
            pltpu.SemaphoreType.DMA((12,)),
        ],
        compiler_params=pltpu.CompilerParams(vmem_limit_bytes=VMEM_BYTES),
        cost_estimate=pl.CostEstimate(flops=400_000_000, bytes_accessed=12_000_000, transcendentals=0),
        name="couple_pass",
    )(codes, low, own, high, first, second)


def down_body(core, parent, far_hbm, trans_hbm, basis_hbm, mine, given, out, far, trans, basis, ones, twos, sem):
    leaves = basis.shape[0]
    columns = out.shape[0]
    reads = []
    for i, (source, dest) in enumerate(((far_hbm, far), (trans_hbm, trans), (basis_hbm, basis))):
        reads.append(pltpu.make_async_copy(source, dest, sem.at[i]))
        reads[-1].start()
    half = low_lanes((columns, 128))

    def push(d, tile):
        t = jnp.concatenate([trans[2 * tile], trans[2 * tile + 1]], axis=0)
        return fold(lax.dot_general(stack(d), t, NT, preferred_element_type=f32)) + far[tile]

    def spread(tile):
        turned = pltpu.roll(tile, 64, 1)
        return jnp.where(half, tile, turned), jnp.where(half, turned, tile)

    last = leaves - 1
    above = stack(parent[...])
    reads[0].wait()
    reads[1].wait()
    t = trans[2 * last]
    t = jnp.concatenate([t, t], axis=0)
    sources = [fold(lax.dot_general(above, t, NT, preferred_element_type=f32)) + far[last]]
    start, width = last, 1
    while width < 16:
        start = start - width
        made = [push(d, start + i) for i, d in enumerate(sources)]
        sources = [d for tile in made for d in spread(tile)]
        width = 2 * width
    start = start - width
    for i, d in enumerate(sources):
        ones[i] = push(d, start + i)

    @pl.loop(0, width, unroll=8)
    def _(i):
        for u, d in enumerate(spread(ones[i])):
            twos[2 * i + u] = push(d, 2 * i + u)

    reads[2].wait()

    @pl.loop(0, leaves // 2, unroll=4)
    def _(i):
        for u, d in enumerate(spread(twos[i])):
            leaf = 2 * i + u
            out[:, pl.ds(pl.multiple_of(leaf * 128, 128), 128)] = fold(
                jnp.dot(stack(d), stack(basis[leaf]), preferred_element_type=f32)
            )

    size = mine.shape[1]
    out[:, pl.ds(pl.multiple_of(core[0] * size, size), size)] += mine[...]
    out[:, pl.ds(pl.multiple_of((1 - core[0]) * size, size), size)] += given[...]


def down_pass(core, parent, far, trans, basis, mine, given):
    leaves = basis.shape[0]
    columns = parent.shape[0]
    return pl.pallas_call(
        down_body,
        out_shape=jax.ShapeDtypeStruct((columns, leaves * 128), f32),
        in_specs=[SM, VM, HBM, HBM, HBM, VM, VM],
        out_specs=VM,
        scratch_shapes=[
            pltpu.VMEM(far.shape, f32),
            pltpu.VMEM(trans.shape, bf16),
            pltpu.VMEM(basis.shape, f32),
            pltpu.VMEM((leaves // 4, columns, 128), f32),
            pltpu.VMEM((leaves // 2, columns, 128), f32),
            pltpu.SemaphoreType.DMA((3,)),
        ],
        compiler_params=pltpu.CompilerParams(vmem_limit_bytes=VMEM_BYTES),
        cost_estimate=pl.CostEstimate(flops=200_000_000, bytes_accessed=7_000_000, transcendentals=0),
        name="down_pass",
    )(core, parent, far, trans, basis, mine, given)


near_weight = 0.1
smoothing = 0.0025
PAIR = 2

def near_body(unroll, chunks, core, lists, live, targets, *refs):
    origins, refs = refs[: 2 * chunks], refs[2 * chunks :]
    begin = None
    if chunks == 2:
        begin, refs = refs[0:2], refs[2:]
    mine, other, columns_of, total, weights, places, sem, *sources = refs
    leaves = mine.shape[1] // 128
    width = sources[0].shape[1] // 128
    core = core[0]
    side = chunks - 1
    base = core * leaves
    reads = []
    for i, (origin, source) in enumerate(zip(origins, sources)):
        reads.append(pltpu.make_async_copy(origin, source, sem.at[i]))
        reads[-1].start()
    weights[chunks * width] = jnp.zeros(weights.shape[1:], bf16)
    places[chunks * width] = jnp.zeros(places.shape[1:], f32)
    blank = jnp.zeros((5, 128), f32)

    @pl.loop(0, leaves // 16)
    def _(g):
        rows = []
        for u in range(16):
            at = pl.ds(pl.multiple_of((core * leaves + 16 * g + u) * 128, 128), 128)
            rows += [targets[:, at], blank]
        t = jnp.transpose(jnp.concatenate(rows, axis=0))
        for u in range(16):
            for c in range(3):
                columns_of[16 * g + u, c] = jnp.broadcast_to(t[:, 8 * u + c : 8 * u + c + 1], (128, 128))
            total[16 * g + u] = jnp.zeros((128, 128), f32)

    for read in reads:
        read.wait()
    for c in range(chunks):
        near_ref, far_ref = sources[2 * c], sources[2 * c + 1]
        lower = 0 if chunks == 1 or c == 1 else core * (leaves // 8)
        upper = width // 8 if chunks == 1 or c == 0 else (core + 1) * (leaves // 8)

        @pl.loop(lower, upper)
        def _(g, c=c, near_ref=near_ref, far_ref=far_ref):
            for u in range(8):
                j = 8 * g + u
                at = pl.ds(pl.multiple_of(j * 128, 128), 128)
                x = near_weight * jnp.concatenate([near_ref[0:32, at], far_ref[0:32, at]], axis=0)
                weights[c * width + j] = stack(x)
                places[c * width + j, 0:3] = near_ref[32:35, at]

    items = lax.fori_loop(
        0, leaves, lambda i, s: s + jnp.maximum((live[side, base + i] + PAIR - 1) // PAIR, 1), jnp.int32(0)
    )

    def block(leaf, slot):
        kernels, parts = [], []
        for u in range(PAIR):
            j = lists[side, slot + u, base + leaf]
            s = places[j]
            d = columns_of[leaf, 0] - s[0:1]
            squared = d * d + smoothing
            d = columns_of[leaf, 1] - s[1:2]
            squared = squared + d * d
            d = columns_of[leaf, 2] - s[2:3]
            squared = squared + d * d
            kernels += split(lax.rsqrt(squared))
            x = weights[j]
            parts += [x, x]
        return lax.dot_general(
            jnp.concatenate(kernels, axis=1),
            jnp.concatenate(parts, axis=1),
            NT,
            preferred_element_type=f32,
        )

    def step(b, carry):
        leaf, slot = carry
        made = []
        for u in range(unroll):
            place = jnp.where(b * unroll + u < items, leaf, leaves)
            made.append((place, block(leaf, slot)))
            done = slot + PAIR >= live[side, base + leaf]
            leaf = jnp.where(done, jnp.minimum(leaf + 1, leaves - 1), leaf)
            slot = jnp.where(done, 0, slot + PAIR)
        for place, x in made:
            total[place] += x
        return leaf, slot

    lax.fori_loop(0, (items + unroll - 1) // unroll, step, (jnp.int32(0), jnp.int32(0)))

    @pl.loop(0, leaves, unroll=8)
    def _(leaf):
        at = pl.ds(pl.multiple_of(leaf * 128, 128), 128)
        x = jnp.transpose(both(total[leaf]))
        if begin is None:
            mine[:, at] = x[0:32]
            other[:, at] = x[32:64]
        else:
            mine[:, at] = begin[0][:, at] + x[0:32]
            other[:, at] = begin[1][:, at] + x[32:64]


def near_pass(unroll, core, lists, live, targets, sources, begin=()):
    leaves = lists.shape[2] // 2
    chunks = len(sources) // 2
    held = chunks * (sources[0].shape[1] // 128) + 1
    side = jax.ShapeDtypeStruct((32, leaves * 128), f32)
    arrays = (targets, *sources, *begin)
    return pl.pallas_call(
        functools.partial(near_body, unroll, chunks),
        out_shape=(side, side),
        in_specs=[SM, SM, SM, VM] + [HBM] * len(sources) + [VM] * len(begin),
        out_specs=(VM, VM),
        scratch_shapes=[
            pltpu.VMEM((leaves, 3, 128, 128), f32),
            pltpu.VMEM((leaves + 1, 128, 128), f32),
            pltpu.VMEM((held, 128, 128), bf16),
            pltpu.VMEM((held, 8, 128), f32),
            pltpu.SemaphoreType.DMA((len(sources),)),
            *[pltpu.VMEM(x.shape, f32) for x in sources],
        ],
        compiler_params=pltpu.CompilerParams(vmem_limit_bytes=VMEM_BYTES),
        cost_estimate=pl.CostEstimate(flops=1_000, bytes_accessed=1_000, transcendentals=0),
        name="near_pass",
    )(core, lists, live, *arrays)


def local(
    points,
    values,
    near_list,
    near_count,
    basis,
    transfer,
    coupling,
    partners,
    transfer_top,
    coupling_top,
    partners_top,
):
    leaves = basis.shape[0]
    position = lax.axis_index("leaf")
    core = lax.axis_index("rhs")
    count = lax.axis_size("leaf")
    forward = [(i, i + 1) for i in range(count - 1)]
    backward = [(target, source) for source, target in forward]
    swap = [(0, 1), (1, 0)]
    packed = pack(points, values)
    low = lax.ppermute(packed, "leaf", forward)
    high = lax.ppermute(packed, "leaf", backward)
    across = lax.ppermute(values, "rhs", swap)

    def ring(x, stride):
        spot = (position // stride) % 4
        turned = []
        for shift in range(3, 0, -1):
            to = [(i, i + stride * ((i // stride + shift) % 4 - i // stride % 4)) for i in range(count)]
            turned.append(lax.ppermute(x, "leaf", to))
        return turned, spot

    def in_order(turned, x, spot):
        blocks = [*turned, x]
        ordered = []
        for k in range(4):
            block = blocks[3]
            for j in range(3):
                block = jnp.where(spot == (k - j - 1) % 4, blocks[j], block)
            ordered.append(block)
        return jnp.concatenate(ordered, axis=0)

    after = lax.optimization_barrier
    core = core[None].astype(jnp.int32)
    place = position[None].astype(jnp.int32)
    up, share, trans, lists, live, codes = up_pass(
        place, near_list.T, near_count[None], partners.T, basis, values, transfer.transpose(1, 2, 0)
    )
    begin = near_pass(12, core, lists, live, points, (packed, across))
    low, high, coupling, share, begin = after((low, high, coupling, share, begin))
    turned, spot = ring(share[None], 1)
    low_across = lax.ppermute(low, "rhs", swap)
    high_across = lax.ppermute(high, "rhs", swap)
    coupling = coupling.transpose(1, 2, 3, 0)
    first = unbatch(coupling, 0)
    turned, low_across, high_across, up, coupling, first = after(
        (turned, low_across, high_across, up, coupling, first)
    )
    level = in_order(turned, share[None], spot)
    level = jnp.where(jnp.arange(128) < 64, level[0] + level[1], level[2] + level[3])[None]
    turned, spot = ring(level, 4)
    second = unbatch(coupling, 1)
    turned, lists, up, second = after((turned, lists, up, second))
    level = in_order(turned, level, spot)
    turned, spot = ring(level, 16)
    up_low = lax.ppermute(up, "leaf", forward)
    up_high = lax.ppermute(up, "leaf", backward)
    mine, other = near_pass(
        12, core, lists, live, points, (low, low_across, high, high_across), begin
    )
    given = lax.ppermute(other, "rhs", swap)
    mine, up_low, up_high = after((mine, up_low, up_high))
    far = couple_pass(codes, up_low, up, up_high, first, second)
    turned, far = after((turned, far))
    parent = top_pass(place, partners_top.T, (*turned, level), transfer_top, coupling_top)
    return down_pass(core, parent, far, trans, basis, mine, given)


def solution(mesh):
    placed = (
        P(None, "leaf"),
        P("rhs", "leaf"),
        P("leaf", None),
        P("leaf"),
        P("leaf", None, None),
        P("leaf", None, None),
        P("leaf", None, None, None),
        P("leaf", None),
        P(),
        P(),
        P(),
    )
    return jax.shard_map(
        local, mesh=mesh, in_specs=placed, out_specs=P("rhs", "leaf"), check_vma=False
    )
```

```python
import jax, jax.numpy as jnp, functools
from jax import lax
from jax.sharding import PartitionSpec as P
from jax.experimental import pallas as pl
from jax.experimental.pallas import tpu as pltpu
NT = (((1,), (1,)), ((), ()))
SM = pl.BlockSpec(memory_space=pltpu.SMEM)
VM = pl.BlockSpec(memory_space=pltpu.VMEM)
HBM = pl.BlockSpec(memory_space=pltpu.HBM)
PITCH = 136
VMEM_BYTES = 62 << 20
SLOTS = 28
f32 = jnp.float32
bf16 = jnp.bfloat16

def split(x):
    hi = x.astype(bf16)
    return hi, (x - hi.astype(f32)).astype(bf16)

def stack(x):
    hi, lo = split(x)
    return jnp.concatenate([hi, lo], axis=0)

def fold(x):
    half = x.shape[0] // 2
    return x[:half] + x[half:]

def both(x):
    return x + pltpu.roll(x, 64, 1)

def low_lanes(shape):
    return lax.broadcasted_iota(jnp.int32, shape, 1) < 64

def plan(place, near_list, near_count, partners, lists, live, codes):
    slots, leaves = near_list.shape
    local = near_list[...] - place * leaves
    count = near_count[...]
    inside = (local >= 0) & (local < leaves)
    row = lax.broadcasted_iota(jnp.int32, (SLOTS, leaves), 0)
    for side in range(2):
        rank = jnp.zeros((1, leaves), jnp.int32)
        found = jnp.full((SLOTS, leaves), (1 + side) * leaves, jnp.int32)
        for s in range(slots):
            here = inside[s : s + 1] if side == 0 else jnp.logical_not(inside[s : s + 1])
            picked = here & (s < count)
            ids = local[s : s + 1]
            if side == 1:
                ids = jnp.where(ids < 0, ids + leaves, ids)
            found = jnp.where((row == rank) & picked, ids, found)
            rank = rank + picked.astype(jnp.int32)
        lists[side] = found
        live[side : side + 1] = rank
    nodes = partners.shape[1]
    node = lax.broadcasted_iota(jnp.int32, (1, nodes), 1)
    span = jnp.full((1, nodes), leaves, jnp.int32)
    start = jnp.zeros((1, nodes), jnp.int32)
    width, tile, first = leaves // 2, leaves // 2, leaves
    while width >= 1:
        span = jnp.where(node >= first, width, span)
        start = jnp.where(node >= first, 2 * tile, start)
        tile, first, width = tile + max(1, width // 2), first + width, width // 2
    shifted = partners[...] - place * span
    side = jnp.where(shifted < 0, 0, jnp.where(shifted < span, 1, 2))
    codes[...] = side * (2 * leaves) + start + shifted - (side - 1) * span


def up_body(
    place, near_list, near_count, partners, points, basis_hbm, values_hbm, moves_hbm,
    up, share, trans_hbm, packed_hbm, lists, live, codes, rows, basis, values, moves, trans, packed, sem,
):
    leaves = basis.shape[0]
    columns = values.shape[0]
    nodes = moves.shape[2]
    reads = []
    for i in range(4):
        at = pl.ds(16 * i, 16)
        reads.append(pltpu.make_async_copy(moves_hbm.at[at], moves.at[at], sem.at[i]))
    reads.append(pltpu.make_async_copy(values_hbm, values, sem.at[4]))
    reads.append(pltpu.make_async_copy(basis_hbm, basis, sem.at[5]))
    for read in reads:
        read.start()
    plan(place[0], near_list, near_count, partners, lists, live, codes)
    for i in range(4):
        reads[i].wait()

        @pl.loop(16 * i, 16 * i + 16, unroll=8)
        def _(r):
            block = jnp.transpose(moves[r])
            rows[pl.ds(pl.multiple_of(r * PITCH, 8), nodes)] = jnp.concatenate([block, block], axis=1)

    left = low_lanes((64, 128))

    def node(n):
        x = rows[pl.ds(n, 64, stride=PITCH), :]
        hi = x.astype(bf16).astype(f32)
        trans[n] = jnp.where(left, hi, x - hi).astype(bf16)

    whole = nodes // 8 * 8
    pl.loop(0, whole, unroll=8)(node)
    for n in range(whole, nodes):
        node(n)
    trans[nodes] = jnp.zeros(trans.shape[1:], bf16)
    write = pltpu.make_async_copy(trans, trans_hbm, sem.at[6])
    write.start()

    half = low_lanes((columns, 128))

    for read in reads[4:]:
        read.wait()
    for c in range(3):
        for j in range(leaves):
            row = leaves * c + j
            packed[leaves + row // columns, row % columns : row % columns + 1] = points[
                c : c + 1, 128 * j : 128 * j + 128
            ]

    @pl.loop(0, leaves, unroll=8)
    def _(j):
        packed[j] = values[:, pl.ds(pl.multiple_of(j * 128, 128), 128)]

    send = pltpu.make_async_copy(packed, packed_hbm, sem.at[7])
    send.start()

    def leaf_up(i):
        v = stack(values[:, pl.ds(pl.multiple_of(i * 128, 128), 128)])
        return both(fold(lax.dot_general(v, stack(basis[i]), NT, preferred_element_type=f32)))

    @pl.loop(0, leaves // 2, unroll=8)
    def _(p):
        up[p] = jnp.where(half, leaf_up(2 * p), leaf_up(2 * p + 1))

    def lift(tile, row):
        t = jnp.concatenate([trans[row], trans[row + 1]], axis=0)
        return both(fold(jnp.dot(stack(tile), t, preferred_element_type=f32)))

    def pair(tile_a, tile_b, row):
        return jnp.where(half, lift(tile_a, row), lift(tile_b, row + 2))

    start, row, width = 0, 0, leaves
    while width > 16:
        after = start + width // 2

        @pl.loop(0, width // 16)
        def _(g, start=start, row=row, after=after):
            made = []
            for p in range(4):
                q = 4 * g + p
                made.append(pair(up[start + 2 * q], up[start + 2 * q + 1], row + 4 * q))
            for p in range(4):
                up[after + 4 * g + p] = made[p]

        start, row, width = after, row + width, width // 2
    tiles = [up[start + p] for p in range(width // 2)]
    while width > 1:
        after = start + width // 2
        if width >= 4:
            tiles = [pair(tiles[2 * p], tiles[2 * p + 1], row + 4 * p) for p in range(width // 4)]
        else:
            tiles = [lift(tiles[0], row)]
        if after < leaves - 1:
            for p, tile in enumerate(tiles):
                up[after + p] = tile
        start, row, width = after, row + width, width // 2
    up[leaves - 1] = tiles[0]
    share[...] = both(fold(jnp.dot(stack(tiles[0])[:, 0:64], trans[row], preferred_element_type=f32)))
    write.wait()
    send.wait()


def up_pass(place, near_list, near_count, partners, points, basis, values, moves):
    leaves = basis.shape[0]
    columns = values.shape[0]
    nodes = moves.shape[2]
    return pl.pallas_call(
        up_body,
        out_shape=(
            jax.ShapeDtypeStruct((leaves, columns, 128), f32),
            jax.ShapeDtypeStruct((columns, 128), f32),
            jax.ShapeDtypeStruct((nodes + 1, 64, 128), bf16),
            jax.ShapeDtypeStruct((leaves + 3 * leaves // columns, columns, 128), f32),
            jax.ShapeDtypeStruct((2, SLOTS, leaves), jnp.int32),
            jax.ShapeDtypeStruct((2, leaves), jnp.int32),
            jax.ShapeDtypeStruct(partners.shape, jnp.int32),
        ),
        in_specs=[SM, VM, VM, VM, VM, HBM, HBM, HBM],
        out_specs=(VM, VM, HBM, HBM, VM, VM, VM),
        scratch_shapes=[
            pltpu.VMEM((64 * PITCH, 128), f32),
            pltpu.VMEM(basis.shape, f32),
            pltpu.VMEM(values.shape, f32),
            pltpu.VMEM(moves.shape, f32),
            pltpu.VMEM((nodes + 1, 64, 128), bf16),
            pltpu.VMEM((leaves + 3 * leaves // columns, columns, 128), f32),
            pltpu.SemaphoreType.DMA((8,)),
        ],
        compiler_params=pltpu.CompilerParams(vmem_limit_bytes=VMEM_BYTES),
        cost_estimate=pl.CostEstimate(flops=400_000_000, bytes_accessed=8_000_000, transcendentals=0),
        name="up_pass",
    )(place, near_list, near_count, partners, points, basis, values, moves)


CHUNK = 32


def unbatch_body(part, matrices, out, held, rows, made, in_sem, out_sem):
    nodes = matrices.shape[3]
    pieces = 4
    step = matrices.shape[1] // pieces
    reads = []
    for i in range(pieces):
        at = pl.ds(i * step, step)
        reads.append(
            pltpu.make_async_copy(matrices.at[pl.ds(2 * part, 2), at], held.at[:, at], in_sem.at[i])
        )
        reads[-1].start()
    for i in range(pieces):
        reads[i].wait()

        @pl.loop(i * step, (i + 1) * step, unroll=8)
        def _(r):
            x = jnp.concatenate([held[0, r], held[1, r]], axis=0)
            rows[pl.ds(pl.multiple_of(r * PITCH, 8), nodes)] = jnp.transpose(x)

    def one(n):
        hi, lo = split(rows[pl.ds(n, 64, stride=PITCH), :])
        made[n, 0:64] = hi
        made[n, 64:128] = lo

    writes = []
    for c, begin in enumerate(range(0, nodes, CHUNK)):
        size = min(CHUNK, nodes - begin)
        whole = begin + size // 8 * 8
        pl.loop(begin, whole, unroll=8)(one)
        for n in range(whole, begin + size):
            one(n)
        at = pl.ds(begin, size)
        writes.append(pltpu.make_async_copy(made.at[at], out.at[at], out_sem.at[c]))
        writes[-1].start()
    for write in writes:
        write.wait()


def unbatch(matrices, part):
    nodes = matrices.shape[3]
    return pl.pallas_call(
        functools.partial(unbatch_body, part),
        out_shape=jax.ShapeDtypeStruct((nodes, 128, 128), bf16),
        in_specs=[HBM],
        out_specs=HBM,
        scratch_shapes=[
            pltpu.VMEM((2, *matrices.shape[1:]), f32),
            pltpu.VMEM((64 * PITCH, 128), f32),
            pltpu.VMEM((nodes, 128, 128), bf16),
            pltpu.SemaphoreType.DMA((4,)),
            pltpu.SemaphoreType.DMA((-(-nodes // CHUNK),)),
        ],
        compiler_params=pltpu.CompilerParams(vmem_limit_bytes=VMEM_BYTES),
        cost_estimate=pl.CostEstimate(flops=1_000, bytes_accessed=1_000, transcendentals=0),
        name="unbatch",
    )(matrices)


def top_body(place, partners, far_three, far_two, far_one, own, moves, matrices, parent, up, block, sem):
    spot = place[0]
    columns = own.shape[1]
    copies = []
    width, row = 32, 0
    for level in range(4):
        index = row + spot // (2 << level)
        copies.append(pltpu.make_async_copy(matrices.at[index], block.at[level], sem.at[level]))
        copies[-1].start()
        row, width = row + width, width // 2
    half = low_lanes((columns, 128))
    for j, ref in enumerate((far_three, far_two, far_one, own)):
        up[pl.ds(4 * ((spot // 16 + 1 + j) % 4), 4)] = ref[...]
    def lift(tile, r):
        t = jnp.concatenate([moves[r], moves[r + 1]], axis=0)
        hi, lo = split(t)
        x = stack(up[tile])
        z = fold(jnp.dot(x, hi, preferred_element_type=f32)) + jnp.dot(x[:columns], lo, preferred_element_type=f32)
        return jnp.concatenate([z, z], axis=1)
    tile0, row, width = 0, 0, 32
    tiles, rows = [], []
    while width >= 4:
        tiles.append(tile0)
        rows.append(row)
        nxt = tile0 + width // 2
        if width > 4:
            for p in range(width // 4):
                up[nxt + p] = jnp.where(half, lift(tile0 + 2 * p, row + 4 * p), lift(tile0 + 2 * p + 1, row + 4 * p + 2))
        tile0, row, width = nxt, row + width, width // 2
    def push(d, r):
        hi, lo = split(moves[r])
        x = stack(d)
        return fold(lax.dot_general(x, hi, NT, preferred_element_type=f32)) + lax.dot_general(x[:columns], lo, NT, preferred_element_type=f32)
    for copy in copies:
        copy.wait()
    fars = []
    for level in range(4):
        index = rows[level] + spot // (2 << level)
        far = jnp.zeros((columns, 64), f32)
        for k in range(4):
            p = partners[k, index]
            tile = up[tiles[level] + p // 2]
            x = stack(jnp.where(p % 2 == 0, tile, pltpu.roll(tile, 64, 1))[:, 0:64])
            hi, lo = split(block[level, k])
            far = far + fold(lax.dot_general(x, hi, NT, preferred_element_type=f32))
            far = far + lax.dot_general(x[:columns], lo, NT, preferred_element_type=f32)
        fars.append(far)
    down = jnp.zeros((columns, 64), f32)
    down = push(down, row + spot // 32)
    for level in range(3, -1, -1):
        down = push(down, rows[level] + spot // (2 << level)) + fars[level]
    parent[...] = jnp.concatenate([down, down], axis=1)

def top_pass(place, partners, gathered, moves, matrices):
    columns = gathered[0].shape[1]
    return pl.pallas_call(
        top_body,
        out_shape=jax.ShapeDtypeStruct((columns, 128), f32),
        in_specs=[SM, SM] + [VM] * 5 + [HBM],
        out_specs=VM,
        scratch_shapes=[pltpu.VMEM((32, columns, 128), f32), pltpu.VMEM((4, 4, 64, 64), f32), pltpu.SemaphoreType.DMA((4,))],
        compiler_params=pltpu.CompilerParams(vmem_limit_bytes=VMEM_BYTES),
        cost_estimate=pl.CostEstimate(flops=50_000_000, bytes_accessed=2_000_000, transcendentals=0),
        name="top_pass",
    )(place, partners, *gathered, moves, matrices)


def couple_body(codes, low, own, high, first, second, far, gather, tiles, held, sem):
    leaves, columns, _ = own.shape
    nodes = first.shape[0]
    takes = []
    for side, ref in enumerate((low, own, high)):
        takes.append(pltpu.make_async_copy(ref, tiles.at[side], sem.at[3 + side]))
        takes[-1].start()
    reads = []
    for i in range(3):
        begin = 42 * i
        at = pl.ds(begin, nodes - begin if i == 2 else 42)
        for h, x in enumerate((first, second)):
            reads.append(pltpu.make_async_copy(x.at[at], held.at[h, at], sem.at[6 + 2 * i + h]))
            reads[-1].start()
    half = low_lanes((columns, 128))
    left = low_lanes((2 * columns, 128))
    for side in range(3):
        takes[side].wait()

        @pl.loop(0, leaves, unroll=16)
        def _(t, side=side):
            x = tiles[side, t]
            gather[0, side * leaves + t] = stack(x)
            gather[1, side * leaves + t] = stack(pltpu.roll(x, 64, 1))

    def pick(n, k, side):
        code = codes[k, n]
        return gather[(code & 1) ^ side, code >> 1]

    def one(n):
        x = jnp.concatenate(
            [
                jnp.where(left, pick(n, 0, 0), pick(n, 1, 1)),
                jnp.where(left, pick(n, 2, 0), pick(n, 3, 1)),
            ],
            axis=1,
        )
        m = jnp.concatenate([held[0, n], held[1, n]], axis=1)
        return both(fold(lax.dot_general(x, m, NT, preferred_element_type=f32)))

    for i in range(3):
        reads[2 * i].wait()
        reads[2 * i + 1].wait()

        @pl.loop(21 * i, 21 * i + 21, unroll=7)
        def _(t):
            far[t] = jnp.where(half, one(2 * t), one(2 * t + 1))

    far[leaves - 1] = one(nodes - 1)


def couple_pass(codes, low, own, high, first, second):
    leaves, columns, _ = own.shape
    return pl.pallas_call(
        couple_body,
        out_shape=jax.ShapeDtypeStruct((leaves, columns, 128), f32),
        in_specs=[SM] + [HBM] * 5,
        out_specs=VM,
        scratch_shapes=[
            pltpu.VMEM((2, 3 * leaves, 2 * columns, 128), bf16),
            pltpu.VMEM((3, leaves, columns, 128), f32),
            pltpu.VMEM((2, *first.shape), bf16),
            pltpu.SemaphoreType.DMA((12,)),
        ],
        compiler_params=pltpu.CompilerParams(vmem_limit_bytes=VMEM_BYTES),
        cost_estimate=pl.CostEstimate(flops=400_000_000, bytes_accessed=12_000_000, transcendentals=0),
        name="couple_pass",
    )(codes, low, own, high, first, second)


def down_body(core, parent, far_hbm, trans_hbm, basis_hbm, mine, given, out, far, trans, basis, ones, twos, sem):
    leaves = basis.shape[0]
    columns = out.shape[0]
    reads = []
    for i, (source, dest) in enumerate(((far_hbm, far), (trans_hbm, trans), (basis_hbm, basis))):
        reads.append(pltpu.make_async_copy(source, dest, sem.at[i]))
        reads[-1].start()
    half = low_lanes((columns, 128))

    def push(d, tile):
        t = jnp.concatenate([trans[2 * tile], trans[2 * tile + 1]], axis=0)
        return fold(lax.dot_general(stack(d), t, NT, preferred_element_type=f32)) + far[tile]

    def spread(tile):
        turned = pltpu.roll(tile, 64, 1)
        return jnp.where(half, tile, turned), jnp.where(half, turned, tile)

    last = leaves - 1
    above = stack(parent[...])
    reads[0].wait()
    reads[1].wait()
    t = trans[2 * last]
    t = jnp.concatenate([t, t], axis=0)
    sources = [fold(lax.dot_general(above, t, NT, preferred_element_type=f32)) + far[last]]
    start, width = last, 1
    while width < 16:
        start = start - width
        made = [push(d, start + i) for i, d in enumerate(sources)]
        sources = [d for tile in made for d in spread(tile)]
        width = 2 * width
    start = start - width
    for i, d in enumerate(sources):
        ones[i] = push(d, start + i)

    @pl.loop(0, width, unroll=8)
    def _(i):
        for u, d in enumerate(spread(ones[i])):
            twos[2 * i + u] = push(d, 2 * i + u)

    reads[2].wait()

    @pl.loop(0, leaves // 2, unroll=4)
    def _(i):
        for u, d in enumerate(spread(twos[i])):
            leaf = 2 * i + u
            out[:, pl.ds(pl.multiple_of(leaf * 128, 128), 128)] = fold(
                jnp.dot(stack(d), stack(basis[leaf]), preferred_element_type=f32)
            )

    size = mine.shape[1]
    out[:, pl.ds(pl.multiple_of(core[0] * size, size), size)] += mine[...]
    out[:, pl.ds(pl.multiple_of((1 - core[0]) * size, size), size)] += given[...]


def down_pass(core, parent, far, trans, basis, mine, given):
    leaves = basis.shape[0]
    columns = parent.shape[0]
    return pl.pallas_call(
        down_body,
        out_shape=jax.ShapeDtypeStruct((columns, leaves * 128), f32),
        in_specs=[SM, VM, HBM, HBM, HBM, VM, VM],
        out_specs=VM,
        scratch_shapes=[
            pltpu.VMEM(far.shape, f32),
            pltpu.VMEM(trans.shape, bf16),
            pltpu.VMEM(basis.shape, f32),
            pltpu.VMEM((leaves // 4, columns, 128), f32),
            pltpu.VMEM((leaves // 2, columns, 128), f32),
            pltpu.SemaphoreType.DMA((3,)),
        ],
        compiler_params=pltpu.CompilerParams(vmem_limit_bytes=VMEM_BYTES),
        cost_estimate=pl.CostEstimate(flops=200_000_000, bytes_accessed=7_000_000, transcendentals=0),
        name="down_pass",
    )(core, parent, far, trans, basis, mine, given)


near_weight = 0.1
smoothing = 0.0025
PAIR = 2

def near_body(unroll, chunks, core, lists, live, targets, *refs):
    origins, refs = refs[: 2 * chunks], refs[2 * chunks :]
    begin = None
    if chunks == 2:
        begin, refs = refs[0:2], refs[2:]
    mine, other, columns_of, total, weights, places, sem, *sources = refs
    leaves = mine.shape[1] // 128
    width = 2 * leaves
    core = core[0]
    side = chunks - 1
    base = core * leaves
    reads = []
    for i, (origin, source) in enumerate(zip(origins, sources)):
        reads.append(pltpu.make_async_copy(origin, source, sem.at[i]))
        reads[-1].start()
    weights[chunks * width] = jnp.zeros(weights.shape[1:], bf16)
    places[chunks * width] = jnp.zeros(places.shape[1:], f32)
    blank = jnp.zeros((5, 128), f32)

    @pl.loop(0, leaves // 16)
    def _(g):
        rows = []
        for u in range(16):
            at = pl.ds(pl.multiple_of((core * leaves + 16 * g + u) * 128, 128), 128)
            rows += [targets[:, at], blank]
        t = jnp.transpose(jnp.concatenate(rows, axis=0))
        for u in range(16):
            for c in range(3):
                columns_of[16 * g + u, c] = jnp.broadcast_to(t[:, 8 * u + c : 8 * u + c + 1], (128, 128))
            total[16 * g + u] = jnp.zeros((128, 128), f32)

    for read in reads:
        read.wait()
    for c in range(chunks):
        near_ref, far_ref = sources[2 * c], sources[2 * c + 1]
        lower = 0 if chunks == 1 or c == 1 else core * (leaves // 8)
        upper = width // 8 if chunks == 1 or c == 0 else (core + 1) * (leaves // 8)

        @pl.loop(lower, upper)
        def _(g, c=c, near_ref=near_ref, far_ref=far_ref):
            for u in range(8):
                j = 8 * g + u
                at = pl.ds(pl.multiple_of(j * 128, 128), 128)
                beside = far_ref[:, at] if chunks == 1 else far_ref[j]
                x = near_weight * jnp.concatenate([near_ref[j], beside], axis=0)
                weights[c * width + j] = stack(x)
                for k in range(3):
                    row = width * k + j
                    places[c * width + j, k : k + 1] = near_ref[width + row // 32, pl.ds(row % 32, 1)]

    items = lax.fori_loop(
        0, leaves, lambda i, s: s + jnp.maximum((live[side, base + i] + PAIR - 1) // PAIR, 1), jnp.int32(0)
    )

    def block(leaf, slot):
        kernels, parts = [], []
        for u in range(PAIR):
            j = lists[side, slot + u, base + leaf]
            s = places[j]
            d = columns_of[leaf, 0] - s[0:1]
            squared = d * d + smoothing
            d = columns_of[leaf, 1] - s[1:2]
            squared = squared + d * d
            d = columns_of[leaf, 2] - s[2:3]
            squared = squared + d * d
            kernels += split(lax.rsqrt(squared))
            x = weights[j]
            parts += [x, x]
        return lax.dot_general(
            jnp.concatenate(kernels, axis=1),
            jnp.concatenate(parts, axis=1),
            NT,
            preferred_element_type=f32,
        )

    def step(b, carry):
        leaf, slot = carry
        made = []
        for u in range(unroll):
            place = jnp.where(b * unroll + u < items, leaf, leaves)
            made.append((place, block(leaf, slot)))
            done = slot + PAIR >= live[side, base + leaf]
            leaf = jnp.where(done, jnp.minimum(leaf + 1, leaves - 1), leaf)
            slot = jnp.where(done, 0, slot + PAIR)
        for place, x in made:
            total[place] += x
        return leaf, slot

    lax.fori_loop(0, (items + unroll - 1) // unroll, step, (jnp.int32(0), jnp.int32(0)))

    @pl.loop(0, leaves, unroll=8)
    def _(leaf):
        at = pl.ds(pl.multiple_of(leaf * 128, 128), 128)
        x = jnp.transpose(both(total[leaf]))
        if begin is None:
            mine[:, at] = x[0:32]
            other[:, at] = x[32:64]
        else:
            mine[:, at] = begin[0][:, at] + x[0:32]
            other[:, at] = begin[1][:, at] + x[32:64]


def near_pass(unroll, core, lists, live, targets, sources, begin=()):
    leaves = lists.shape[2] // 2
    chunks = len(sources) // 2
    held = chunks * 2 * leaves + 1
    side = jax.ShapeDtypeStruct((32, leaves * 128), f32)
    arrays = (targets, *sources, *begin)
    return pl.pallas_call(
        functools.partial(near_body, unroll, chunks),
        out_shape=(side, side),
        in_specs=[SM, SM, SM, VM] + [HBM] * len(sources) + [VM] * len(begin),
        out_specs=(VM, VM),
        scratch_shapes=[
            pltpu.VMEM((leaves, 3, 128, 128), f32),
            pltpu.VMEM((leaves + 1, 128, 128), f32),
            pltpu.VMEM((held, 128, 128), bf16),
            pltpu.VMEM((held, 8, 128), f32),
            pltpu.SemaphoreType.DMA((len(sources),)),
            *[pltpu.VMEM(x.shape, f32) for x in sources],
        ],
        compiler_params=pltpu.CompilerParams(vmem_limit_bytes=VMEM_BYTES),
        cost_estimate=pl.CostEstimate(flops=1_000, bytes_accessed=1_000, transcendentals=0),
        name="near_pass",
    )(core, lists, live, *arrays)


def local(
    points,
    values,
    near_list,
    near_count,
    basis,
    transfer,
    coupling,
    partners,
    transfer_top,
    coupling_top,
    partners_top,
):
    leaves = basis.shape[0]
    position = lax.axis_index("leaf")
    core = lax.axis_index("rhs")
    count = lax.axis_size("leaf")
    forward = [(i, i + 1) for i in range(count - 1)]
    backward = [(target, source) for source, target in forward]
    swap = [(0, 1), (1, 0)]
    across = lax.ppermute(values, "rhs", swap)

    def ring(x, stride):
        spot = (position // stride) % 4
        turned = []
        for shift in range(3, 0, -1):
            to = [(i, i + stride * ((i // stride + shift) % 4 - i // stride % 4)) for i in range(count)]
            turned.append(lax.ppermute(x, "leaf", to))
        return turned, spot

    def in_order(turned, x, spot):
        blocks = [*turned, x]
        ordered = []
        for k in range(4):
            block = blocks[3]
            for j in range(3):
                block = jnp.where(spot == (k - j - 1) % 4, blocks[j], block)
            ordered.append(block)
        return jnp.concatenate(ordered, axis=0)

    after = lax.optimization_barrier
    core = core[None].astype(jnp.int32)
    place = position[None].astype(jnp.int32)
    up, share, trans, packed, lists, live, codes = up_pass(
        place, near_list.T, near_count[None], partners.T, points, basis, values, transfer.transpose(1, 2, 0)
    )
    turned, spot = ring(share[None], 1)
    turned, share, packed = after((turned, share, packed))
    low = lax.ppermute(packed, "leaf", forward)
    high = lax.ppermute(packed, "leaf", backward)
    level = in_order(turned, share[None], spot)
    level = jnp.where(jnp.arange(128) < 64, level[0] + level[1], level[2] + level[3])[None]
    coupling = coupling.transpose(1, 2, 3, 0)
    first = unbatch(coupling, 0)
    lists, first, coupling, level, across = after((lists, first, coupling, level, across))
    turned, spot = ring(level, 4)
    begin = near_pass(12, core, lists, live, points, (packed, across))
    low, high, turned, up, coupling, begin = after((low, high, turned, up, coupling, begin))
    level = in_order(turned, level, spot)
    low_across = lax.ppermute(low, "rhs", swap)
    high_across = lax.ppermute(high, "rhs", swap)
    up_low = lax.ppermute(up, "leaf", forward)
    up_high = lax.ppermute(up, "leaf", backward)
    second = unbatch(coupling, 1)
    low_across, high_across, lists, second, level = after((low_across, high_across, lists, second, level))
    turned, spot = ring(level, 16)
    mine, other = near_pass(
        12, core, lists, live, points, (low, low_across, high, high_across), begin
    )
    turned, mine, other = after((turned, mine, other))
    given = lax.ppermute(other, "rhs", swap)
    parent = top_pass(place, partners_top.T, (*turned, level), transfer_top, coupling_top)
    parent, up_low, up_high = after((parent, up_low, up_high))
    far = couple_pass(codes, up_low, up, up_high, first, second)
    return down_pass(core, parent, far, trans, basis, mine, given)


def solution(mesh):
    placed = (
        P(None, "leaf"),
        P("rhs", "leaf"),
        P("leaf", None),
        P("leaf"),
        P("leaf", None, None),
        P("leaf", None, None),
        P("leaf", None, None, None),
        P("leaf", None),
        P(),
        P(),
        P(),
    )
    return jax.shard_map(
        local, mesh=mesh, in_specs=placed, out_specs=P("rhs", "leaf"), check_vma=False
    )
```

```python
import jax, jax.numpy as jnp, functools
from jax import lax
from jax.sharding import PartitionSpec as P
from jax.experimental import pallas as pl
from jax.experimental.pallas import tpu as pltpu
NT = (((1,), (1,)), ((), ()))
SM = pl.BlockSpec(memory_space=pltpu.SMEM)
VM = pl.BlockSpec(memory_space=pltpu.VMEM)
HBM = pl.BlockSpec(memory_space=pltpu.HBM)
PITCH = 136
VMEM_BYTES = 62 << 20
SLOTS = 28
f32 = jnp.float32
bf16 = jnp.bfloat16

def split(x):
    hi = x.astype(bf16)
    return hi, (x - hi.astype(f32)).astype(bf16)

def stack(x):
    hi, lo = split(x)
    return jnp.concatenate([hi, lo], axis=0)

def fold(x):
    half = x.shape[0] // 2
    return x[:half] + x[half:]

def both(x):
    return x + pltpu.roll(x, 64, 1)

def low_lanes(shape):
    return lax.broadcasted_iota(jnp.int32, shape, 1) < 64

def plan(place, near_list, near_count, partners, lists, live, codes):
    slots, leaves = near_list.shape
    local = near_list[...] - place * leaves
    count = near_count[...]
    inside = (local >= 0) & (local < leaves)
    row = lax.broadcasted_iota(jnp.int32, (SLOTS, leaves), 0)
    for side in range(2):
        rank = jnp.zeros((1, leaves), jnp.int32)
        found = jnp.full((SLOTS, leaves), (1 + side) * leaves, jnp.int32)
        for s in range(slots):
            here = inside[s : s + 1] if side == 0 else jnp.logical_not(inside[s : s + 1])
            picked = here & (s < count)
            ids = local[s : s + 1]
            if side == 1:
                ids = jnp.where(ids < 0, ids + leaves, ids)
            found = jnp.where((row == rank) & picked, ids, found)
            rank = rank + picked.astype(jnp.int32)
        lists[side] = found
        live[side : side + 1] = rank
    nodes = partners.shape[1]
    node = lax.broadcasted_iota(jnp.int32, (1, nodes), 1)
    span = jnp.full((1, nodes), leaves, jnp.int32)
    start = jnp.zeros((1, nodes), jnp.int32)
    width, tile, first = leaves // 2, leaves // 2, leaves
    while width >= 1:
        span = jnp.where(node >= first, width, span)
        start = jnp.where(node >= first, 2 * tile, start)
        tile, first, width = tile + max(1, width // 2), first + width, width // 2
    shifted = partners[...] - place * span
    side = jnp.where(shifted < 0, 0, jnp.where(shifted < span, 1, 2))
    codes[...] = side * (2 * leaves) + start + shifted - (side - 1) * span


def up_body(
    place, near_list, near_count, partners, points, basis_hbm, values_hbm, across_hbm, moves_hbm,
    up, share, trans_hbm, packed_hbm, lists, live, codes, rows, basis, values, across, moves, trans, packed, sem,
):
    leaves = basis.shape[0]
    columns = values.shape[0]
    nodes = moves.shape[2]
    reads = []
    for i in range(4):
        at = pl.ds(16 * i, 16)
        reads.append(pltpu.make_async_copy(moves_hbm.at[at], moves.at[at], sem.at[i]))
    reads.append(pltpu.make_async_copy(values_hbm, values, sem.at[4]))
    reads.append(pltpu.make_async_copy(basis_hbm, basis, sem.at[5]))
    reads.append(pltpu.make_async_copy(across_hbm, across, sem.at[8]))
    for read in reads:
        read.start()
    plan(place[0], near_list, near_count, partners, lists, live, codes)
    for i in range(4):
        reads[i].wait()

        @pl.loop(16 * i, 16 * i + 16, unroll=8)
        def _(r):
            block = jnp.transpose(moves[r])
            rows[pl.ds(pl.multiple_of(r * PITCH, 8), nodes)] = jnp.concatenate([block, block], axis=1)

    left = low_lanes((64, 128))

    def node(n):
        x = rows[pl.ds(n, 64, stride=PITCH), :]
        hi = x.astype(bf16).astype(f32)
        trans[n] = jnp.where(left, hi, x - hi).astype(bf16)

    whole = nodes // 8 * 8
    pl.loop(0, whole, unroll=8)(node)
    for n in range(whole, nodes):
        node(n)
    trans[nodes] = jnp.zeros(trans.shape[1:], bf16)
    write = pltpu.make_async_copy(trans, trans_hbm, sem.at[6])
    write.start()

    half = low_lanes((columns, 128))

    for read in reads[4:]:
        read.wait()
    block = leaves // 2
    for c in range(3):
        for j in range(leaves):
            packed[j // block, 2 * block + c, j % block : j % block + 1] = points[
                c : c + 1, 128 * j : 128 * j + 128
            ]
    for side in range(2):

        @pl.loop(0, block, unroll=8)
        def _(j, side=side):
            at = pl.ds(pl.multiple_of((side * block + j) * 128, 128), 128)
            packed[side, j] = values[:, at]
            packed[side, block + j] = across[:, at]

    send = pltpu.make_async_copy(packed, packed_hbm, sem.at[7])
    send.start()

    def leaf_up(i):
        v = stack(values[:, pl.ds(pl.multiple_of(i * 128, 128), 128)])
        return both(fold(lax.dot_general(v, stack(basis[i]), NT, preferred_element_type=f32)))

    @pl.loop(0, leaves // 2, unroll=8)
    def _(p):
        up[p] = jnp.where(half, leaf_up(2 * p), leaf_up(2 * p + 1))

    def lift(tile, row):
        t = jnp.concatenate([trans[row], trans[row + 1]], axis=0)
        return both(fold(jnp.dot(stack(tile), t, preferred_element_type=f32)))

    def pair(tile_a, tile_b, row):
        return jnp.where(half, lift(tile_a, row), lift(tile_b, row + 2))

    start, row, width = 0, 0, leaves
    while width > 16:
        after = start + width // 2

        @pl.loop(0, width // 16)
        def _(g, start=start, row=row, after=after):
            made = []
            for p in range(4):
                q = 4 * g + p
                made.append(pair(up[start + 2 * q], up[start + 2 * q + 1], row + 4 * q))
            for p in range(4):
                up[after + 4 * g + p] = made[p]

        start, row, width = after, row + width, width // 2
    tiles = [up[start + p] for p in range(width // 2)]
    while width > 1:
        after = start + width // 2
        if width >= 4:
            tiles = [pair(tiles[2 * p], tiles[2 * p + 1], row + 4 * p) for p in range(width // 4)]
        else:
            tiles = [lift(tiles[0], row)]
        if after < leaves - 1:
            for p, tile in enumerate(tiles):
                up[after + p] = tile
        start, row, width = after, row + width, width // 2
    up[leaves - 1] = tiles[0]
    share[...] = both(fold(jnp.dot(stack(tiles[0])[:, 0:64], trans[row], preferred_element_type=f32)))
    write.wait()
    send.wait()


def up_pass(place, near_list, near_count, partners, points, basis, values, across, moves):
    leaves = basis.shape[0]
    columns = values.shape[0]
    nodes = moves.shape[2]
    return pl.pallas_call(
        up_body,
        out_shape=(
            jax.ShapeDtypeStruct((leaves, columns, 128), f32),
            jax.ShapeDtypeStruct((columns, 128), f32),
            jax.ShapeDtypeStruct((nodes + 1, 64, 128), bf16),
            jax.ShapeDtypeStruct((2, leaves + 3, columns, 128), f32),
            jax.ShapeDtypeStruct((2, SLOTS, leaves), jnp.int32),
            jax.ShapeDtypeStruct((2, leaves), jnp.int32),
            jax.ShapeDtypeStruct(partners.shape, jnp.int32),
        ),
        in_specs=[SM, VM, VM, VM, VM, HBM, HBM, HBM, HBM],
        out_specs=(VM, VM, HBM, HBM, VM, VM, VM),
        scratch_shapes=[
            pltpu.VMEM((64 * PITCH, 128), f32),
            pltpu.VMEM(basis.shape, f32),
            pltpu.VMEM(values.shape, f32),
            pltpu.VMEM(values.shape, f32),
            pltpu.VMEM(moves.shape, f32),
            pltpu.VMEM((nodes + 1, 64, 128), bf16),
            pltpu.VMEM((2, leaves + 3, columns, 128), f32),
            pltpu.SemaphoreType.DMA((9,)),
        ],
        compiler_params=pltpu.CompilerParams(vmem_limit_bytes=VMEM_BYTES),
        cost_estimate=pl.CostEstimate(flops=400_000_000, bytes_accessed=8_000_000, transcendentals=0),
        name="up_pass",
    )(place, near_list, near_count, partners, points, basis, values, across, moves)


CHUNK = 32


def unbatch_body(part, matrices, out, held, rows, made, in_sem, out_sem):
    nodes = matrices.shape[3]
    pieces = 4
    step = matrices.shape[1] // pieces
    reads = []
    for i in range(pieces):
        at = pl.ds(i * step, step)
        reads.append(
            pltpu.make_async_copy(matrices.at[pl.ds(2 * part, 2), at], held.at[:, at], in_sem.at[i])
        )
        reads[-1].start()
    for i in range(pieces):
        reads[i].wait()

        @pl.loop(i * step, (i + 1) * step, unroll=8)
        def _(r):
            x = jnp.concatenate([held[0, r], held[1, r]], axis=0)
            rows[pl.ds(pl.multiple_of(r * PITCH, 8), nodes)] = jnp.transpose(x)

    def one(n):
        hi, lo = split(rows[pl.ds(n, 64, stride=PITCH), :])
        made[n, 0:64] = hi
        made[n, 64:128] = lo

    writes = []
    for c, begin in enumerate(range(0, nodes, CHUNK)):
        size = min(CHUNK, nodes - begin)
        whole = begin + size // 8 * 8
        pl.loop(begin, whole, unroll=8)(one)
        for n in range(whole, begin + size):
            one(n)
        at = pl.ds(begin, size)
        writes.append(pltpu.make_async_copy(made.at[at], out.at[at], out_sem.at[c]))
        writes[-1].start()
    for write in writes:
        write.wait()


def unbatch(matrices, part):
    nodes = matrices.shape[3]
    return pl.pallas_call(
        functools.partial(unbatch_body, part),
        out_shape=jax.ShapeDtypeStruct((nodes, 128, 128), bf16),
        in_specs=[HBM],
        out_specs=HBM,
        scratch_shapes=[
            pltpu.VMEM((2, *matrices.shape[1:]), f32),
            pltpu.VMEM((64 * PITCH, 128), f32),
            pltpu.VMEM((nodes, 128, 128), bf16),
            pltpu.SemaphoreType.DMA((4,)),
            pltpu.SemaphoreType.DMA((-(-nodes // CHUNK),)),
        ],
        compiler_params=pltpu.CompilerParams(vmem_limit_bytes=VMEM_BYTES),
        cost_estimate=pl.CostEstimate(flops=1_000, bytes_accessed=1_000, transcendentals=0),
        name="unbatch",
    )(matrices)


def top_body(place, partners, far_three, far_two, far_one, own, moves, matrices, parent, up, block, sem):
    spot = place[0]
    columns = own.shape[1]
    copies = []
    width, row = 32, 0
    for level in range(4):
        index = row + spot // (2 << level)
        copies.append(pltpu.make_async_copy(matrices.at[index], block.at[level], sem.at[level]))
        copies[-1].start()
        row, width = row + width, width // 2
    half = low_lanes((columns, 128))
    for j, ref in enumerate((far_three, far_two, far_one, own)):
        up[pl.ds(4 * ((spot // 16 + 1 + j) % 4), 4)] = ref[...]
    def lift(tile, r):
        t = jnp.concatenate([moves[r], moves[r + 1]], axis=0)
        hi, lo = split(t)
        x = stack(up[tile])
        z = fold(jnp.dot(x, hi, preferred_element_type=f32)) + jnp.dot(x[:columns], lo, preferred_element_type=f32)
        return jnp.concatenate([z, z], axis=1)
    tile0, row, width = 0, 0, 32
    tiles, rows = [], []
    while width >= 4:
        tiles.append(tile0)
        rows.append(row)
        nxt = tile0 + width // 2
        if width > 4:
            for p in range(width // 4):
                up[nxt + p] = jnp.where(half, lift(tile0 + 2 * p, row + 4 * p), lift(tile0 + 2 * p + 1, row + 4 * p + 2))
        tile0, row, width = nxt, row + width, width // 2
    def push(d, r):
        hi, lo = split(moves[r])
        x = stack(d)
        return fold(lax.dot_general(x, hi, NT, preferred_element_type=f32)) + lax.dot_general(x[:columns], lo, NT, preferred_element_type=f32)
    for copy in copies:
        copy.wait()
    fars = []
    for level in range(4):
        index = rows[level] + spot // (2 << level)
        far = jnp.zeros((columns, 64), f32)
        for k in range(4):
            p = partners[k, index]
            tile = up[tiles[level] + p // 2]
            x = stack(jnp.where(p % 2 == 0, tile, pltpu.roll(tile, 64, 1))[:, 0:64])
            hi, lo = split(block[level, k])
            far = far + fold(lax.dot_general(x, hi, NT, preferred_element_type=f32))
            far = far + lax.dot_general(x[:columns], lo, NT, preferred_element_type=f32)
        fars.append(far)
    down = jnp.zeros((columns, 64), f32)
    down = push(down, row + spot // 32)
    for level in range(3, -1, -1):
        down = push(down, rows[level] + spot // (2 << level)) + fars[level]
    parent[...] = jnp.concatenate([down, down], axis=1)

def top_pass(place, partners, gathered, moves, matrices):
    columns = gathered[0].shape[1]
    return pl.pallas_call(
        top_body,
        out_shape=jax.ShapeDtypeStruct((columns, 128), f32),
        in_specs=[SM, SM] + [VM] * 5 + [HBM],
        out_specs=VM,
        scratch_shapes=[pltpu.VMEM((32, columns, 128), f32), pltpu.VMEM((4, 4, 64, 64), f32), pltpu.SemaphoreType.DMA((4,))],
        compiler_params=pltpu.CompilerParams(vmem_limit_bytes=VMEM_BYTES),
        cost_estimate=pl.CostEstimate(flops=50_000_000, bytes_accessed=2_000_000, transcendentals=0),
        name="top_pass",
    )(place, partners, *gathered, moves, matrices)


def couple_body(codes, low, own, high, first, second, far, gather, tiles, held, sem):
    leaves, columns, _ = own.shape
    nodes = first.shape[0]
    takes = []
    for side, ref in enumerate((low, own, high)):
        takes.append(pltpu.make_async_copy(ref, tiles.at[side], sem.at[3 + side]))
        takes[-1].start()
    reads = []
    for i in range(3):
        begin = 42 * i
        at = pl.ds(begin, nodes - begin if i == 2 else 42)
        for h, x in enumerate((first, second)):
            reads.append(pltpu.make_async_copy(x.at[at], held.at[h, at], sem.at[6 + 2 * i + h]))
            reads[-1].start()
    half = low_lanes((columns, 128))
    left = low_lanes((2 * columns, 128))
    for side in range(3):
        takes[side].wait()

        @pl.loop(0, leaves, unroll=16)
        def _(t, side=side):
            x = tiles[side, t]
            gather[0, side * leaves + t] = stack(x)
            gather[1, side * leaves + t] = stack(pltpu.roll(x, 64, 1))

    def pick(n, k, side):
        code = codes[k, n]
        return gather[(code & 1) ^ side, code >> 1]

    def one(n):
        x = jnp.concatenate(
            [
                jnp.where(left, pick(n, 0, 0), pick(n, 1, 1)),
                jnp.where(left, pick(n, 2, 0), pick(n, 3, 1)),
            ],
            axis=1,
        )
        m = jnp.concatenate([held[0, n], held[1, n]], axis=1)
        return both(fold(lax.dot_general(x, m, NT, preferred_element_type=f32)))

    for i in range(3):
        reads[2 * i].wait()
        reads[2 * i + 1].wait()

        @pl.loop(21 * i, 21 * i + 21, unroll=7)
        def _(t):
            far[t] = jnp.where(half, one(2 * t), one(2 * t + 1))

    far[leaves - 1] = one(nodes - 1)


def couple_pass(codes, low, own, high, first, second):
    leaves, columns, _ = own.shape
    return pl.pallas_call(
        couple_body,
        out_shape=jax.ShapeDtypeStruct((leaves, columns, 128), f32),
        in_specs=[SM] + [HBM] * 5,
        out_specs=VM,
        scratch_shapes=[
            pltpu.VMEM((2, 3 * leaves, 2 * columns, 128), bf16),
            pltpu.VMEM((3, leaves, columns, 128), f32),
            pltpu.VMEM((2, *first.shape), bf16),
            pltpu.SemaphoreType.DMA((12,)),
        ],
        compiler_params=pltpu.CompilerParams(vmem_limit_bytes=VMEM_BYTES),
        cost_estimate=pl.CostEstimate(flops=400_000_000, bytes_accessed=12_000_000, transcendentals=0),
        name="couple_pass",
    )(codes, low, own, high, first, second)


def down_body(core, parent, far_hbm, trans_hbm, basis_hbm, mine, given, out, far, trans, basis, ones, twos, sem):
    leaves = basis.shape[0]
    columns = out.shape[0]
    reads = []
    for i, (source, dest) in enumerate(((far_hbm, far), (trans_hbm, trans), (basis_hbm, basis))):
        reads.append(pltpu.make_async_copy(source, dest, sem.at[i]))
        reads[-1].start()
    half = low_lanes((columns, 128))

    def push(d, tile):
        t = jnp.concatenate([trans[2 * tile], trans[2 * tile + 1]], axis=0)
        return fold(lax.dot_general(stack(d), t, NT, preferred_element_type=f32)) + far[tile]

    def spread(tile):
        turned = pltpu.roll(tile, 64, 1)
        return jnp.where(half, tile, turned), jnp.where(half, turned, tile)

    last = leaves - 1
    above = stack(parent[...])
    reads[0].wait()
    reads[1].wait()
    t = trans[2 * last]
    t = jnp.concatenate([t, t], axis=0)
    sources = [fold(lax.dot_general(above, t, NT, preferred_element_type=f32)) + far[last]]
    start, width = last, 1
    while width < 16:
        start = start - width
        made = [push(d, start + i) for i, d in enumerate(sources)]
        sources = [d for tile in made for d in spread(tile)]
        width = 2 * width
    start = start - width
    for i, d in enumerate(sources):
        ones[i] = push(d, start + i)

    @pl.loop(0, width, unroll=8)
    def _(i):
        for u, d in enumerate(spread(ones[i])):
            twos[2 * i + u] = push(d, 2 * i + u)

    reads[2].wait()

    @pl.loop(0, leaves // 2, unroll=4)
    def _(i):
        for u, d in enumerate(spread(twos[i])):
            leaf = 2 * i + u
            out[:, pl.ds(pl.multiple_of(leaf * 128, 128), 128)] = fold(
                jnp.dot(stack(d), stack(basis[leaf]), preferred_element_type=f32)
            )

    size = mine.shape[1]
    out[:, pl.ds(pl.multiple_of(core[0] * size, size), size)] += mine[...]
    out[:, pl.ds(pl.multiple_of((1 - core[0]) * size, size), size)] += given[...]


def down_pass(core, parent, far, trans, basis, mine, given):
    leaves = basis.shape[0]
    columns = parent.shape[0]
    return pl.pallas_call(
        down_body,
        out_shape=jax.ShapeDtypeStruct((columns, leaves * 128), f32),
        in_specs=[SM, VM, HBM, HBM, HBM, VM, VM],
        out_specs=VM,
        scratch_shapes=[
            pltpu.VMEM(far.shape, f32),
            pltpu.VMEM(trans.shape, bf16),
            pltpu.VMEM(basis.shape, f32),
            pltpu.VMEM((leaves // 4, columns, 128), f32),
            pltpu.VMEM((leaves // 2, columns, 128), f32),
            pltpu.SemaphoreType.DMA((3,)),
        ],
        compiler_params=pltpu.CompilerParams(vmem_limit_bytes=VMEM_BYTES),
        cost_estimate=pl.CostEstimate(flops=200_000_000, bytes_accessed=7_000_000, transcendentals=0),
        name="down_pass",
    )(core, parent, far, trans, basis, mine, given)


near_weight = 0.1
smoothing = 0.0025
PAIR = 2

def near_body(unroll, chunks, core, lists, live, targets, *refs):
    origins, refs = refs[:chunks], refs[chunks:]
    begin = None
    if chunks == 2:
        begin, refs = refs[0:2], refs[2:]
    mine, other, columns_of, total, weights, places, sem, *sources = refs
    leaves = mine.shape[1] // 128
    width = 2 * leaves
    core = core[0]
    side = chunks - 1
    mark = core * leaves
    reads = []
    for i, (origin, source) in enumerate(zip(origins, sources)):
        reads.append(pltpu.make_async_copy(origin, source, sem.at[i]))
        reads[-1].start()
    weights[chunks * width] = jnp.zeros(weights.shape[1:], bf16)
    places[chunks * width] = jnp.zeros(places.shape[1:], f32)
    blank = jnp.zeros((5, 128), f32)

    @pl.loop(0, leaves // 16)
    def _(g):
        rows = []
        for u in range(16):
            at = pl.ds(pl.multiple_of((core * leaves + 16 * g + u) * 128, 128), 128)
            rows += [targets[:, at], blank]
        t = jnp.transpose(jnp.concatenate(rows, axis=0))
        for u in range(16):
            for c in range(3):
                columns_of[16 * g + u, c] = jnp.broadcast_to(t[:, 8 * u + c : 8 * u + c + 1], (128, 128))
            total[16 * g + u] = jnp.zeros((128, 128), f32)

    for read in reads:
        read.wait()

    def load(block, base, turn):
        @pl.loop(0, leaves // 8)
        def _(g):
            for u in range(8):
                j = 8 * g + u
                x = [block[j], block[leaves + j]]
                weights[base + j] = stack(near_weight * jnp.concatenate(x[::-1] if turn else x, axis=0))
                for c in range(3):
                    places[base + j, c : c + 1] = block[2 * leaves + c, pl.ds(j, 1)]

    base = width * core if chunks == 2 else 0
    load(sources[0].at[0], base, False)
    load(sources[0].at[1], base + leaves, False)
    if chunks == 2:
        load(sources[1], width - leaves * core, True)
    items = lax.fori_loop(
        0, leaves, lambda i, s: s + jnp.maximum((live[side, mark + i] + PAIR - 1) // PAIR, 1), jnp.int32(0)
    )

    def block(leaf, slot):
        kernels, parts = [], []
        for u in range(PAIR):
            j = lists[side, slot + u, mark + leaf]
            s = places[j]
            d = columns_of[leaf, 0] - s[0:1]
            squared = d * d + smoothing
            d = columns_of[leaf, 1] - s[1:2]
            squared = squared + d * d
            d = columns_of[leaf, 2] - s[2:3]
            squared = squared + d * d
            kernels += split(lax.rsqrt(squared))
            x = weights[j]
            parts += [x, x]
        return lax.dot_general(
            jnp.concatenate(kernels, axis=1),
            jnp.concatenate(parts, axis=1),
            NT,
            preferred_element_type=f32,
        )

    def step(b, carry):
        leaf, slot = carry
        made = []
        for u in range(unroll):
            place = jnp.where(b * unroll + u < items, leaf, leaves)
            made.append((place, block(leaf, slot)))
            done = slot + PAIR >= live[side, mark + leaf]
            leaf = jnp.where(done, jnp.minimum(leaf + 1, leaves - 1), leaf)
            slot = jnp.where(done, 0, slot + PAIR)
        for place, x in made:
            total[place] += x
        return leaf, slot

    lax.fori_loop(0, (items + unroll - 1) // unroll, step, (jnp.int32(0), jnp.int32(0)))

    @pl.loop(0, leaves, unroll=8)
    def _(leaf):
        at = pl.ds(pl.multiple_of(leaf * 128, 128), 128)
        x = jnp.transpose(both(total[leaf]))
        if begin is None:
            mine[:, at] = x[0:32]
            other[:, at] = x[32:64]
        else:
            mine[:, at] = begin[0][:, at] + x[0:32]
            other[:, at] = begin[1][:, at] + x[32:64]


def near_pass(unroll, core, lists, live, targets, sources, begin=()):
    leaves = lists.shape[2] // 2
    chunks = len(sources)
    held = chunks * 2 * leaves + 1
    side = jax.ShapeDtypeStruct((32, leaves * 128), f32)
    arrays = (targets, *sources, *begin)
    return pl.pallas_call(
        functools.partial(near_body, unroll, chunks),
        out_shape=(side, side),
        in_specs=[SM, SM, SM, VM] + [HBM] * len(sources) + [VM] * len(begin),
        out_specs=(VM, VM),
        scratch_shapes=[
            pltpu.VMEM((leaves, 3, 128, 128), f32),
            pltpu.VMEM((leaves + 1, 128, 128), f32),
            pltpu.VMEM((held, 128, 128), bf16),
            pltpu.VMEM((held, 8, 128), f32),
            pltpu.SemaphoreType.DMA((len(sources),)),
            *[pltpu.VMEM(x.shape, f32) for x in sources],
        ],
        compiler_params=pltpu.CompilerParams(vmem_limit_bytes=VMEM_BYTES),
        cost_estimate=pl.CostEstimate(flops=1_000, bytes_accessed=1_000, transcendentals=0),
        name="near_pass",
    )(core, lists, live, *arrays)


def local(
    points,
    values,
    near_list,
    near_count,
    basis,
    transfer,
    coupling,
    partners,
    transfer_top,
    coupling_top,
    partners_top,
):
    leaves = basis.shape[0]
    position = lax.axis_index("leaf")
    core = lax.axis_index("rhs")
    count = lax.axis_size("leaf")
    forward = [(i, i + 1) for i in range(count - 1)]
    backward = [(target, source) for source, target in forward]
    swap = [(0, 1), (1, 0)]
    across = lax.ppermute(values, "rhs", swap)

    def ring(x, stride):
        spot = (position // stride) % 4
        turned = []
        for shift in range(3, 0, -1):
            to = [(i, i + stride * ((i // stride + shift) % 4 - i // stride % 4)) for i in range(count)]
            turned.append(lax.ppermute(x, "leaf", to))
        return turned, spot

    def in_order(turned, x, spot):
        blocks = [*turned, x]
        ordered = []
        for k in range(4):
            block = blocks[3]
            for j in range(3):
                block = jnp.where(spot == (k - j - 1) % 4, blocks[j], block)
            ordered.append(block)
        return jnp.concatenate(ordered, axis=0)

    after = lax.optimization_barrier
    core = core[None].astype(jnp.int32)
    place = position[None].astype(jnp.int32)
    coupling = coupling.transpose(1, 2, 3, 0)
    first = unbatch(coupling, 0)
    across, first, coupling = after((across, first, coupling))
    up, share, trans, packed, lists, live, codes = up_pass(
        place,
        near_list.T,
        near_count[None],
        partners.T,
        points,
        basis,
        values,
        across,
        transfer.transpose(1, 2, 0),
    )
    turned, spot = ring(share[None], 1)
    turned, share, packed = after((turned, share, packed))
    outward = [(2 * i, 2 * i + 2) for i in range(count - 1)]
    outward += [(2 * i + 3, 2 * i + 1) for i in range(count - 1)]
    beside = lax.ppermute(packed, ("leaf", "rhs"), outward)
    level = in_order(turned, share[None], spot)
    level = jnp.where(jnp.arange(128) < 64, level[0] + level[1], level[2] + level[3])[None]
    turned, spot = ring(level, 4)
    begin = near_pass(12, core, lists, live, points, (packed,))
    coupling, turned, begin = after((coupling, turned, begin))
    level = in_order(turned, level, spot)
    second = unbatch(coupling, 1)
    beside, up, level, lists, second = after((beside, up, level, lists, second))
    passed = lax.dynamic_index_in_dim(beside, 1 - core[0], 0, keepdims=False)
    passed = lax.ppermute(passed, "rhs", swap)
    turned, spot = ring(level, 16)
    up_low = lax.ppermute(up, "leaf", forward)
    up_high = lax.ppermute(up, "leaf", backward)
    mine, other = near_pass(12, core, lists, live, points, (beside, passed), begin)
    turned, mine, other = after((turned, mine, other))
    given = lax.ppermute(other, "rhs", swap)
    parent = top_pass(place, partners_top.T, (*turned, level), transfer_top, coupling_top)
    parent, up_low, up_high = after((parent, up_low, up_high))
    far = couple_pass(codes, up_low, up, up_high, first, second)
    return down_pass(core, parent, far, trans, basis, mine, given)


def solution(mesh):
    placed = (
        P(None, "leaf"),
        P("rhs", "leaf"),
        P("leaf", None),
        P("leaf"),
        P("leaf", None, None),
        P("leaf", None, None),
        P("leaf", None, None, None),
        P("leaf", None),
        P(),
        P(),
        P(),
    )
    return jax.shard_map(
        local, mesh=mesh, in_specs=placed, out_specs=P("rhs", "leaf"), check_vma=False
    )
```

```python
import jax, jax.numpy as jnp, functools
from jax import lax
from jax.sharding import PartitionSpec as P
from jax.experimental import pallas as pl
from jax.experimental.pallas import tpu as pltpu
NT = (((1,), (1,)), ((), ()))
SM = pl.BlockSpec(memory_space=pltpu.SMEM)
VM = pl.BlockSpec(memory_space=pltpu.VMEM)
HBM = pl.BlockSpec(memory_space=pltpu.HBM)
PITCH = 136
VMEM_BYTES = 62 << 20
SLOTS = 28
f32 = jnp.float32
bf16 = jnp.bfloat16

def split(x):
    hi = x.astype(bf16)
    return hi, (x - hi.astype(f32)).astype(bf16)

def stack(x):
    hi, lo = split(x)
    return jnp.concatenate([hi, lo], axis=0)

def fold(x):
    half = x.shape[0] // 2
    return x[:half] + x[half:]

def both(x):
    return x + pltpu.roll(x, 64, 1)

def low_lanes(shape):
    return lax.broadcasted_iota(jnp.int32, shape, 1) < 64

def plan(place, near_list, near_count, partners, lists, live, codes):
    slots, leaves = near_list.shape
    local = near_list[...] - place * leaves
    count = near_count[...]
    inside = (local >= 0) & (local < leaves)
    row = lax.broadcasted_iota(jnp.int32, (SLOTS, leaves), 0)
    for side in range(2):
        rank = jnp.zeros((1, leaves), jnp.int32)
        found = jnp.full((SLOTS, leaves), (1 + side) * leaves, jnp.int32)
        for s in range(slots):
            here = inside[s : s + 1] if side == 0 else jnp.logical_not(inside[s : s + 1])
            picked = here & (s < count)
            ids = local[s : s + 1]
            if side == 1:
                ids = jnp.where(ids < 0, ids + leaves, ids)
            found = jnp.where((row == rank) & picked, ids, found)
            rank = rank + picked.astype(jnp.int32)
        lists[side] = found
        live[side : side + 1] = rank
    nodes = partners.shape[1]
    node = lax.broadcasted_iota(jnp.int32, (1, nodes), 1)
    span = jnp.full((1, nodes), leaves, jnp.int32)
    start = jnp.zeros((1, nodes), jnp.int32)
    width, tile, first = leaves // 2, leaves // 2, leaves
    while width >= 1:
        span = jnp.where(node >= first, width, span)
        start = jnp.where(node >= first, 2 * tile, start)
        tile, first, width = tile + max(1, width // 2), first + width, width // 2
    shifted = partners[...] - place * span
    side = jnp.where(shifted < 0, 0, jnp.where(shifted < span, 1, 2))
    codes[...] = side * (2 * leaves) + start + shifted - (side - 1) * span


def up_body(
    place, near_list, near_count, partners, basis_hbm, values_hbm, moves_hbm,
    up, share, trans_hbm, lists, live, codes, rows, basis, values, moves, trans, sem,
):
    leaves = basis.shape[0]
    columns = values.shape[0]
    nodes = moves.shape[2]
    reads = []
    for i in range(4):
        at = pl.ds(16 * i, 16)
        reads.append(pltpu.make_async_copy(moves_hbm.at[at], moves.at[at], sem.at[i]))
    reads.append(pltpu.make_async_copy(values_hbm, values, sem.at[4]))
    reads.append(pltpu.make_async_copy(basis_hbm, basis, sem.at[5]))
    for read in reads:
        read.start()
    plan(place[0], near_list, near_count, partners, lists, live, codes)
    for i in range(4):
        reads[i].wait()

        @pl.loop(16 * i, 16 * i + 16, unroll=8)
        def _(r):
            block = jnp.transpose(moves[r])
            rows[pl.ds(pl.multiple_of(r * PITCH, 8), nodes)] = jnp.concatenate([block, block], axis=1)

    left = low_lanes((64, 128))

    def node(n):
        x = rows[pl.ds(n, 64, stride=PITCH), :]
        hi = x.astype(bf16).astype(f32)
        trans[n] = jnp.where(left, hi, x - hi).astype(bf16)

    whole = nodes // 8 * 8
    pl.loop(0, whole, unroll=8)(node)
    for n in range(whole, nodes):
        node(n)
    trans[nodes] = jnp.zeros(trans.shape[1:], bf16)
    write = pltpu.make_async_copy(trans, trans_hbm, sem.at[6])
    write.start()

    half = low_lanes((columns, 128))

    for read in reads[4:]:
        read.wait()
    def leaf_up(i):
        v = stack(values[:, pl.ds(pl.multiple_of(i * 128, 128), 128)])
        return both(fold(lax.dot_general(v, stack(basis[i]), NT, preferred_element_type=f32)))

    @pl.loop(0, leaves // 2, unroll=8)
    def _(p):
        up[p] = jnp.where(half, leaf_up(2 * p), leaf_up(2 * p + 1))

    def lift(tile, row):
        t = jnp.concatenate([trans[row], trans[row + 1]], axis=0)
        return both(fold(jnp.dot(stack(tile), t, preferred_element_type=f32)))

    def pair(tile_a, tile_b, row):
        return jnp.where(half, lift(tile_a, row), lift(tile_b, row + 2))

    start, row, width = 0, 0, leaves
    while width > 16:
        after = start + width // 2

        @pl.loop(0, width // 16)
        def _(g, start=start, row=row, after=after):
            made = []
            for p in range(4):
                q = 4 * g + p
                made.append(pair(up[start + 2 * q], up[start + 2 * q + 1], row + 4 * q))
            for p in range(4):
                up[after + 4 * g + p] = made[p]

        start, row, width = after, row + width, width // 2
    tiles = [up[start + p] for p in range(width // 2)]
    while width > 1:
        after = start + width // 2
        if width >= 4:
            tiles = [pair(tiles[2 * p], tiles[2 * p + 1], row + 4 * p) for p in range(width // 4)]
        else:
            tiles = [lift(tiles[0], row)]
        if after < leaves - 1:
            for p, tile in enumerate(tiles):
                up[after + p] = tile
        start, row, width = after, row + width, width // 2
    up[leaves - 1] = tiles[0]
    share[...] = both(fold(jnp.dot(stack(tiles[0])[:, 0:64], trans[row], preferred_element_type=f32)))
    write.wait()


def up_pass(place, near_list, near_count, partners, basis, values, moves):
    leaves = basis.shape[0]
    columns = values.shape[0]
    nodes = moves.shape[2]
    return pl.pallas_call(
        up_body,
        out_shape=(
            jax.ShapeDtypeStruct((leaves, columns, 128), f32),
            jax.ShapeDtypeStruct((columns, 128), f32),
            jax.ShapeDtypeStruct((nodes + 1, 64, 128), bf16),
            jax.ShapeDtypeStruct((2, SLOTS, leaves), jnp.int32),
            jax.ShapeDtypeStruct((2, leaves), jnp.int32),
            jax.ShapeDtypeStruct(partners.shape, jnp.int32),
        ),
        in_specs=[SM, VM, VM, VM, HBM, HBM, HBM],
        out_specs=(VM, VM, HBM, VM, VM, VM),
        scratch_shapes=[
            pltpu.VMEM((64 * PITCH, 128), f32),
            pltpu.VMEM(basis.shape, f32),
            pltpu.VMEM(values.shape, f32),
            pltpu.VMEM(moves.shape, f32),
            pltpu.VMEM((nodes + 1, 64, 128), bf16),
            pltpu.SemaphoreType.DMA((7,)),
        ],
        compiler_params=pltpu.CompilerParams(vmem_limit_bytes=VMEM_BYTES),
        cost_estimate=pl.CostEstimate(flops=400_000_000, bytes_accessed=8_000_000, transcendentals=0),
        name="up_pass",
    )(place, near_list, near_count, partners, basis, values, moves)


CHUNK = 32


def unbatch_body(part, matrices, out, held, rows, made, in_sem, out_sem, between=None):
    nodes = matrices.shape[3]
    pieces = 4
    step = matrices.shape[1] // pieces
    reads = []
    for i in range(pieces):
        at = pl.ds(i * step, step)
        reads.append(
            pltpu.make_async_copy(matrices.at[pl.ds(2 * part, 2), at], held.at[:, at], in_sem.at[i])
        )
        reads[-1].start()
    if between is not None:
        between()
    for i in range(pieces):
        reads[i].wait()

        @pl.loop(i * step, (i + 1) * step, unroll=8)
        def _(r):
            x = jnp.concatenate([held[0, r], held[1, r]], axis=0)
            rows[pl.ds(pl.multiple_of(r * PITCH, 8), nodes)] = jnp.transpose(x)

    def one(n):
        hi, lo = split(rows[pl.ds(n, 64, stride=PITCH), :])
        made[n, 0:64] = hi
        made[n, 64:128] = lo

    writes = []
    for c, begin in enumerate(range(0, nodes, CHUNK)):
        size = min(CHUNK, nodes - begin)
        whole = begin + size // 8 * 8
        pl.loop(begin, whole, unroll=8)(one)
        for n in range(whole, begin + size):
            one(n)
        at = pl.ds(begin, size)
        writes.append(pltpu.make_async_copy(made.at[at], out.at[at], out_sem.at[c]))
        writes[-1].start()
    for write in writes:
        write.wait()


def unbatch_pack_body(
    part, matrices, points, values_hbm, across_hbm, out, packed_hbm,
    held, rows, made, in_sem, out_sem, values, across, packed, sem,
):
    takes = [
        pltpu.make_async_copy(values_hbm, values, sem.at[0]),
        pltpu.make_async_copy(across_hbm, across, sem.at[1]),
    ]
    for take in takes:
        take.start()
    send = pltpu.make_async_copy(packed, packed_hbm, sem.at[2])

    def between():
        for take in takes:
            take.wait()
        arrange(points, values, across, packed)
        send.start()

    unbatch_body(part, matrices, out, held, rows, made, in_sem, out_sem, between)
    send.wait()


def arrange(points, values, across, packed):
    leaves = values.shape[1] // 128
    block = leaves // 2
    for c in range(3):
        for j in range(leaves):
            packed[j // block, 2 * block + c, j % block : j % block + 1] = points[
                c : c + 1, 128 * j : 128 * j + 128
            ]
    for side in range(2):

        @pl.loop(0, block, unroll=8)
        def _(j, side=side):
            at = pl.ds(pl.multiple_of((side * block + j) * 128, 128), 128)
            packed[side, j] = values[:, at]
            packed[side, block + j] = across[:, at]


def unbatch_scratch(matrices):
    nodes = matrices.shape[3]
    return [
        pltpu.VMEM((2, *matrices.shape[1:]), f32),
        pltpu.VMEM((64 * PITCH, 128), f32),
        pltpu.VMEM((nodes, 128, 128), bf16),
        pltpu.SemaphoreType.DMA((4,)),
        pltpu.SemaphoreType.DMA((-(-nodes // CHUNK),)),
    ]


def unbatch_pack(matrices, part, points, values, across):
    columns, width = values.shape
    packed = (2, width // 128 + 3, columns, 128)
    return pl.pallas_call(
        functools.partial(unbatch_pack_body, part),
        out_shape=(
            jax.ShapeDtypeStruct((matrices.shape[3], 128, 128), bf16),
            jax.ShapeDtypeStruct(packed, f32),
        ),
        in_specs=[HBM, VM, HBM, HBM],
        out_specs=(HBM, HBM),
        scratch_shapes=[
            *unbatch_scratch(matrices),
            pltpu.VMEM(values.shape, f32),
            pltpu.VMEM(values.shape, f32),
            pltpu.VMEM(packed, f32),
            pltpu.SemaphoreType.DMA((3,)),
        ],
        compiler_params=pltpu.CompilerParams(vmem_limit_bytes=VMEM_BYTES),
        cost_estimate=pl.CostEstimate(flops=1_000, bytes_accessed=1_000, transcendentals=0),
        name="unbatch_pack",
    )(matrices, points, values, across)


def unbatch(matrices, part):
    nodes = matrices.shape[3]
    return pl.pallas_call(
        functools.partial(unbatch_body, part),
        out_shape=jax.ShapeDtypeStruct((nodes, 128, 128), bf16),
        in_specs=[HBM],
        out_specs=HBM,
        scratch_shapes=unbatch_scratch(matrices),
        compiler_params=pltpu.CompilerParams(vmem_limit_bytes=VMEM_BYTES),
        cost_estimate=pl.CostEstimate(flops=1_000, bytes_accessed=1_000, transcendentals=0),
        name="unbatch",
    )(matrices)


def top_chain(place, partners, gathered, moves, up, block, arrived):
    spot = place[0]
    columns = gathered[0].shape[1]
    half = low_lanes((columns, 128))
    for j, ref in enumerate(gathered):
        up[pl.ds(4 * ((spot // 16 + 1 + j) % 4), 4)] = ref[...]
    def lift(tile, r):
        t = jnp.concatenate([moves[r], moves[r + 1]], axis=0)
        hi, lo = split(t)
        x = stack(up[tile])
        z = fold(jnp.dot(x, hi, preferred_element_type=f32)) + jnp.dot(x[:columns], lo, preferred_element_type=f32)
        return jnp.concatenate([z, z], axis=1)
    tile0, row, width = 0, 0, 32
    tiles, rows = [], []
    while width >= 4:
        tiles.append(tile0)
        rows.append(row)
        nxt = tile0 + width // 2
        if width > 4:
            for p in range(width // 4):
                up[nxt + p] = jnp.where(half, lift(tile0 + 2 * p, row + 4 * p), lift(tile0 + 2 * p + 1, row + 4 * p + 2))
        tile0, row, width = nxt, row + width, width // 2
    def push(d, r):
        hi, lo = split(moves[r])
        x = stack(d)
        return fold(lax.dot_general(x, hi, NT, preferred_element_type=f32)) + lax.dot_general(x[:columns], lo, NT, preferred_element_type=f32)
    arrived()
    fars = []
    for level in range(4):
        index = rows[level] + spot // (2 << level)
        far = jnp.zeros((columns, 64), f32)
        for k in range(4):
            p = partners[k, index]
            tile = up[tiles[level] + p // 2]
            x = stack(jnp.where(p % 2 == 0, tile, pltpu.roll(tile, 64, 1))[:, 0:64])
            hi, lo = split(block[level, k])
            far = far + fold(lax.dot_general(x, hi, NT, preferred_element_type=f32))
            far = far + lax.dot_general(x[:columns], lo, NT, preferred_element_type=f32)
        fars.append(far)
    down = jnp.zeros((columns, 64), f32)
    down = push(down, row + spot // 32)
    for level in range(3, -1, -1):
        down = push(down, rows[level] + spot // (2 << level)) + fars[level]
    return jnp.concatenate([down, down], axis=1)


def couple(codes, far, gather, tiles, held, takes, reads):
    _, leaves, columns, _ = tiles.shape
    nodes = held.shape[1]
    half = low_lanes((columns, 128))
    left = low_lanes((2 * columns, 128))
    for side in range(3):
        takes[side].wait()

        @pl.loop(0, leaves, unroll=16)
        def _(t, side=side):
            x = tiles[side, t]
            gather[0, side * leaves + t] = stack(x)
            gather[1, side * leaves + t] = stack(pltpu.roll(x, 64, 1))

    def pick(n, k, side):
        code = codes[k, n]
        return gather[(code & 1) ^ side, code >> 1]

    def one(n):
        x = jnp.concatenate(
            [
                jnp.where(left, pick(n, 0, 0), pick(n, 1, 1)),
                jnp.where(left, pick(n, 2, 0), pick(n, 3, 1)),
            ],
            axis=1,
        )
        m = jnp.concatenate([held[0, n], held[1, n]], axis=1)
        return both(fold(lax.dot_general(x, m, NT, preferred_element_type=f32)))

    for i in range(3):
        reads[2 * i].wait()
        reads[2 * i + 1].wait()

        @pl.loop(21 * i, 21 * i + 21, unroll=7)
        def _(t):
            far[t] = jnp.where(half, one(2 * t), one(2 * t + 1))

    far[leaves - 1] = one(nodes - 1)


def descend(core, parent, far, trans, basis, mine, given, out, ones, twos, moved, based):
    leaves = basis.shape[0]
    columns = out.shape[0]
    half = low_lanes((columns, 128))

    def push(d, tile):
        t = jnp.concatenate([trans[2 * tile], trans[2 * tile + 1]], axis=0)
        return fold(lax.dot_general(stack(d), t, NT, preferred_element_type=f32)) + far[tile]

    def spread(tile):
        turned = pltpu.roll(tile, 64, 1)
        return jnp.where(half, tile, turned), jnp.where(half, turned, tile)

    last = leaves - 1
    above = stack(parent)
    moved.wait()
    t = trans[2 * last]
    t = jnp.concatenate([t, t], axis=0)
    sources = [fold(lax.dot_general(above, t, NT, preferred_element_type=f32)) + far[last]]
    start, width = last, 1
    while width < 16:
        start = start - width
        made = [push(d, start + i) for i, d in enumerate(sources)]
        sources = [d for tile in made for d in spread(tile)]
        width = 2 * width
    start = start - width
    for i, d in enumerate(sources):
        ones[i] = push(d, start + i)

    @pl.loop(0, width, unroll=8)
    def _(i):
        for u, d in enumerate(spread(ones[i])):
            twos[2 * i + u] = push(d, 2 * i + u)

    based.wait()

    @pl.loop(0, leaves // 2, unroll=4)
    def _(i):
        for u, d in enumerate(spread(twos[i])):
            leaf = 2 * i + u
            out[:, pl.ds(pl.multiple_of(leaf * 128, 128), 128)] = fold(
                jnp.dot(stack(d), stack(basis[leaf]), preferred_element_type=f32)
            )

    size = mine.shape[1]
    out[:, pl.ds(pl.multiple_of(core[0] * size, size), size)] += mine[...]
    out[:, pl.ds(pl.multiple_of((1 - core[0]) * size, size), size)] += given[...]


def finish_body(
    core, place, codes, partners, three, two, one, level, mine, given,
    moves_hbm, matrices, low, own, high, first, second, trans_hbm, basis_hbm, out,
    moves, block, up, tiles, held, trans, basis, gather, far, ones, twos, sem,
):
    spot = place[0]
    queue = []

    def bring(source, dest):
        copy = pltpu.make_async_copy(source, dest, sem.at[len(queue)])
        copy.start()
        queue.append(copy)
        return copy

    lifted = bring(moves_hbm, moves)
    blocks = []
    width, row = 32, 0
    for i in range(4):
        blocks.append(bring(matrices.at[row + spot // (2 << i)], block.at[i]))
        row, width = row + width, width // 2
    takes = [bring(ref, tiles.at[side]) for side, ref in enumerate((low, own, high))]
    nodes = first.shape[0]
    reads = []
    for i in range(3):
        at = pl.ds(42 * i, nodes - 84 if i == 2 else 42)
        for h, x in enumerate((first, second)):
            reads.append(bring(x.at[at], held.at[h, at]))
    moved = bring(trans_hbm, trans)
    based = bring(basis_hbm, basis)

    def arrived():
        for copy in blocks:
            copy.wait()

    lifted.wait()
    parent = top_chain(place, partners, (three, two, one, level), moves, up, block, arrived)
    couple(codes, far, gather, tiles, held, takes, reads)
    descend(core, parent, far, trans, basis, mine, given, out, ones, twos, moved, based)


def finish(core, place, codes, partners, gathered, mine, given, moves, matrices, low, own, high, first, second, trans, basis):
    leaves, columns, _ = own.shape
    return pl.pallas_call(
        finish_body,
        out_shape=jax.ShapeDtypeStruct((columns, leaves * 128), f32),
        in_specs=[SM] * 4 + [VM] * 6 + [HBM] * 9,
        out_specs=VM,
        scratch_shapes=[
            pltpu.VMEM(moves.shape, f32),
            pltpu.VMEM((4, *matrices.shape[1:]), f32),
            pltpu.VMEM((32, columns, 128), f32),
            pltpu.VMEM((3, leaves, columns, 128), f32),
            pltpu.VMEM((2, *first.shape), bf16),
            pltpu.VMEM(trans.shape, bf16),
            pltpu.VMEM(basis.shape, f32),
            pltpu.VMEM((2, 3 * leaves, 2 * columns, 128), bf16),
            pltpu.VMEM((leaves, columns, 128), f32),
            pltpu.VMEM((leaves // 4, columns, 128), f32),
            pltpu.VMEM((leaves // 2, columns, 128), f32),
            pltpu.SemaphoreType.DMA((16,)),
        ],
        compiler_params=pltpu.CompilerParams(vmem_limit_bytes=VMEM_BYTES),
        cost_estimate=pl.CostEstimate(flops=1_000_000_000, bytes_accessed=20_000_000, transcendentals=0),
        name="finish",
    )(core, place, codes, partners, *gathered, mine, given, moves, matrices, low, own, high, first, second, trans, basis)


near_weight = 0.1
smoothing = 0.0025
PAIR = 2

def near_body(unroll, chunks, core, lists, live, targets, *refs):
    origins, refs = refs[:chunks], refs[chunks:]
    begin = None
    if chunks == 2:
        begin, refs = refs[0:2], refs[2:]
    mine, other, columns_of, total, weights, places, sem, *sources = refs
    leaves = mine.shape[1] // 128
    width = 2 * leaves
    core = core[0]
    side = chunks - 1
    mark = core * leaves
    reads = []
    for i, (origin, source) in enumerate(zip(origins, sources)):
        reads.append(pltpu.make_async_copy(origin, source, sem.at[i]))
        reads[-1].start()
    weights[chunks * width] = jnp.zeros(weights.shape[1:], bf16)
    places[chunks * width] = jnp.zeros(places.shape[1:], f32)
    blank = jnp.zeros((5, 128), f32)

    @pl.loop(0, leaves // 16)
    def _(g):
        rows = []
        for u in range(16):
            at = pl.ds(pl.multiple_of((core * leaves + 16 * g + u) * 128, 128), 128)
            rows += [targets[:, at], blank]
        t = jnp.transpose(jnp.concatenate(rows, axis=0))
        for u in range(16):
            for c in range(3):
                columns_of[16 * g + u, c] = jnp.broadcast_to(t[:, 8 * u + c : 8 * u + c + 1], (128, 128))
            total[16 * g + u] = jnp.zeros((128, 128), f32)

    for read in reads:
        read.wait()

    def load(block, base, turn):
        @pl.loop(0, leaves // 8)
        def _(g):
            for u in range(8):
                j = 8 * g + u
                x = [block[j], block[leaves + j]]
                weights[base + j] = stack(near_weight * jnp.concatenate(x[::-1] if turn else x, axis=0))
                for c in range(3):
                    places[base + j, c : c + 1] = block[2 * leaves + c, pl.ds(j, 1)]

    base = width * core if chunks == 2 else 0
    load(sources[0].at[0], base, False)
    load(sources[0].at[1], base + leaves, False)
    if chunks == 2:
        load(sources[1], width - leaves * core, True)
    items = lax.fori_loop(
        0, leaves, lambda i, s: s + jnp.maximum((live[side, mark + i] + PAIR - 1) // PAIR, 1), jnp.int32(0)
    )

    def block(leaf, slot):
        kernels, parts = [], []
        for u in range(PAIR):
            j = lists[side, slot + u, mark + leaf]
            s = places[j]
            d = columns_of[leaf, 0] - s[0:1]
            squared = d * d + smoothing
            d = columns_of[leaf, 1] - s[1:2]
            squared = squared + d * d
            d = columns_of[leaf, 2] - s[2:3]
            squared = squared + d * d
            kernels += split(lax.rsqrt(squared))
            x = weights[j]
            parts += [x, x]
        return lax.dot_general(
            jnp.concatenate(kernels, axis=1),
            jnp.concatenate(parts, axis=1),
            NT,
            preferred_element_type=f32,
        )

    def step(b, carry):
        leaf, slot = carry
        made = []
        for u in range(unroll):
            place = jnp.where(b * unroll + u < items, leaf, leaves)
            made.append((place, block(leaf, slot)))
            done = slot + PAIR >= live[side, mark + leaf]
            leaf = jnp.where(done, jnp.minimum(leaf + 1, leaves - 1), leaf)
            slot = jnp.where(done, 0, slot + PAIR)
        for place, x in made:
            total[place] += x
        return leaf, slot

    lax.fori_loop(0, (items + unroll - 1) // unroll, step, (jnp.int32(0), jnp.int32(0)))

    @pl.loop(0, leaves, unroll=8)
    def _(leaf):
        at = pl.ds(pl.multiple_of(leaf * 128, 128), 128)
        x = jnp.transpose(both(total[leaf]))
        if begin is None:
            mine[:, at] = x[0:32]
            other[:, at] = x[32:64]
        else:
            mine[:, at] = begin[0][:, at] + x[0:32]
            other[:, at] = begin[1][:, at] + x[32:64]


def near_pass(unroll, core, lists, live, targets, sources, begin=()):
    leaves = lists.shape[2] // 2
    chunks = len(sources)
    held = chunks * 2 * leaves + 1
    side = jax.ShapeDtypeStruct((32, leaves * 128), f32)
    arrays = (targets, *sources, *begin)
    return pl.pallas_call(
        functools.partial(near_body, unroll, chunks),
        out_shape=(side, side),
        in_specs=[SM, SM, SM, VM] + [HBM] * len(sources) + [VM] * len(begin),
        out_specs=(VM, VM),
        scratch_shapes=[
            pltpu.VMEM((leaves, 3, 128, 128), f32),
            pltpu.VMEM((leaves + 1, 128, 128), f32),
            pltpu.VMEM((held, 128, 128), bf16),
            pltpu.VMEM((held, 8, 128), f32),
            pltpu.SemaphoreType.DMA((len(sources),)),
            *[pltpu.VMEM(x.shape, f32) for x in sources],
        ],
        compiler_params=pltpu.CompilerParams(vmem_limit_bytes=VMEM_BYTES),
        cost_estimate=pl.CostEstimate(flops=1_000, bytes_accessed=1_000, transcendentals=0),
        name="near_pass",
    )(core, lists, live, *arrays)


def local(
    points,
    values,
    near_list,
    near_count,
    basis,
    transfer,
    coupling,
    partners,
    transfer_top,
    coupling_top,
    partners_top,
):
    leaves = basis.shape[0]
    position = lax.axis_index("leaf")
    core = lax.axis_index("rhs")
    count = lax.axis_size("leaf")
    forward = [(i, i + 1) for i in range(count - 1)]
    backward = [(target, source) for source, target in forward]
    swap = [(0, 1), (1, 0)]
    across = lax.ppermute(values, "rhs", swap)

    def ring(x, stride):
        spot = (position // stride) % 4
        turned = []
        for shift in range(3, 0, -1):
            to = [(i, i + stride * ((i // stride + shift) % 4 - i // stride % 4)) for i in range(count)]
            turned.append(lax.ppermute(x, "leaf", to))
        return turned, spot

    def in_order(turned, x, spot):
        blocks = [*turned, x]
        ordered = []
        for k in range(4):
            block = blocks[3]
            for j in range(3):
                block = jnp.where(spot == (k - j - 1) % 4, blocks[j], block)
            ordered.append(block)
        return jnp.concatenate(ordered, axis=0)

    after = lax.optimization_barrier
    core = core[None].astype(jnp.int32)
    place = position[None].astype(jnp.int32)
    coupling = coupling.transpose(1, 2, 3, 0)
    up, share, trans, lists, live, codes = up_pass(
        place, near_list.T, near_count[None], partners.T, basis, values, transfer.transpose(1, 2, 0)
    )
    turned, spot = ring(share[None], 1)
    share, coupling, across = after((share, coupling, across))
    first, packed = unbatch_pack(coupling, 0, points, values, across)
    turned, share, packed = after((turned, share, packed))
    outward = [(2 * i, 2 * i + 2) for i in range(count - 1)]
    outward += [(2 * i + 3, 2 * i + 1) for i in range(count - 1)]
    beside = lax.ppermute(packed, ("leaf", "rhs"), outward)
    level = in_order(turned, share[None], spot)
    level = jnp.where(jnp.arange(128) < 64, level[0] + level[1], level[2] + level[3])[None]
    turned, spot = ring(level, 4)
    begin = near_pass(12, core, lists, live, points, (packed,))
    coupling, turned, beside, begin = after((coupling, turned, beside, begin))
    level = in_order(turned, level, spot)
    turned, spot = ring(level, 16)
    passed = lax.dynamic_index_in_dim(beside, 1 - core[0], 0, keepdims=False)
    passed = lax.ppermute(passed, "rhs", swap)
    turned, up, coupling = after((turned, up, coupling))
    up_low = lax.ppermute(up, "leaf", forward)
    up_high = lax.ppermute(up, "leaf", backward)
    second = unbatch(coupling, 1)
    passed, lists, second = after((passed, lists, second))
    mine, other = near_pass(12, core, lists, live, points, (beside, passed), begin)
    given = lax.ppermute(other, "rhs", swap)
    return finish(
        core,
        place,
        codes,
        partners_top.T,
        (*turned, level),
        mine,
        given,
        transfer_top,
        coupling_top,
        up_low,
        up,
        up_high,
        first,
        second,
        trans,
        basis,
    )


def solution(mesh):
    placed = (
        P(None, "leaf"),
        P("rhs", "leaf"),
        P("leaf", None),
        P("leaf"),
        P("leaf", None, None),
        P("leaf", None, None),
        P("leaf", None, None, None),
        P("leaf", None),
        P(),
        P(),
        P(),
    )
    return jax.shard_map(
        local, mesh=mesh, in_specs=placed, out_specs=P("rhs", "leaf"), check_vma=False
    )
```

```python
import jax, jax.numpy as jnp, functools
from jax import lax
from jax.sharding import PartitionSpec as P
from jax.experimental import pallas as pl
from jax.experimental.pallas import tpu as pltpu
NT = (((1,), (1,)), ((), ()))
SM = pl.BlockSpec(memory_space=pltpu.SMEM)
VM = pl.BlockSpec(memory_space=pltpu.VMEM)
HBM = pl.BlockSpec(memory_space=pltpu.HBM)
PITCH = 136
VMEM_BYTES = 62 << 20
SLOTS = 28
f32 = jnp.float32
bf16 = jnp.bfloat16

def split(x):
    hi = x.astype(bf16)
    return hi, (x - hi.astype(f32)).astype(bf16)

def stack(x):
    hi, lo = split(x)
    return jnp.concatenate([hi, lo], axis=0)

def fold(x):
    half = x.shape[0] // 2
    return x[:half] + x[half:]

def both(x):
    return x + pltpu.roll(x, 64, 1)

def low_lanes(shape):
    return lax.broadcasted_iota(jnp.int32, shape, 1) < 64

def plan(place, near_list, near_count, partners, lists, live, codes):
    slots, leaves = near_list.shape
    local = near_list[...] - place * leaves
    count = near_count[...]
    inside = (local >= 0) & (local < leaves)
    row = lax.broadcasted_iota(jnp.int32, (SLOTS, leaves), 0)
    for side in range(2):
        rank = jnp.zeros((1, leaves), jnp.int32)
        found = jnp.full((SLOTS, leaves), (1 + side) * leaves, jnp.int32)
        for s in range(slots):
            here = inside[s : s + 1] if side == 0 else jnp.logical_not(inside[s : s + 1])
            picked = here & (s < count)
            ids = local[s : s + 1]
            if side == 1:
                ids = jnp.where(ids < 0, ids + leaves, ids)
            found = jnp.where((row == rank) & picked, ids, found)
            rank = rank + picked.astype(jnp.int32)
        lists[side] = found
        live[side : side + 1] = rank
    nodes = partners.shape[1]
    node = lax.broadcasted_iota(jnp.int32, (1, nodes), 1)
    span = jnp.full((1, nodes), leaves, jnp.int32)
    start = jnp.zeros((1, nodes), jnp.int32)
    width, tile, first = leaves // 2, leaves // 2, leaves
    while width >= 1:
        span = jnp.where(node >= first, width, span)
        start = jnp.where(node >= first, 2 * tile, start)
        tile, first, width = tile + max(1, width // 2), first + width, width // 2
    shifted = partners[...] - place * span
    side = jnp.where(shifted < 0, 0, jnp.where(shifted < span, 1, 2))
    codes[...] = side * (2 * leaves) + start + shifted - (side - 1) * span


def up_body(
    place, near_list, near_count, partners, basis_hbm, values_hbm, moves_hbm,
    up, share, trans_hbm, lists, live, codes, rows, basis, values, moves, trans, sem,
):
    leaves = basis.shape[0]
    columns = values.shape[0]
    nodes = moves.shape[2]
    reads = []
    for i in range(4):
        at = pl.ds(16 * i, 16)
        reads.append(pltpu.make_async_copy(moves_hbm.at[at], moves.at[at], sem.at[i]))
    reads.append(pltpu.make_async_copy(values_hbm, values, sem.at[4]))
    reads.append(pltpu.make_async_copy(basis_hbm, basis, sem.at[5]))
    for read in reads:
        read.start()
    plan(place[0], near_list, near_count, partners, lists, live, codes)
    for i in range(4):
        reads[i].wait()

        @pl.loop(16 * i, 16 * i + 16, unroll=8)
        def _(r):
            block = jnp.transpose(moves[r])
            rows[pl.ds(pl.multiple_of(r * PITCH, 8), nodes)] = jnp.concatenate([block, block], axis=1)

    left = low_lanes((64, 128))

    def node(n):
        x = rows[pl.ds(n, 64, stride=PITCH), :]
        hi = x.astype(bf16).astype(f32)
        trans[n] = jnp.where(left, hi, x - hi).astype(bf16)

    whole = nodes // 8 * 8
    pl.loop(0, whole, unroll=8)(node)
    for n in range(whole, nodes):
        node(n)
    trans[nodes] = jnp.zeros(trans.shape[1:], bf16)
    write = pltpu.make_async_copy(trans, trans_hbm, sem.at[6])
    write.start()

    half = low_lanes((columns, 128))

    for read in reads[4:]:
        read.wait()
    def leaf_up(i):
        v = stack(values[:, pl.ds(pl.multiple_of(i * 128, 128), 128)])
        return both(fold(lax.dot_general(v, stack(basis[i]), NT, preferred_element_type=f32)))

    @pl.loop(0, leaves // 2, unroll=8)
    def _(p):
        up[p] = jnp.where(half, leaf_up(2 * p), leaf_up(2 * p + 1))

    def lift(tile, row):
        t = jnp.concatenate([trans[row], trans[row + 1]], axis=0)
        return both(fold(jnp.dot(stack(tile), t, preferred_element_type=f32)))

    def pair(tile_a, tile_b, row):
        return jnp.where(half, lift(tile_a, row), lift(tile_b, row + 2))

    start, row, width = 0, 0, leaves
    while width > 16:
        after = start + width // 2

        @pl.loop(0, width // 16)
        def _(g, start=start, row=row, after=after):
            made = []
            for p in range(4):
                q = 4 * g + p
                made.append(pair(up[start + 2 * q], up[start + 2 * q + 1], row + 4 * q))
            for p in range(4):
                up[after + 4 * g + p] = made[p]

        start, row, width = after, row + width, width // 2
    tiles = [up[start + p] for p in range(width // 2)]
    while width > 1:
        after = start + width // 2
        if width >= 4:
            tiles = [pair(tiles[2 * p], tiles[2 * p + 1], row + 4 * p) for p in range(width // 4)]
        else:
            tiles = [lift(tiles[0], row)]
        if after < leaves - 1:
            for p, tile in enumerate(tiles):
                up[after + p] = tile
        start, row, width = after, row + width, width // 2
    up[leaves - 1] = tiles[0]
    share[...] = both(fold(jnp.dot(stack(tiles[0])[:, 0:64], trans[row], preferred_element_type=f32)))
    write.wait()


def up_pass(place, near_list, near_count, partners, basis, values, moves):
    leaves = basis.shape[0]
    columns = values.shape[0]
    nodes = moves.shape[2]
    return pl.pallas_call(
        up_body,
        out_shape=(
            jax.ShapeDtypeStruct((leaves, columns, 128), f32),
            jax.ShapeDtypeStruct((columns, 128), f32),
            jax.ShapeDtypeStruct((nodes + 1, 64, 128), bf16),
            jax.ShapeDtypeStruct((2, SLOTS, leaves), jnp.int32),
            jax.ShapeDtypeStruct((2, leaves), jnp.int32),
            jax.ShapeDtypeStruct(partners.shape, jnp.int32),
        ),
        in_specs=[SM, VM, VM, VM, HBM, HBM, HBM],
        out_specs=(VM, VM, HBM, VM, VM, VM),
        scratch_shapes=[
            pltpu.VMEM((64 * PITCH, 128), f32),
            pltpu.VMEM(basis.shape, f32),
            pltpu.VMEM(values.shape, f32),
            pltpu.VMEM(moves.shape, f32),
            pltpu.VMEM((nodes + 1, 64, 128), bf16),
            pltpu.SemaphoreType.DMA((7,)),
        ],
        compiler_params=pltpu.CompilerParams(vmem_limit_bytes=VMEM_BYTES),
        cost_estimate=pl.CostEstimate(flops=400_000_000, bytes_accessed=8_000_000, transcendentals=0),
        name="up_pass",
    )(place, near_list, near_count, partners, basis, values, moves)


CHUNK = 32


def unbatch_body(part, matrices, out, held, rows, made, in_sem, out_sem):
    nodes = matrices.shape[3]
    pieces = 4
    step = matrices.shape[1] // pieces
    reads = []
    for i in range(pieces):
        at = pl.ds(i * step, step)
        reads.append(
            pltpu.make_async_copy(matrices.at[pl.ds(2 * part, 2), at], held.at[:, at], in_sem.at[i])
        )
        reads[-1].start()
    for i in range(pieces):
        reads[i].wait()

        @pl.loop(i * step, (i + 1) * step, unroll=8)
        def _(r):
            x = jnp.concatenate([held[0, r], held[1, r]], axis=0)
            rows[pl.ds(pl.multiple_of(r * PITCH, 8), nodes)] = jnp.transpose(x)

    def one(n):
        hi, lo = split(rows[pl.ds(n, 64, stride=PITCH), :])
        made[n, 0:64] = hi
        made[n, 64:128] = lo

    writes = []
    for c, begin in enumerate(range(0, nodes, CHUNK)):
        size = min(CHUNK, nodes - begin)
        whole = begin + size // 8 * 8
        pl.loop(begin, whole, unroll=8)(one)
        for n in range(whole, begin + size):
            one(n)
        at = pl.ds(begin, size)
        writes.append(pltpu.make_async_copy(made.at[at], out.at[at], out_sem.at[c]))
        writes[-1].start()
    for write in writes:
        write.wait()


def arrange(points, values, across, packed):
    leaves = values.shape[1] // 128
    block = leaves // 2
    for c in range(3):
        for j in range(leaves):
            packed[j // block, 2 * block + c, j % block : j % block + 1] = points[
                c : c + 1, 128 * j : 128 * j + 128
            ]
    for side in range(2):

        @pl.loop(0, block, unroll=8)
        def _(j, side=side):
            at = pl.ds(pl.multiple_of((side * block + j) * 128, 128), 128)
            packed[side, j] = values[:, at]
            packed[side, block + j] = across[:, at]


def pack_body(points, values_hbm, across_hbm, out_hbm, values, across, packed, sem):
    takes = [
        pltpu.make_async_copy(values_hbm, values, sem.at[0]),
        pltpu.make_async_copy(across_hbm, across, sem.at[1]),
    ]
    for take in takes:
        take.start()
    for take in takes:
        take.wait()
    arrange(points, values, across, packed)
    sends = [pltpu.make_async_copy(packed.at[i], out_hbm.at[i], sem.at[2 + i]) for i in range(2)]
    for send in sends:
        send.start()
    for send in sends:
        send.wait()


def pack(points, values, across):
    columns, width = values.shape
    packed = (2, width // 128 + 3, columns, 128)
    return pl.pallas_call(
        pack_body,
        out_shape=jax.ShapeDtypeStruct(packed, f32),
        in_specs=[VM, HBM, HBM],
        out_specs=HBM,
        scratch_shapes=[
            pltpu.VMEM(values.shape, f32),
            pltpu.VMEM(values.shape, f32),
            pltpu.VMEM(packed, f32),
            pltpu.SemaphoreType.DMA((4,)),
        ],
        compiler_params=pltpu.CompilerParams(vmem_limit_bytes=VMEM_BYTES),
        name="pack",
    )(points, values, across)


def unbatch(matrices, part):
    nodes = matrices.shape[3]
    return pl.pallas_call(
        functools.partial(unbatch_body, part),
        out_shape=jax.ShapeDtypeStruct((nodes, 128, 128), bf16),
        in_specs=[HBM],
        out_specs=HBM,
        scratch_shapes=[
            pltpu.VMEM((2, *matrices.shape[1:]), f32),
            pltpu.VMEM((64 * PITCH, 128), f32),
            pltpu.VMEM((nodes, 128, 128), bf16),
            pltpu.SemaphoreType.DMA((4,)),
            pltpu.SemaphoreType.DMA((-(-nodes // CHUNK),)),
        ],
        compiler_params=pltpu.CompilerParams(vmem_limit_bytes=VMEM_BYTES),
        cost_estimate=pl.CostEstimate(flops=1_000, bytes_accessed=1_000, transcendentals=0),
        name="unbatch",
    )(matrices)


def top_chain(place, partners, gathered, moves, up, block, arrived):
    spot = place[0]
    columns = gathered[0].shape[1]
    half = low_lanes((columns, 128))
    for j, ref in enumerate(gathered):
        up[pl.ds(4 * ((spot // 16 + 1 + j) % 4), 4)] = ref[...]
    def lift(tile, r):
        t = jnp.concatenate([moves[r], moves[r + 1]], axis=0)
        hi, lo = split(t)
        x = stack(up[tile])
        z = fold(jnp.dot(x, hi, preferred_element_type=f32)) + jnp.dot(x[:columns], lo, preferred_element_type=f32)
        return jnp.concatenate([z, z], axis=1)
    tile0, row, width = 0, 0, 32
    tiles, rows = [], []
    while width >= 4:
        tiles.append(tile0)
        rows.append(row)
        nxt = tile0 + width // 2
        if width > 4:
            for p in range(width // 4):
                up[nxt + p] = jnp.where(half, lift(tile0 + 2 * p, row + 4 * p), lift(tile0 + 2 * p + 1, row + 4 * p + 2))
        tile0, row, width = nxt, row + width, width // 2
    def push(d, r):
        hi, lo = split(moves[r])
        x = stack(d)
        return fold(lax.dot_general(x, hi, NT, preferred_element_type=f32)) + lax.dot_general(x[:columns], lo, NT, preferred_element_type=f32)
    arrived()
    fars = []
    for level in range(4):
        index = rows[level] + spot // (2 << level)
        far = jnp.zeros((columns, 64), f32)
        for k in range(4):
            p = partners[k, index]
            tile = up[tiles[level] + p // 2]
            x = stack(jnp.where(p % 2 == 0, tile, pltpu.roll(tile, 64, 1))[:, 0:64])
            hi, lo = split(block[level, k])
            far = far + fold(lax.dot_general(x, hi, NT, preferred_element_type=f32))
            far = far + lax.dot_general(x[:columns], lo, NT, preferred_element_type=f32)
        fars.append(far)
    down = jnp.zeros((columns, 64), f32)
    down = push(down, row + spot // 32)
    for level in range(3, -1, -1):
        down = push(down, rows[level] + spot // (2 << level)) + fars[level]
    return jnp.concatenate([down, down], axis=1)


def couple(codes, far, gather, tiles, held, takes, reads):
    _, leaves, columns, _ = tiles.shape
    nodes = held.shape[1]
    half = low_lanes((columns, 128))
    left = low_lanes((2 * columns, 128))
    for side in range(3):
        takes[side].wait()

        @pl.loop(0, leaves, unroll=16)
        def _(t, side=side):
            x = tiles[side, t]
            gather[0, side * leaves + t] = stack(x)
            gather[1, side * leaves + t] = stack(pltpu.roll(x, 64, 1))

    def pick(n, k, side):
        code = codes[k, n]
        return gather[(code & 1) ^ side, code >> 1]

    def one(n):
        x = jnp.concatenate(
            [
                jnp.where(left, pick(n, 0, 0), pick(n, 1, 1)),
                jnp.where(left, pick(n, 2, 0), pick(n, 3, 1)),
            ],
            axis=1,
        )
        m = jnp.concatenate([held[0, n], held[1, n]], axis=1)
        return both(fold(lax.dot_general(x, m, NT, preferred_element_type=f32)))

    for i in range(3):
        reads[2 * i].wait()
        reads[2 * i + 1].wait()

        @pl.loop(21 * i, 21 * i + 21, unroll=7)
        def _(t):
            far[t] = jnp.where(half, one(2 * t), one(2 * t + 1))

    far[leaves - 1] = one(nodes - 1)


def descend(core, parent, far, trans, basis, mine, given, out, ones, twos, moved, based):
    leaves = basis.shape[0]
    columns = out.shape[0]
    half = low_lanes((columns, 128))

    def push(d, tile):
        t = jnp.concatenate([trans[2 * tile], trans[2 * tile + 1]], axis=0)
        return fold(lax.dot_general(stack(d), t, NT, preferred_element_type=f32)) + far[tile]

    def spread(tile):
        turned = pltpu.roll(tile, 64, 1)
        return jnp.where(half, tile, turned), jnp.where(half, turned, tile)

    last = leaves - 1
    above = stack(parent)
    moved.wait()
    t = trans[2 * last]
    t = jnp.concatenate([t, t], axis=0)
    sources = [fold(lax.dot_general(above, t, NT, preferred_element_type=f32)) + far[last]]
    start, width = last, 1
    while width < 16:
        start = start - width
        made = [push(d, start + i) for i, d in enumerate(sources)]
        sources = [d for tile in made for d in spread(tile)]
        width = 2 * width
    start = start - width
    for i, d in enumerate(sources):
        ones[i] = push(d, start + i)

    @pl.loop(0, width, unroll=8)
    def _(i):
        for u, d in enumerate(spread(ones[i])):
            twos[2 * i + u] = push(d, 2 * i + u)

    based.wait()

    @pl.loop(0, leaves // 2, unroll=4)
    def _(i):
        for u, d in enumerate(spread(twos[i])):
            leaf = 2 * i + u
            out[:, pl.ds(pl.multiple_of(leaf * 128, 128), 128)] = fold(
                jnp.dot(stack(d), stack(basis[leaf]), preferred_element_type=f32)
            )

    size = mine.shape[1]
    out[:, pl.ds(pl.multiple_of(core[0] * size, size), size)] += mine[...]
    out[:, pl.ds(pl.multiple_of((1 - core[0]) * size, size), size)] += given[...]


def finish_body(
    core, place, codes, partners, three, two, one, level, mine, given,
    moves_hbm, matrices, low, own, high, first, second, trans_hbm, basis_hbm, out,
    moves, block, up, tiles, held, trans, basis, gather, far, ones, twos, sem,
):
    spot = place[0]
    queue = []

    def bring(source, dest):
        copy = pltpu.make_async_copy(source, dest, sem.at[len(queue)])
        copy.start()
        queue.append(copy)
        return copy

    lifted = bring(moves_hbm, moves)
    blocks = []
    width, row = 32, 0
    for i in range(4):
        blocks.append(bring(matrices.at[row + spot // (2 << i)], block.at[i]))
        row, width = row + width, width // 2
    takes = [bring(ref, tiles.at[side]) for side, ref in enumerate((low, own, high))]
    nodes = first.shape[0]
    reads = []
    for i in range(3):
        at = pl.ds(42 * i, nodes - 84 if i == 2 else 42)
        for h, x in enumerate((first, second)):
            reads.append(bring(x.at[at], held.at[h, at]))
    moved = bring(trans_hbm, trans)
    based = bring(basis_hbm, basis)

    def arrived():
        for copy in blocks:
            copy.wait()

    lifted.wait()
    parent = top_chain(place, partners, (three, two, one, level), moves, up, block, arrived)
    couple(codes, far, gather, tiles, held, takes, reads)
    descend(core, parent, far, trans, basis, mine, given, out, ones, twos, moved, based)


def finish(core, place, codes, partners, gathered, mine, given, moves, matrices, low, own, high, first, second, trans, basis):
    leaves, columns, _ = own.shape
    return pl.pallas_call(
        finish_body,
        out_shape=jax.ShapeDtypeStruct((columns, leaves * 128), f32),
        in_specs=[SM] * 4 + [VM] * 6 + [HBM] * 9,
        out_specs=VM,
        scratch_shapes=[
            pltpu.VMEM(moves.shape, f32),
            pltpu.VMEM((4, *matrices.shape[1:]), f32),
            pltpu.VMEM((32, columns, 128), f32),
            pltpu.VMEM((3, leaves, columns, 128), f32),
            pltpu.VMEM((2, *first.shape), bf16),
            pltpu.VMEM(trans.shape, bf16),
            pltpu.VMEM(basis.shape, f32),
            pltpu.VMEM((2, 3 * leaves, 2 * columns, 128), bf16),
            pltpu.VMEM((leaves, columns, 128), f32),
            pltpu.VMEM((leaves // 4, columns, 128), f32),
            pltpu.VMEM((leaves // 2, columns, 128), f32),
            pltpu.SemaphoreType.DMA((16,)),
        ],
        compiler_params=pltpu.CompilerParams(vmem_limit_bytes=VMEM_BYTES),
        cost_estimate=pl.CostEstimate(flops=1_000_000_000, bytes_accessed=20_000_000, transcendentals=0),
        name="finish",
    )(core, place, codes, partners, *gathered, mine, given, moves, matrices, low, own, high, first, second, trans, basis)


near_weight = 0.1
smoothing = 0.0025
PAIR = 2

def near_body(unroll, chunks, core, lists, live, targets, *refs):
    origins, refs = refs[:chunks], refs[chunks:]
    begin = None
    if chunks == 2:
        begin, refs = refs[0:2], refs[2:]
    mine, other, columns_of, total, weights, places, sem, *sources = refs
    leaves = mine.shape[1] // 128
    width = 2 * leaves
    core = core[0]
    side = chunks - 1
    mark = core * leaves
    reads = []
    for i, (origin, source) in enumerate(zip(origins, sources)):
        reads.append(pltpu.make_async_copy(origin, source, sem.at[i]))
        reads[-1].start()
    weights[chunks * width] = jnp.zeros(weights.shape[1:], bf16)
    places[chunks * width] = jnp.zeros(places.shape[1:], f32)
    blank = jnp.zeros((5, 128), f32)

    @pl.loop(0, leaves // 16)
    def _(g):
        rows = []
        for u in range(16):
            at = pl.ds(pl.multiple_of((core * leaves + 16 * g + u) * 128, 128), 128)
            rows += [targets[:, at], blank]
        t = jnp.transpose(jnp.concatenate(rows, axis=0))
        for u in range(16):
            for c in range(3):
                columns_of[16 * g + u, c] = jnp.broadcast_to(t[:, 8 * u + c : 8 * u + c + 1], (128, 128))
            total[16 * g + u] = jnp.zeros((128, 128), f32)

    for read in reads:
        read.wait()

    def load(block, base, turn):
        @pl.loop(0, leaves // 8)
        def _(g):
            for u in range(8):
                j = 8 * g + u
                x = [block[j], block[leaves + j]]
                weights[base + j] = stack(near_weight * jnp.concatenate(x[::-1] if turn else x, axis=0))
                for c in range(3):
                    places[base + j, c : c + 1] = block[2 * leaves + c, pl.ds(j, 1)]

    base = width * core if chunks == 2 else 0
    load(sources[0].at[0], base, False)
    load(sources[0].at[1], base + leaves, False)
    if chunks == 2:
        load(sources[1], width - leaves * core, True)
    items = lax.fori_loop(
        0, leaves, lambda i, s: s + jnp.maximum((live[side, mark + i] + PAIR - 1) // PAIR, 1), jnp.int32(0)
    )

    def block(leaf, slot):
        kernels, parts = [], []
        for u in range(PAIR):
            j = lists[side, slot + u, mark + leaf]
            s = places[j]
            d = columns_of[leaf, 0] - s[0:1]
            squared = d * d + smoothing
            d = columns_of[leaf, 1] - s[1:2]
            squared = squared + d * d
            d = columns_of[leaf, 2] - s[2:3]
            squared = squared + d * d
            kernels += split(lax.rsqrt(squared))
            x = weights[j]
            parts += [x, x]
        return lax.dot_general(
            jnp.concatenate(kernels, axis=1),
            jnp.concatenate(parts, axis=1),
            NT,
            preferred_element_type=f32,
        )

    def step(b, carry):
        leaf, slot = carry
        made = []
        for u in range(unroll):
            place = jnp.where(b * unroll + u < items, leaf, leaves)
            made.append((place, block(leaf, slot)))
            done = slot + PAIR >= live[side, mark + leaf]
            leaf = jnp.where(done, jnp.minimum(leaf + 1, leaves - 1), leaf)
            slot = jnp.where(done, 0, slot + PAIR)
        for place, x in made:
            total[place] += x
        return leaf, slot

    lax.fori_loop(0, (items + unroll - 1) // unroll, step, (jnp.int32(0), jnp.int32(0)))

    @pl.loop(0, leaves, unroll=8)
    def _(leaf):
        at = pl.ds(pl.multiple_of(leaf * 128, 128), 128)
        x = jnp.transpose(both(total[leaf]))
        if begin is None:
            mine[:, at] = x[0:32]
            other[:, at] = x[32:64]
        else:
            mine[:, at] = begin[0][:, at] + x[0:32]
            other[:, at] = begin[1][:, at] + x[32:64]


def near_pass(unroll, core, lists, live, targets, sources, begin=()):
    leaves = lists.shape[2] // 2
    chunks = len(sources)
    held = chunks * 2 * leaves + 1
    side = jax.ShapeDtypeStruct((32, leaves * 128), f32)
    arrays = (targets, *sources, *begin)
    return pl.pallas_call(
        functools.partial(near_body, unroll, chunks),
        out_shape=(side, side),
        in_specs=[SM, SM, SM, VM] + [HBM] * len(sources) + [VM] * len(begin),
        out_specs=(VM, VM),
        scratch_shapes=[
            pltpu.VMEM((leaves, 3, 128, 128), f32),
            pltpu.VMEM((leaves + 1, 128, 128), f32),
            pltpu.VMEM((held, 128, 128), bf16),
            pltpu.VMEM((held, 8, 128), f32),
            pltpu.SemaphoreType.DMA((len(sources),)),
            *[pltpu.VMEM(x.shape, f32) for x in sources],
        ],
        compiler_params=pltpu.CompilerParams(vmem_limit_bytes=VMEM_BYTES),
        cost_estimate=pl.CostEstimate(flops=1_000, bytes_accessed=1_000, transcendentals=0),
        name="near_pass",
    )(core, lists, live, *arrays)


def local(
    points,
    values,
    near_list,
    near_count,
    basis,
    transfer,
    coupling,
    partners,
    transfer_top,
    coupling_top,
    partners_top,
):
    leaves = basis.shape[0]
    position = lax.axis_index("leaf")
    core = lax.axis_index("rhs")
    count = lax.axis_size("leaf")
    forward = [(i, i + 1) for i in range(count - 1)]
    backward = [(target, source) for source, target in forward]
    swap = [(0, 1), (1, 0)]
    across = lax.ppermute(values, "rhs", swap)

    def ring(x, stride):
        spot = (position // stride) % 4
        turned = []
        for shift in range(3, 0, -1):
            to = [(i, i + stride * ((i // stride + shift) % 4 - i // stride % 4)) for i in range(count)]
            turned.append(lax.ppermute(x, "leaf", to))
        return turned, spot

    def in_order(turned, x, spot):
        blocks = [*turned, x]
        ordered = []
        for k in range(4):
            block = blocks[3]
            for j in range(3):
                block = jnp.where(spot == (k - j - 1) % 4, blocks[j], block)
            ordered.append(block)
        return jnp.concatenate(ordered, axis=0)

    after = lax.optimization_barrier
    core = core[None].astype(jnp.int32)
    place = position[None].astype(jnp.int32)
    coupling = coupling.transpose(1, 2, 3, 0)
    first = unbatch(coupling, 0)
    across, first, coupling = after((across, first, coupling))
    packed = pack(points, values, across)
    outward = [(2 * i, 2 * i + 2) for i in range(count - 1)]
    outward += [(2 * i + 3, 2 * i + 1) for i in range(count - 1)]
    beside = lax.ppermute(packed, ("leaf", "rhs"), outward)
    place, packed = after((place, packed))
    up, share, trans, lists, live, codes = up_pass(
        place, near_list.T, near_count[None], partners.T, basis, values, transfer.transpose(1, 2, 0)
    )
    begin = near_pass(12, core, lists, live, points, (packed,))
    share, beside, begin = after((share, beside, begin))
    turned, spot = ring(share[None], 1)
    passed = lax.dynamic_index_in_dim(beside, 1 - core[0], 0, keepdims=False)
    passed = lax.ppermute(passed, "rhs", swap)
    turned, passed, up = after((turned, passed, up))
    level = in_order(turned, share[None], spot)
    level = jnp.where(jnp.arange(128) < 64, level[0] + level[1], level[2] + level[3])[None]
    turned, spot = ring(level, 4)
    up_low = lax.ppermute(up, "leaf", forward)
    up_high = lax.ppermute(up, "leaf", backward)
    mine, other = near_pass(12, core, lists, live, points, (beside, passed), begin)
    turned, mine, other, coupling, up_low = after((turned, mine, other, coupling, up_low))
    level = in_order(turned, level, spot)
    turned, spot = ring(level, 16)
    given = lax.ppermute(other, "rhs", swap)
    second = unbatch(coupling, 1)
    turned, given, up_low, up_high, second = after((turned, given, up_low, up_high, second))
    return finish(
        core,
        place,
        codes,
        partners_top.T,
        (*turned, level),
        mine,
        given,
        transfer_top,
        coupling_top,
        up_low,
        up,
        up_high,
        first,
        second,
        trans,
        basis,
    )


def solution(mesh):
    placed = (
        P(None, "leaf"),
        P("rhs", "leaf"),
        P("leaf", None),
        P("leaf"),
        P("leaf", None, None),
        P("leaf", None, None),
        P("leaf", None, None, None),
        P("leaf", None),
        P(),
        P(),
        P(),
    )
    return jax.shard_map(
        local, mesh=mesh, in_specs=placed, out_specs=P("rhs", "leaf"), check_vma=False
    )
```

```python
import jax, jax.numpy as jnp, functools
from jax import lax
from jax.sharding import PartitionSpec as P
from jax.experimental import pallas as pl
from jax.experimental.pallas import tpu as pltpu
NT = (((1,), (1,)), ((), ()))
SM = pl.BlockSpec(memory_space=pltpu.SMEM)
VM = pl.BlockSpec(memory_space=pltpu.VMEM)
HBM = pl.BlockSpec(memory_space=pltpu.HBM)
PITCH = 136
VMEM_BYTES = 62 << 20
SLOTS = 28
f32 = jnp.float32
bf16 = jnp.bfloat16

def split(x):
    hi = x.astype(bf16)
    return hi, (x - hi.astype(f32)).astype(bf16)

def stack(x):
    hi, lo = split(x)
    return jnp.concatenate([hi, lo], axis=0)

def fold(x):
    half = x.shape[0] // 2
    return x[:half] + x[half:]

def both(x):
    return x + pltpu.roll(x, 64, 1)

def low_lanes(shape):
    return lax.broadcasted_iota(jnp.int32, shape, 1) < 64

def plan(place, near_list, near_count, partners, lists, live, codes):
    slots, leaves = near_list.shape
    local = near_list[...] - place * leaves
    count = near_count[...]
    inside = (local >= 0) & (local < leaves)
    row = lax.broadcasted_iota(jnp.int32, (SLOTS, leaves), 0)
    for side in range(2):
        rank = jnp.zeros((1, leaves), jnp.int32)
        found = jnp.full((SLOTS, leaves), (1 + side) * leaves, jnp.int32)
        for s in range(slots):
            here = inside[s : s + 1] if side == 0 else jnp.logical_not(inside[s : s + 1])
            picked = here & (s < count)
            ids = local[s : s + 1]
            if side == 1:
                ids = jnp.where(ids < 0, ids + leaves, ids)
            found = jnp.where((row == rank) & picked, ids, found)
            rank = rank + picked.astype(jnp.int32)
        lists[side] = found
        live[side : side + 1] = rank
    nodes = partners.shape[1]
    node = lax.broadcasted_iota(jnp.int32, (1, nodes), 1)
    span = jnp.full((1, nodes), leaves, jnp.int32)
    start = jnp.zeros((1, nodes), jnp.int32)
    width, tile, first = leaves // 2, leaves // 2, leaves
    while width >= 1:
        span = jnp.where(node >= first, width, span)
        start = jnp.where(node >= first, 2 * tile, start)
        tile, first, width = tile + max(1, width // 2), first + width, width // 2
    shifted = partners[...] - place * span
    side = jnp.where(shifted < 0, 0, jnp.where(shifted < span, 1, 2))
    codes[...] = side * (2 * leaves) + start + shifted - (side - 1) * span


def up_body(
    place, near_list, near_count, partners, basis_hbm, values_hbm, moves_hbm,
    up, share, trans_hbm, lists, live, codes, rows, basis, values, moves, trans, sem,
):
    leaves = basis.shape[0]
    columns = values.shape[0]
    nodes = moves.shape[2]
    reads = []
    for i in range(4):
        at = pl.ds(16 * i, 16)
        reads.append(pltpu.make_async_copy(moves_hbm.at[at], moves.at[at], sem.at[i]))
    reads.append(pltpu.make_async_copy(values_hbm, values, sem.at[4]))
    reads.append(pltpu.make_async_copy(basis_hbm, basis, sem.at[5]))
    for read in reads:
        read.start()
    plan(place[0], near_list, near_count, partners, lists, live, codes)
    for i in range(4):
        reads[i].wait()

        @pl.loop(16 * i, 16 * i + 16, unroll=8)
        def _(r):
            block = jnp.transpose(moves[r])
            rows[pl.ds(pl.multiple_of(r * PITCH, 8), nodes)] = jnp.concatenate([block, block], axis=1)

    left = low_lanes((64, 128))

    def node(n):
        x = rows[pl.ds(n, 64, stride=PITCH), :]
        hi = x.astype(bf16).astype(f32)
        trans[n] = jnp.where(left, hi, x - hi).astype(bf16)

    whole = nodes // 8 * 8
    pl.loop(0, whole, unroll=8)(node)
    for n in range(whole, nodes):
        node(n)
    trans[nodes] = jnp.zeros(trans.shape[1:], bf16)
    write = pltpu.make_async_copy(trans, trans_hbm, sem.at[6])
    write.start()

    half = low_lanes((columns, 128))

    for read in reads[4:]:
        read.wait()
    def leaf_up(i):
        v = stack(values[:, pl.ds(pl.multiple_of(i * 128, 128), 128)])
        return both(fold(lax.dot_general(v, stack(basis[i]), NT, preferred_element_type=f32)))

    @pl.loop(0, leaves // 2, unroll=8)
    def _(p):
        up[p] = jnp.where(half, leaf_up(2 * p), leaf_up(2 * p + 1))

    def lift(tile, row):
        t = jnp.concatenate([trans[row], trans[row + 1]], axis=0)
        return both(fold(jnp.dot(stack(tile), t, preferred_element_type=f32)))

    def pair(tile_a, tile_b, row):
        return jnp.where(half, lift(tile_a, row), lift(tile_b, row + 2))

    start, row, width = 0, 0, leaves
    while width > 16:
        after = start + width // 2

        @pl.loop(0, width // 16)
        def _(g, start=start, row=row, after=after):
            made = []
            for p in range(4):
                q = 4 * g + p
                made.append(pair(up[start + 2 * q], up[start + 2 * q + 1], row + 4 * q))
            for p in range(4):
                up[after + 4 * g + p] = made[p]

        start, row, width = after, row + width, width // 2
    tiles = [up[start + p] for p in range(width // 2)]
    while width > 1:
        after = start + width // 2
        if width >= 4:
            tiles = [pair(tiles[2 * p], tiles[2 * p + 1], row + 4 * p) for p in range(width // 4)]
        else:
            tiles = [lift(tiles[0], row)]
        if after < leaves - 1:
            for p, tile in enumerate(tiles):
                up[after + p] = tile
        start, row, width = after, row + width, width // 2
    up[leaves - 1] = tiles[0]
    share[...] = both(fold(jnp.dot(stack(tiles[0])[:, 0:64], trans[row], preferred_element_type=f32)))
    write.wait()


def up_pass(place, near_list, near_count, partners, basis, values, moves):
    leaves = basis.shape[0]
    columns = values.shape[0]
    nodes = moves.shape[2]
    return pl.pallas_call(
        up_body,
        out_shape=(
            jax.ShapeDtypeStruct((leaves, columns, 128), f32),
            jax.ShapeDtypeStruct((columns, 128), f32),
            jax.ShapeDtypeStruct((nodes + 1, 64, 128), bf16),
            jax.ShapeDtypeStruct((2, SLOTS, leaves), jnp.int32),
            jax.ShapeDtypeStruct((2, leaves), jnp.int32),
            jax.ShapeDtypeStruct(partners.shape, jnp.int32),
        ),
        in_specs=[SM, VM, VM, VM, HBM, HBM, HBM],
        out_specs=(VM, VM, HBM, VM, VM, VM),
        scratch_shapes=[
            pltpu.VMEM((64 * PITCH, 128), f32),
            pltpu.VMEM(basis.shape, f32),
            pltpu.VMEM(values.shape, f32),
            pltpu.VMEM(moves.shape, f32),
            pltpu.VMEM((nodes + 1, 64, 128), bf16),
            pltpu.SemaphoreType.DMA((7,)),
        ],
        compiler_params=pltpu.CompilerParams(vmem_limit_bytes=VMEM_BYTES),
        cost_estimate=pl.CostEstimate(flops=400_000_000, bytes_accessed=8_000_000, transcendentals=0),
        name="up_pass",
    )(place, near_list, near_count, partners, basis, values, moves)


CHUNK = 32


def unbatch_body(part, matrices, out, held, rows, made, in_sem, out_sem):
    nodes = matrices.shape[3]
    pieces = 4
    step = matrices.shape[1] // pieces
    reads = []
    for i in range(pieces):
        at = pl.ds(i * step, step)
        reads.append(
            pltpu.make_async_copy(matrices.at[pl.ds(2 * part, 2), at], held.at[:, at], in_sem.at[i])
        )
        reads[-1].start()
    for i in range(pieces):
        reads[i].wait()

        @pl.loop(i * step, (i + 1) * step, unroll=8)
        def _(r):
            x = jnp.concatenate([held[0, r], held[1, r]], axis=0)
            rows[pl.ds(pl.multiple_of(r * PITCH, 8), nodes)] = jnp.transpose(x)

    def one(n):
        hi, lo = split(rows[pl.ds(n, 64, stride=PITCH), :])
        made[n, 0:64] = hi
        made[n, 64:128] = lo

    writes = []
    for c, begin in enumerate(range(0, nodes, CHUNK)):
        size = min(CHUNK, nodes - begin)
        whole = begin + size // 8 * 8
        pl.loop(begin, whole, unroll=8)(one)
        for n in range(whole, begin + size):
            one(n)
        at = pl.ds(begin, size)
        writes.append(pltpu.make_async_copy(made.at[at], out.at[at], out_sem.at[c]))
        writes[-1].start()
    for write in writes:
        write.wait()


def pack_body(points, values_hbm, across_hbm, out_hbm, values, across, packed, sem):
    leaves = values.shape[1] // 128
    block = leaves // 2
    takes = []
    for side in range(2):
        at = pl.ds(side * block * 128, block * 128)
        for k, (source, dest) in enumerate(((values_hbm, values), (across_hbm, across))):
            takes.append(
                pltpu.make_async_copy(source.at[:, at], dest.at[:, at], sem.at[2 * side + k])
            )
            takes[-1].start()
    for c in range(3):
        for j in range(leaves):
            packed[j // block, 2 * block + c, j % block : j % block + 1] = points[
                c : c + 1, 128 * j : 128 * j + 128
            ]
    sends = []
    for side in range(2):
        takes[2 * side].wait()
        takes[2 * side + 1].wait()

        @pl.loop(0, block, unroll=8)
        def _(j, side=side):
            at = pl.ds(pl.multiple_of((side * block + j) * 128, 128), 128)
            packed[side, j] = values[:, at]
            packed[side, block + j] = across[:, at]

        sends.append(pltpu.make_async_copy(packed.at[side], out_hbm.at[side], sem.at[4 + side]))
        sends[-1].start()
    for send in sends:
        send.wait()


def pack(points, values, across):
    columns, width = values.shape
    packed = (2, width // 128 + 3, columns, 128)
    return pl.pallas_call(
        pack_body,
        out_shape=jax.ShapeDtypeStruct(packed, f32),
        in_specs=[VM, HBM, HBM],
        out_specs=HBM,
        scratch_shapes=[
            pltpu.VMEM(values.shape, f32),
            pltpu.VMEM(values.shape, f32),
            pltpu.VMEM(packed, f32),
            pltpu.SemaphoreType.DMA((6,)),
        ],
        compiler_params=pltpu.CompilerParams(vmem_limit_bytes=VMEM_BYTES),
        name="pack",
    )(points, values, across)


def unbatch(matrices, part):
    nodes = matrices.shape[3]
    return pl.pallas_call(
        functools.partial(unbatch_body, part),
        out_shape=jax.ShapeDtypeStruct((nodes, 128, 128), bf16),
        in_specs=[HBM],
        out_specs=HBM,
        scratch_shapes=[
            pltpu.VMEM((2, *matrices.shape[1:]), f32),
            pltpu.VMEM((64 * PITCH, 128), f32),
            pltpu.VMEM((nodes, 128, 128), bf16),
            pltpu.SemaphoreType.DMA((4,)),
            pltpu.SemaphoreType.DMA((-(-nodes // CHUNK),)),
        ],
        compiler_params=pltpu.CompilerParams(vmem_limit_bytes=VMEM_BYTES),
        cost_estimate=pl.CostEstimate(flops=1_000, bytes_accessed=1_000, transcendentals=0),
        name="unbatch",
    )(matrices)


def top_chain(place, partners, gathered, moves, up, block, arrived):
    spot = place[0]
    columns = gathered[0].shape[1]
    half = low_lanes((columns, 128))
    for j, ref in enumerate(gathered):
        up[pl.ds(4 * ((spot // 16 + 1 + j) % 4), 4)] = ref[...]
    def lift(tile, r):
        t = jnp.concatenate([moves[r], moves[r + 1]], axis=0)
        hi, lo = split(t)
        x = stack(up[tile])
        z = fold(jnp.dot(x, hi, preferred_element_type=f32)) + jnp.dot(x[:columns], lo, preferred_element_type=f32)
        return jnp.concatenate([z, z], axis=1)
    tile0, row, width = 0, 0, 32
    tiles, rows = [], []
    while width >= 4:
        tiles.append(tile0)
        rows.append(row)
        nxt = tile0 + width // 2
        if width > 4:
            for p in range(width // 4):
                up[nxt + p] = jnp.where(half, lift(tile0 + 2 * p, row + 4 * p), lift(tile0 + 2 * p + 1, row + 4 * p + 2))
        tile0, row, width = nxt, row + width, width // 2
    def push(d, r):
        hi, lo = split(moves[r])
        x = stack(d)
        return fold(lax.dot_general(x, hi, NT, preferred_element_type=f32)) + lax.dot_general(x[:columns], lo, NT, preferred_element_type=f32)
    arrived()
    fars = []
    for level in range(4):
        index = rows[level] + spot // (2 << level)
        far = jnp.zeros((columns, 64), f32)
        for k in range(4):
            p = partners[k, index]
            tile = up[tiles[level] + p // 2]
            x = stack(jnp.where(p % 2 == 0, tile, pltpu.roll(tile, 64, 1))[:, 0:64])
            hi, lo = split(block[level, k])
            far = far + fold(lax.dot_general(x, hi, NT, preferred_element_type=f32))
            far = far + lax.dot_general(x[:columns], lo, NT, preferred_element_type=f32)
        fars.append(far)
    down = jnp.zeros((columns, 64), f32)
    down = push(down, row + spot // 32)
    for level in range(3, -1, -1):
        down = push(down, rows[level] + spot // (2 << level)) + fars[level]
    return jnp.concatenate([down, down], axis=1)


def couple(codes, far, gather, tiles, held, takes, reads):
    _, leaves, columns, _ = tiles.shape
    nodes = held.shape[1]
    half = low_lanes((columns, 128))
    left = low_lanes((2 * columns, 128))
    for side in range(3):
        takes[side].wait()

        @pl.loop(0, leaves, unroll=16)
        def _(t, side=side):
            x = tiles[side, t]
            gather[0, side * leaves + t] = stack(x)
            gather[1, side * leaves + t] = stack(pltpu.roll(x, 64, 1))

    def pick(n, k, side):
        code = codes[k, n]
        return gather[(code & 1) ^ side, code >> 1]

    def one(n):
        x = jnp.concatenate(
            [
                jnp.where(left, pick(n, 0, 0), pick(n, 1, 1)),
                jnp.where(left, pick(n, 2, 0), pick(n, 3, 1)),
            ],
            axis=1,
        )
        m = jnp.concatenate([held[0, n], held[1, n]], axis=1)
        return both(fold(lax.dot_general(x, m, NT, preferred_element_type=f32)))

    for i in range(3):
        reads[2 * i].wait()
        reads[2 * i + 1].wait()

        @pl.loop(21 * i, 21 * i + 21, unroll=7)
        def _(t):
            far[t] = jnp.where(half, one(2 * t), one(2 * t + 1))

    far[leaves - 1] = one(nodes - 1)


def descend(core, parent, far, trans, basis, mine, given, out, ones, twos, moved, based):
    leaves = basis.shape[0]
    columns = out.shape[0]
    half = low_lanes((columns, 128))

    def push(d, tile):
        t = jnp.concatenate([trans[2 * tile], trans[2 * tile + 1]], axis=0)
        return fold(lax.dot_general(stack(d), t, NT, preferred_element_type=f32)) + far[tile]

    def spread(tile):
        turned = pltpu.roll(tile, 64, 1)
        return jnp.where(half, tile, turned), jnp.where(half, turned, tile)

    last = leaves - 1
    above = stack(parent)
    moved.wait()
    t = trans[2 * last]
    t = jnp.concatenate([t, t], axis=0)
    sources = [fold(lax.dot_general(above, t, NT, preferred_element_type=f32)) + far[last]]
    start, width = last, 1
    while width < 16:
        start = start - width
        made = [push(d, start + i) for i, d in enumerate(sources)]
        sources = [d for tile in made for d in spread(tile)]
        width = 2 * width
    start = start - width
    for i, d in enumerate(sources):
        ones[i] = push(d, start + i)

    @pl.loop(0, width, unroll=8)
    def _(i):
        for u, d in enumerate(spread(ones[i])):
            twos[2 * i + u] = push(d, 2 * i + u)

    based.wait()

    @pl.loop(0, leaves // 2, unroll=4)
    def _(i):
        for u, d in enumerate(spread(twos[i])):
            leaf = 2 * i + u
            out[:, pl.ds(pl.multiple_of(leaf * 128, 128), 128)] = fold(
                jnp.dot(stack(d), stack(basis[leaf]), preferred_element_type=f32)
            )

    size = mine.shape[1]
    out[:, pl.ds(pl.multiple_of(core[0] * size, size), size)] += mine[...]
    out[:, pl.ds(pl.multiple_of((1 - core[0]) * size, size), size)] += given[...]


def finish_body(
    core, place, codes, partners, three, two, one, level, mine, given,
    moves_hbm, matrices, low, own, high, first, second, trans_hbm, basis_hbm, out,
    moves, block, up, tiles, held, trans, basis, gather, far, ones, twos, sem,
):
    spot = place[0]
    queue = []

    def bring(source, dest):
        copy = pltpu.make_async_copy(source, dest, sem.at[len(queue)])
        copy.start()
        queue.append(copy)
        return copy

    lifted = bring(moves_hbm, moves)
    blocks = []
    width, row = 32, 0
    for i in range(4):
        blocks.append(bring(matrices.at[row + spot // (2 << i)], block.at[i]))
        row, width = row + width, width // 2
    takes = [bring(ref, tiles.at[side]) for side, ref in enumerate((low, own, high))]
    nodes = first.shape[0]
    reads = []
    for i in range(3):
        at = pl.ds(42 * i, nodes - 84 if i == 2 else 42)
        for h, x in enumerate((first, second)):
            reads.append(bring(x.at[at], held.at[h, at]))
    moved = bring(trans_hbm, trans)
    based = bring(basis_hbm, basis)

    def arrived():
        for copy in blocks:
            copy.wait()

    lifted.wait()
    parent = top_chain(place, partners, (three, two, one, level), moves, up, block, arrived)
    couple(codes, far, gather, tiles, held, takes, reads)
    descend(core, parent, far, trans, basis, mine, given, out, ones, twos, moved, based)


def finish(core, place, codes, partners, gathered, mine, given, moves, matrices, low, own, high, first, second, trans, basis):
    leaves, columns, _ = own.shape
    return pl.pallas_call(
        finish_body,
        out_shape=jax.ShapeDtypeStruct((columns, leaves * 128), f32),
        in_specs=[SM] * 4 + [VM] * 6 + [HBM] * 9,
        out_specs=VM,
        scratch_shapes=[
            pltpu.VMEM(moves.shape, f32),
            pltpu.VMEM((4, *matrices.shape[1:]), f32),
            pltpu.VMEM((32, columns, 128), f32),
            pltpu.VMEM((3, leaves, columns, 128), f32),
            pltpu.VMEM((2, *first.shape), bf16),
            pltpu.VMEM(trans.shape, bf16),
            pltpu.VMEM(basis.shape, f32),
            pltpu.VMEM((2, 3 * leaves, 2 * columns, 128), bf16),
            pltpu.VMEM((leaves, columns, 128), f32),
            pltpu.VMEM((leaves // 4, columns, 128), f32),
            pltpu.VMEM((leaves // 2, columns, 128), f32),
            pltpu.SemaphoreType.DMA((16,)),
        ],
        compiler_params=pltpu.CompilerParams(vmem_limit_bytes=VMEM_BYTES),
        cost_estimate=pl.CostEstimate(flops=1_000_000_000, bytes_accessed=20_000_000, transcendentals=0),
        name="finish",
    )(core, place, codes, partners, *gathered, mine, given, moves, matrices, low, own, high, first, second, trans, basis)


near_weight = 0.1
smoothing = 0.0025
PAIR = 2

def near_body(unroll, chunks, core, lists, live, targets, *refs):
    origins, refs = refs[:chunks], refs[chunks:]
    begin = None
    if chunks == 2:
        begin, refs = refs[0:2], refs[2:]
    mine, other, columns_of, total, weights, places, sem, *sources = refs
    leaves = mine.shape[1] // 128
    width = 2 * leaves
    core = core[0]
    side = chunks - 1
    mark = core * leaves
    reads = []
    for i, (origin, source) in enumerate(zip(origins, sources)):
        reads.append(pltpu.make_async_copy(origin, source, sem.at[i]))
        reads[-1].start()
    weights[chunks * width] = jnp.zeros(weights.shape[1:], bf16)
    places[chunks * width] = jnp.zeros(places.shape[1:], f32)
    blank = jnp.zeros((5, 128), f32)

    @pl.loop(0, leaves // 16)
    def _(g):
        rows = []
        for u in range(16):
            at = pl.ds(pl.multiple_of((core * leaves + 16 * g + u) * 128, 128), 128)
            rows += [targets[:, at], blank]
        t = jnp.transpose(jnp.concatenate(rows, axis=0))
        for u in range(16):
            for c in range(3):
                columns_of[16 * g + u, c] = jnp.broadcast_to(t[:, 8 * u + c : 8 * u + c + 1], (128, 128))
            total[16 * g + u] = jnp.zeros((128, 128), f32)

    for read in reads:
        read.wait()

    def load(block, base, turn):
        @pl.loop(0, leaves // 8)
        def _(g):
            for u in range(8):
                j = 8 * g + u
                x = [block[j], block[leaves + j]]
                weights[base + j] = stack(near_weight * jnp.concatenate(x[::-1] if turn else x, axis=0))
                for c in range(3):
                    places[base + j, c : c + 1] = block[2 * leaves + c, pl.ds(j, 1)]

    base = width * core if chunks == 2 else 0
    load(sources[0].at[0], base, False)
    load(sources[0].at[1], base + leaves, False)
    if chunks == 2:
        load(sources[1], width - leaves * core, True)
    items = lax.fori_loop(
        0, leaves, lambda i, s: s + jnp.maximum((live[side, mark + i] + PAIR - 1) // PAIR, 1), jnp.int32(0)
    )

    def block(leaf, slot):
        kernels, parts = [], []
        for u in range(PAIR):
            j = lists[side, slot + u, mark + leaf]
            s = places[j]
            d = columns_of[leaf, 0] - s[0:1]
            squared = d * d + smoothing
            d = columns_of[leaf, 1] - s[1:2]
            squared = squared + d * d
            d = columns_of[leaf, 2] - s[2:3]
            squared = squared + d * d
            kernels += split(lax.rsqrt(squared))
            x = weights[j]
            parts += [x, x]
        return lax.dot_general(
            jnp.concatenate(kernels, axis=1),
            jnp.concatenate(parts, axis=1),
            NT,
            preferred_element_type=f32,
        )

    def step(b, carry):
        leaf, slot = carry
        made = []
        for u in range(unroll):
            place = jnp.where(b * unroll + u < items, leaf, leaves)
            made.append((place, block(leaf, slot)))
            done = slot + PAIR >= live[side, mark + leaf]
            leaf = jnp.where(done, jnp.minimum(leaf + 1, leaves - 1), leaf)
            slot = jnp.where(done, 0, slot + PAIR)
        for place, x in made:
            total[place] += x
        return leaf, slot

    lax.fori_loop(0, (items + unroll - 1) // unroll, step, (jnp.int32(0), jnp.int32(0)))

    @pl.loop(0, leaves, unroll=8)
    def _(leaf):
        at = pl.ds(pl.multiple_of(leaf * 128, 128), 128)
        x = jnp.transpose(both(total[leaf]))
        if begin is None:
            mine[:, at] = x[0:32]
            other[:, at] = x[32:64]
        else:
            mine[:, at] = begin[0][:, at] + x[0:32]
            other[:, at] = begin[1][:, at] + x[32:64]


def near_pass(unroll, core, lists, live, targets, sources, begin=()):
    leaves = lists.shape[2] // 2
    chunks = len(sources)
    held = chunks * 2 * leaves + 1
    side = jax.ShapeDtypeStruct((32, leaves * 128), f32)
    arrays = (targets, *sources, *begin)
    return pl.pallas_call(
        functools.partial(near_body, unroll, chunks),
        out_shape=(side, side),
        in_specs=[SM, SM, SM, VM] + [HBM] * len(sources) + [VM] * len(begin),
        out_specs=(VM, VM),
        scratch_shapes=[
            pltpu.VMEM((leaves, 3, 128, 128), f32),
            pltpu.VMEM((leaves + 1, 128, 128), f32),
            pltpu.VMEM((held, 128, 128), bf16),
            pltpu.VMEM((held, 8, 128), f32),
            pltpu.SemaphoreType.DMA((len(sources),)),
            *[pltpu.VMEM(x.shape, f32) for x in sources],
        ],
        compiler_params=pltpu.CompilerParams(vmem_limit_bytes=VMEM_BYTES),
        cost_estimate=pl.CostEstimate(flops=1_000, bytes_accessed=1_000, transcendentals=0),
        name="near_pass",
    )(core, lists, live, *arrays)


def local(
    points,
    values,
    near_list,
    near_count,
    basis,
    transfer,
    coupling,
    partners,
    transfer_top,
    coupling_top,
    partners_top,
):
    leaves = basis.shape[0]
    position = lax.axis_index("leaf")
    core = lax.axis_index("rhs")
    count = lax.axis_size("leaf")
    forward = [(i, i + 1) for i in range(count - 1)]
    backward = [(target, source) for source, target in forward]
    swap = [(0, 1), (1, 0)]
    across = lax.ppermute(values, "rhs", swap)

    def ring(x, stride):
        spot = (position // stride) % 4
        turned = []
        for shift in range(3, 0, -1):
            to = [(i, i + stride * ((i // stride + shift) % 4 - i // stride % 4)) for i in range(count)]
            turned.append(lax.ppermute(x, "leaf", to))
        return turned, spot

    def in_order(turned, x, spot):
        blocks = [*turned, x]
        ordered = []
        for k in range(4):
            block = blocks[3]
            for j in range(3):
                block = jnp.where(spot == (k - j - 1) % 4, blocks[j], block)
            ordered.append(block)
        return jnp.concatenate(ordered, axis=0)

    after = lax.optimization_barrier
    core = core[None].astype(jnp.int32)
    place = position[None].astype(jnp.int32)
    coupling = coupling.transpose(1, 2, 3, 0)
    first = unbatch(coupling, 0)
    across, first, coupling = after((across, first, coupling))
    packed = pack(points, values, across)
    outward = [(2 * i, 2 * i + 2) for i in range(count - 1)]
    outward += [(2 * i + 3, 2 * i + 1) for i in range(count - 1)]
    beside = lax.ppermute(packed, ("leaf", "rhs"), outward)
    place, packed = after((place, packed))
    up, share, trans, lists, live, codes = up_pass(
        place, near_list.T, near_count[None], partners.T, basis, values, transfer.transpose(1, 2, 0)
    )
    begin = near_pass(12, core, lists, live, points, (packed,))
    share, beside, begin = after((share, beside, begin))
    turned, spot = ring(share[None], 1)
    passed = lax.dynamic_index_in_dim(beside, 1 - core[0], 0, keepdims=False)
    passed = lax.ppermute(passed, "rhs", swap)
    level = in_order(turned, share[None], spot)
    level = jnp.where(jnp.arange(128) < 64, level[0] + level[1], level[2] + level[3])[None]
    turned, spot = ring(level, 4)
    level = in_order(turned, level, spot)
    turned, spot = ring(level, 16)
    turned, passed, up = after((turned, passed, up))
    up_low = lax.ppermute(up, "leaf", forward)
    up_high = lax.ppermute(up, "leaf", backward)
    mine, other = near_pass(12, core, lists, live, points, (beside, passed), begin)
    mine, other, coupling = after((mine, other, coupling))
    given = lax.ppermute(other, "rhs", swap)
    second = unbatch(coupling, 1)
    given, up_low, up_high, second = after((given, up_low, up_high, second))
    return finish(
        core,
        place,
        codes,
        partners_top.T,
        (*turned, level),
        mine,
        given,
        transfer_top,
        coupling_top,
        up_low,
        up,
        up_high,
        first,
        second,
        trans,
        basis,
    )


def solution(mesh):
    placed = (
        P(None, "leaf"),
        P("rhs", "leaf"),
        P("leaf", None),
        P("leaf"),
        P("leaf", None, None),
        P("leaf", None, None),
        P("leaf", None, None, None),
        P("leaf", None),
        P(),
        P(),
        P(),
    )
    return jax.shard_map(
        local, mesh=mesh, in_specs=placed, out_specs=P("rhs", "leaf"), check_vma=False
    )
```

```python
import jax, jax.numpy as jnp, functools
from jax import lax
from jax.sharding import PartitionSpec as P
from jax.experimental import pallas as pl
from jax.experimental.pallas import tpu as pltpu
NT = (((1,), (1,)), ((), ()))
SM = pl.BlockSpec(memory_space=pltpu.SMEM)
VM = pl.BlockSpec(memory_space=pltpu.VMEM)
HBM = pl.BlockSpec(memory_space=pltpu.HBM)
PITCH = 136
VMEM_BYTES = 62 << 20
SLOTS = 28
f32 = jnp.float32
bf16 = jnp.bfloat16

def split(x):
    hi = x.astype(bf16)
    return hi, (x - hi.astype(f32)).astype(bf16)

def stack(x):
    hi, lo = split(x)
    return jnp.concatenate([hi, lo], axis=0)

def fold(x):
    half = x.shape[0] // 2
    return x[:half] + x[half:]

def both(x):
    return x + pltpu.roll(x, 64, 1)

def low_lanes(shape):
    return lax.broadcasted_iota(jnp.int32, shape, 1) < 64

def plan(place, near_list, near_count, partners, lists, live, codes):
    slots, leaves = near_list.shape
    local = near_list[...] - place * leaves
    count = near_count[...]
    inside = (local >= 0) & (local < leaves)
    row = lax.broadcasted_iota(jnp.int32, (SLOTS, leaves), 0)
    for side in range(2):
        rank = jnp.zeros((1, leaves), jnp.int32)
        found = jnp.full((SLOTS, leaves), (1 + side) * leaves, jnp.int32)
        for s in range(slots):
            here = inside[s : s + 1] if side == 0 else jnp.logical_not(inside[s : s + 1])
            picked = here & (s < count)
            ids = local[s : s + 1]
            if side == 1:
                ids = jnp.where(ids < 0, ids + leaves, ids)
            found = jnp.where((row == rank) & picked, ids, found)
            rank = rank + picked.astype(jnp.int32)
        lists[side] = found
        live[side : side + 1] = rank
    nodes = partners.shape[1]
    node = lax.broadcasted_iota(jnp.int32, (1, nodes), 1)
    span = jnp.full((1, nodes), leaves, jnp.int32)
    start = jnp.zeros((1, nodes), jnp.int32)
    width, tile, first = leaves // 2, leaves // 2, leaves
    while width >= 1:
        span = jnp.where(node >= first, width, span)
        start = jnp.where(node >= first, 2 * tile, start)
        tile, first, width = tile + max(1, width // 2), first + width, width // 2
    shifted = partners[...] - place * span
    side = jnp.where(shifted < 0, 0, jnp.where(shifted < span, 1, 2))
    codes[...] = side * (2 * leaves) + start + shifted - (side - 1) * span


def up_body(
    place, near_list, near_count, partners, basis_hbm, values_hbm, moves_hbm,
    up, share, trans_hbm, lists, live, codes, rows, basis, values, moves, trans, sem,
):
    leaves = basis.shape[0]
    columns = values.shape[0]
    nodes = moves.shape[2]
    reads = []
    for i in range(4):
        at = pl.ds(16 * i, 16)
        reads.append(pltpu.make_async_copy(moves_hbm.at[at], moves.at[at], sem.at[i]))
    reads.append(pltpu.make_async_copy(values_hbm, values, sem.at[4]))
    reads.append(pltpu.make_async_copy(basis_hbm, basis, sem.at[5]))
    for read in reads:
        read.start()
    plan(place[0], near_list, near_count, partners, lists, live, codes)
    for i in range(4):
        reads[i].wait()

        @pl.loop(16 * i, 16 * i + 16, unroll=8)
        def _(r):
            block = jnp.transpose(moves[r])
            rows[pl.ds(pl.multiple_of(r * PITCH, 8), nodes)] = jnp.concatenate([block, block], axis=1)

    left = low_lanes((64, 128))

    def node(n):
        x = rows[pl.ds(n, 64, stride=PITCH), :]
        hi = x.astype(bf16).astype(f32)
        trans[n] = jnp.where(left, hi, x - hi).astype(bf16)

    whole = nodes // 8 * 8
    pl.loop(0, whole, unroll=8)(node)
    for n in range(whole, nodes):
        node(n)
    trans[nodes] = jnp.zeros(trans.shape[1:], bf16)
    write = pltpu.make_async_copy(trans, trans_hbm, sem.at[6])
    write.start()

    half = low_lanes((columns, 128))

    for read in reads[4:]:
        read.wait()
    def leaf_up(i):
        v = stack(values[:, pl.ds(pl.multiple_of(i * 128, 128), 128)])
        return both(fold(lax.dot_general(v, stack(basis[i]), NT, preferred_element_type=f32)))

    @pl.loop(0, leaves // 2, unroll=8)
    def _(p):
        up[p] = jnp.where(half, leaf_up(2 * p), leaf_up(2 * p + 1))

    def lift(tile, row):
        t = jnp.concatenate([trans[row], trans[row + 1]], axis=0)
        return both(fold(jnp.dot(stack(tile), t, preferred_element_type=f32)))

    def pair(tile_a, tile_b, row):
        return jnp.where(half, lift(tile_a, row), lift(tile_b, row + 2))

    start, row, width = 0, 0, leaves
    while width > 16:
        after = start + width // 2

        @pl.loop(0, width // 16)
        def _(g, start=start, row=row, after=after):
            made = []
            for p in range(4):
                q = 4 * g + p
                made.append(pair(up[start + 2 * q], up[start + 2 * q + 1], row + 4 * q))
            for p in range(4):
                up[after + 4 * g + p] = made[p]

        start, row, width = after, row + width, width // 2
    tiles = [up[start + p] for p in range(width // 2)]
    while width > 1:
        after = start + width // 2
        if width >= 4:
            tiles = [pair(tiles[2 * p], tiles[2 * p + 1], row + 4 * p) for p in range(width // 4)]
        else:
            tiles = [lift(tiles[0], row)]
        if after < leaves - 1:
            for p, tile in enumerate(tiles):
                up[after + p] = tile
        start, row, width = after, row + width, width // 2
    up[leaves - 1] = tiles[0]
    share[...] = both(fold(jnp.dot(stack(tiles[0])[:, 0:64], trans[row], preferred_element_type=f32)))
    write.wait()


def up_pass(place, near_list, near_count, partners, basis, values, moves):
    leaves = basis.shape[0]
    columns = values.shape[0]
    nodes = moves.shape[2]
    return pl.pallas_call(
        up_body,
        out_shape=(
            jax.ShapeDtypeStruct((leaves, columns, 128), f32),
            jax.ShapeDtypeStruct((columns, 128), f32),
            jax.ShapeDtypeStruct((nodes + 1, 64, 128), bf16),
            jax.ShapeDtypeStruct((2, SLOTS, leaves), jnp.int32),
            jax.ShapeDtypeStruct((2, leaves), jnp.int32),
            jax.ShapeDtypeStruct(partners.shape, jnp.int32),
        ),
        in_specs=[SM, VM, VM, VM, HBM, HBM, HBM],
        out_specs=(VM, VM, HBM, VM, VM, VM),
        scratch_shapes=[
            pltpu.VMEM((64 * PITCH, 128), f32),
            pltpu.VMEM(basis.shape, f32),
            pltpu.VMEM(values.shape, f32),
            pltpu.VMEM(moves.shape, f32),
            pltpu.VMEM((nodes + 1, 64, 128), bf16),
            pltpu.SemaphoreType.DMA((7,)),
        ],
        compiler_params=pltpu.CompilerParams(vmem_limit_bytes=VMEM_BYTES),
        cost_estimate=pl.CostEstimate(flops=400_000_000, bytes_accessed=8_000_000, transcendentals=0),
        name="up_pass",
    )(place, near_list, near_count, partners, basis, values, moves)


CHUNK = 32


def unbatch_body(part, matrices, out, held, rows, made, in_sem, out_sem):
    nodes = matrices.shape[3]
    pieces = 4
    step = matrices.shape[1] // pieces
    reads = []
    for i in range(pieces):
        at = pl.ds(i * step, step)
        reads.append(
            pltpu.make_async_copy(matrices.at[pl.ds(2 * part, 2), at], held.at[:, at], in_sem.at[i])
        )
        reads[-1].start()
    for i in range(pieces):
        reads[i].wait()

        @pl.loop(i * step, (i + 1) * step, unroll=8)
        def _(r):
            x = jnp.concatenate([held[0, r], held[1, r]], axis=0)
            rows[pl.ds(pl.multiple_of(r * PITCH, 8), nodes)] = jnp.transpose(x)

    def one(n):
        hi, lo = split(rows[pl.ds(n, 64, stride=PITCH), :])
        made[n, 0:64] = hi
        made[n, 64:128] = lo

    writes = []
    for c, begin in enumerate(range(0, nodes, CHUNK)):
        size = min(CHUNK, nodes - begin)
        whole = begin + size // 8 * 8
        pl.loop(begin, whole, unroll=8)(one)
        for n in range(whole, begin + size):
            one(n)
        at = pl.ds(begin, size)
        writes.append(pltpu.make_async_copy(made.at[at], out.at[at], out_sem.at[c]))
        writes[-1].start()
    for write in writes:
        write.wait()


def pack_body(points, values_hbm, across_hbm, out_hbm, values, across, packed, sem):
    leaves = values.shape[1] // 128
    block = leaves // 2
    takes = []
    for side in range(2):
        at = pl.ds(side * block * 128, block * 128)
        for k, (source, dest) in enumerate(((values_hbm, values), (across_hbm, across))):
            takes.append(
                pltpu.make_async_copy(source.at[:, at], dest.at[:, at], sem.at[2 * side + k])
            )
            takes[-1].start()
    for c in range(3):
        for j in range(leaves):
            packed[j // block, 2 * block + c, j % block : j % block + 1] = points[
                c : c + 1, 128 * j : 128 * j + 128
            ]
    sends = []
    for side in range(2):
        takes[2 * side].wait()
        takes[2 * side + 1].wait()

        @pl.loop(0, block, unroll=8)
        def _(j, side=side):
            at = pl.ds(pl.multiple_of((side * block + j) * 128, 128), 128)
            packed[side, j] = values[:, at]
            packed[side, block + j] = across[:, at]

        sends.append(pltpu.make_async_copy(packed.at[side], out_hbm.at[side], sem.at[4 + side]))
        sends[-1].start()
    for send in sends:
        send.wait()


def pack(points, values, across):
    columns, width = values.shape
    packed = (2, width // 128 + 3, columns, 128)
    return pl.pallas_call(
        pack_body,
        out_shape=jax.ShapeDtypeStruct(packed, f32),
        in_specs=[VM, HBM, HBM],
        out_specs=HBM,
        scratch_shapes=[
            pltpu.VMEM(values.shape, f32),
            pltpu.VMEM(values.shape, f32),
            pltpu.VMEM(packed, f32),
            pltpu.SemaphoreType.DMA((6,)),
        ],
        compiler_params=pltpu.CompilerParams(vmem_limit_bytes=VMEM_BYTES),
        name="pack",
    )(points, values, across)


def unbatch(matrices, part):
    nodes = matrices.shape[3]
    return pl.pallas_call(
        functools.partial(unbatch_body, part),
        out_shape=jax.ShapeDtypeStruct((nodes, 128, 128), bf16),
        in_specs=[HBM],
        out_specs=HBM,
        scratch_shapes=[
            pltpu.VMEM((2, *matrices.shape[1:]), f32),
            pltpu.VMEM((64 * PITCH, 128), f32),
            pltpu.VMEM((nodes, 128, 128), bf16),
            pltpu.SemaphoreType.DMA((4,)),
            pltpu.SemaphoreType.DMA((-(-nodes // CHUNK),)),
        ],
        compiler_params=pltpu.CompilerParams(vmem_limit_bytes=VMEM_BYTES),
        cost_estimate=pl.CostEstimate(flops=1_000, bytes_accessed=1_000, transcendentals=0),
        name="unbatch",
    )(matrices)


def top_chain(place, partners, gathered, moves, up, block, arrived):
    spot = place[0]
    columns = gathered[0].shape[1]
    half = low_lanes((columns, 128))
    for j, ref in enumerate(gathered):
        up[pl.ds(4 * ((spot // 16 + 1 + j) % 4), 4)] = ref[...]
    def lift(tile, r):
        t = jnp.concatenate([moves[r], moves[r + 1]], axis=0)
        hi, lo = split(t)
        x = stack(up[tile])
        z = fold(jnp.dot(x, hi, preferred_element_type=f32)) + jnp.dot(x[:columns], lo, preferred_element_type=f32)
        return jnp.concatenate([z, z], axis=1)
    tile0, row, width = 0, 0, 32
    tiles, rows = [], []
    while width >= 4:
        tiles.append(tile0)
        rows.append(row)
        nxt = tile0 + width // 2
        if width > 4:
            for p in range(width // 4):
                up[nxt + p] = jnp.where(half, lift(tile0 + 2 * p, row + 4 * p), lift(tile0 + 2 * p + 1, row + 4 * p + 2))
        tile0, row, width = nxt, row + width, width // 2
    def push(d, r):
        hi, lo = split(moves[r])
        x = stack(d)
        return fold(lax.dot_general(x, hi, NT, preferred_element_type=f32)) + lax.dot_general(x[:columns], lo, NT, preferred_element_type=f32)
    arrived()
    fars = []
    for level in range(4):
        index = rows[level] + spot // (2 << level)
        far = jnp.zeros((columns, 64), f32)
        for k in range(4):
            p = partners[k, index]
            tile = up[tiles[level] + p // 2]
            x = stack(jnp.where(p % 2 == 0, tile, pltpu.roll(tile, 64, 1))[:, 0:64])
            hi, lo = split(block[level, k])
            far = far + fold(lax.dot_general(x, hi, NT, preferred_element_type=f32))
            far = far + lax.dot_general(x[:columns], lo, NT, preferred_element_type=f32)
        fars.append(far)
    down = jnp.zeros((columns, 64), f32)
    down = push(down, row + spot // 32)
    for level in range(3, -1, -1):
        down = push(down, rows[level] + spot // (2 << level)) + fars[level]
    return jnp.concatenate([down, down], axis=1)


def couple(codes, far, gather, tiles, held, takes, reads):
    _, leaves, columns, _ = tiles.shape
    nodes = held.shape[1]
    half = low_lanes((columns, 128))
    left = low_lanes((2 * columns, 128))
    for side in range(3):
        takes[side].wait()

        @pl.loop(0, leaves, unroll=16)
        def _(t, side=side):
            x = tiles[side, t]
            gather[0, side * leaves + t] = stack(x)
            gather[1, side * leaves + t] = stack(pltpu.roll(x, 64, 1))

    def pick(n, k, side):
        code = codes[k, n]
        return gather[(code & 1) ^ side, code >> 1]

    def one(n):
        x = jnp.concatenate(
            [
                jnp.where(left, pick(n, 0, 0), pick(n, 1, 1)),
                jnp.where(left, pick(n, 2, 0), pick(n, 3, 1)),
            ],
            axis=1,
        )
        m = jnp.concatenate([held[0, n], held[1, n]], axis=1)
        return both(fold(lax.dot_general(x, m, NT, preferred_element_type=f32)))

    for i in range(3):
        reads[2 * i].wait()
        reads[2 * i + 1].wait()

        @pl.loop(21 * i, 21 * i + 21, unroll=7)
        def _(t):
            far[t] = jnp.where(half, one(2 * t), one(2 * t + 1))

    far[leaves - 1] = one(nodes - 1)


def descend(core, parent, far, trans, basis, mine, given, out, ones, twos, moved, based):
    leaves = basis.shape[0]
    columns = out.shape[0]
    half = low_lanes((columns, 128))

    def push(d, tile):
        t = jnp.concatenate([trans[2 * tile], trans[2 * tile + 1]], axis=0)
        return fold(lax.dot_general(stack(d), t, NT, preferred_element_type=f32)) + far[tile]

    def spread(tile):
        turned = pltpu.roll(tile, 64, 1)
        return jnp.where(half, tile, turned), jnp.where(half, turned, tile)

    last = leaves - 1
    above = stack(parent)
    moved.wait()
    t = trans[2 * last]
    t = jnp.concatenate([t, t], axis=0)
    sources = [fold(lax.dot_general(above, t, NT, preferred_element_type=f32)) + far[last]]
    start, width = last, 1
    while width < 16:
        start = start - width
        made = [push(d, start + i) for i, d in enumerate(sources)]
        sources = [d for tile in made for d in spread(tile)]
        width = 2 * width
    start = start - width
    for i, d in enumerate(sources):
        ones[i] = push(d, start + i)

    @pl.loop(0, width, unroll=8)
    def _(i):
        for u, d in enumerate(spread(ones[i])):
            twos[2 * i + u] = push(d, 2 * i + u)

    based.wait()

    @pl.loop(0, leaves // 2, unroll=4)
    def _(i):
        for u, d in enumerate(spread(twos[i])):
            leaf = 2 * i + u
            out[:, pl.ds(pl.multiple_of(leaf * 128, 128), 128)] = fold(
                jnp.dot(stack(d), stack(basis[leaf]), preferred_element_type=f32)
            )

    size = mine.shape[1]
    out[:, pl.ds(pl.multiple_of(core[0] * size, size), size)] += mine[...]
    out[:, pl.ds(pl.multiple_of((1 - core[0]) * size, size), size)] += given[...]


def finish_body(
    core, place, codes, partners, three, two, one, level, mine, given,
    moves_hbm, matrices, low, own, high, first, second, trans_hbm, basis_hbm, out,
    moves, block, up, tiles, held, trans, basis, gather, far, ones, twos, sem,
):
    spot = place[0]
    queue = []

    def bring(source, dest):
        copy = pltpu.make_async_copy(source, dest, sem.at[len(queue)])
        copy.start()
        queue.append(copy)
        return copy

    lifted = bring(moves_hbm, moves)
    blocks = []
    width, row = 32, 0
    for i in range(4):
        blocks.append(bring(matrices.at[row + spot // (2 << i)], block.at[i]))
        row, width = row + width, width // 2
    takes = [bring(ref, tiles.at[side]) for side, ref in enumerate((low, own, high))]
    nodes = first.shape[0]
    reads = []
    for i in range(3):
        at = pl.ds(42 * i, nodes - 84 if i == 2 else 42)
        for h, x in enumerate((first, second)):
            reads.append(bring(x.at[at], held.at[h, at]))
    moved = bring(trans_hbm, trans)
    based = bring(basis_hbm, basis)

    def arrived():
        for copy in blocks:
            copy.wait()

    lifted.wait()
    parent = top_chain(place, partners, (three, two, one, level), moves, up, block, arrived)
    couple(codes, far, gather, tiles, held, takes, reads)
    descend(core, parent, far, trans, basis, mine, given, out, ones, twos, moved, based)


def finish(core, place, codes, partners, gathered, mine, given, moves, matrices, low, own, high, first, second, trans, basis):
    leaves, columns, _ = own.shape
    return pl.pallas_call(
        finish_body,
        out_shape=jax.ShapeDtypeStruct((columns, leaves * 128), f32),
        in_specs=[SM] * 4 + [VM] * 6 + [HBM] * 9,
        out_specs=VM,
        scratch_shapes=[
            pltpu.VMEM(moves.shape, f32),
            pltpu.VMEM((4, *matrices.shape[1:]), f32),
            pltpu.VMEM((32, columns, 128), f32),
            pltpu.VMEM((3, leaves, columns, 128), f32),
            pltpu.VMEM((2, *first.shape), bf16),
            pltpu.VMEM(trans.shape, bf16),
            pltpu.VMEM(basis.shape, f32),
            pltpu.VMEM((2, 3 * leaves, 2 * columns, 128), bf16),
            pltpu.VMEM((leaves, columns, 128), f32),
            pltpu.VMEM((leaves // 4, columns, 128), f32),
            pltpu.VMEM((leaves // 2, columns, 128), f32),
            pltpu.SemaphoreType.DMA((16,)),
        ],
        compiler_params=pltpu.CompilerParams(vmem_limit_bytes=VMEM_BYTES),
        cost_estimate=pl.CostEstimate(flops=1_000_000_000, bytes_accessed=20_000_000, transcendentals=0),
        name="finish",
    )(core, place, codes, partners, *gathered, mine, given, moves, matrices, low, own, high, first, second, trans, basis)


near_weight = 0.1
smoothing = 0.0025
PAIR = 2

def near_body(unroll, chunks, core, lists, live, targets, *refs):
    origins, refs = refs[:chunks], refs[chunks:]
    begin = None
    if chunks == 2:
        begin, refs = refs[0:2], refs[2:]
    mine, other, columns_of, total, weights, places, sem, *sources = refs
    leaves = mine.shape[1] // 128
    width = 2 * leaves
    core = core[0]
    side = chunks - 1
    mark = core * leaves
    reads = []
    for i, (origin, source) in enumerate(zip(origins, sources)):
        reads.append(pltpu.make_async_copy(origin, source, sem.at[i]))
        reads[-1].start()
    weights[chunks * width] = jnp.zeros(weights.shape[1:], bf16)
    places[chunks * width] = jnp.zeros(places.shape[1:], f32)
    blank = jnp.zeros((5, 128), f32)

    @pl.loop(0, leaves // 16)
    def _(g):
        rows = []
        for u in range(16):
            at = pl.ds(pl.multiple_of((core * leaves + 16 * g + u) * 128, 128), 128)
            rows += [targets[:, at], blank]
        t = jnp.transpose(jnp.concatenate(rows, axis=0))
        for u in range(16):
            for c in range(3):
                columns_of[16 * g + u, c] = jnp.broadcast_to(t[:, 8 * u + c : 8 * u + c + 1], (128, 128))
            total[16 * g + u] = jnp.zeros((128, 128), f32)

    for read in reads:
        read.wait()

    def load(block, base, turn):
        @pl.loop(0, leaves // 8)
        def _(g):
            for u in range(8):
                j = 8 * g + u
                x = [block[j], block[leaves + j]]
                weights[base + j] = stack(near_weight * jnp.concatenate(x[::-1] if turn else x, axis=0))
                for c in range(3):
                    places[base + j, c : c + 1] = block[2 * leaves + c, pl.ds(j, 1)]

    base = width * core if chunks == 2 else 0
    load(sources[0].at[0], base, False)
    load(sources[0].at[1], base + leaves, False)
    if chunks == 2:
        load(sources[1], width - leaves * core, True)
    items = lax.fori_loop(
        0, leaves, lambda i, s: s + jnp.maximum((live[side, mark + i] + PAIR - 1) // PAIR, 1), jnp.int32(0)
    )

    def block(leaf, slot):
        kernels, parts = [], []
        for u in range(PAIR):
            j = lists[side, slot + u, mark + leaf]
            s = places[j]
            d = columns_of[leaf, 0] - s[0:1]
            squared = d * d + smoothing
            d = columns_of[leaf, 1] - s[1:2]
            squared = squared + d * d
            d = columns_of[leaf, 2] - s[2:3]
            squared = squared + d * d
            kernels += split(lax.rsqrt(squared))
            x = weights[j]
            parts += [x, x]
        return lax.dot_general(
            jnp.concatenate(kernels, axis=1),
            jnp.concatenate(parts, axis=1),
            NT,
            preferred_element_type=f32,
        )

    def step(b, carry):
        leaf, slot = carry
        made = []
        for u in range(unroll):
            place = jnp.where(b * unroll + u < items, leaf, leaves)
            made.append((place, block(leaf, slot)))
            done = slot + PAIR >= live[side, mark + leaf]
            leaf = jnp.where(done, jnp.minimum(leaf + 1, leaves - 1), leaf)
            slot = jnp.where(done, 0, slot + PAIR)
        for place, x in made:
            total[place] += x
        return leaf, slot

    lax.fori_loop(0, (items + unroll - 1) // unroll, step, (jnp.int32(0), jnp.int32(0)))

    @pl.loop(0, leaves, unroll=8)
    def _(leaf):
        at = pl.ds(pl.multiple_of(leaf * 128, 128), 128)
        x = jnp.transpose(both(total[leaf]))
        if begin is None:
            mine[:, at] = x[0:32]
            other[:, at] = x[32:64]
        else:
            mine[:, at] = begin[0][:, at] + x[0:32]
            other[:, at] = begin[1][:, at] + x[32:64]


def near_pass(unroll, core, lists, live, targets, sources, begin=()):
    leaves = lists.shape[2] // 2
    chunks = len(sources)
    held = chunks * 2 * leaves + 1
    side = jax.ShapeDtypeStruct((32, leaves * 128), f32)
    arrays = (targets, *sources, *begin)
    return pl.pallas_call(
        functools.partial(near_body, unroll, chunks),
        out_shape=(side, side),
        in_specs=[SM, SM, SM, VM] + [HBM] * len(sources) + [VM] * len(begin),
        out_specs=(VM, VM),
        scratch_shapes=[
            pltpu.VMEM((leaves, 3, 128, 128), f32),
            pltpu.VMEM((leaves + 1, 128, 128), f32),
            pltpu.VMEM((held, 128, 128), bf16),
            pltpu.VMEM((held, 8, 128), f32),
            pltpu.SemaphoreType.DMA((len(sources),)),
            *[pltpu.VMEM(x.shape, f32) for x in sources],
        ],
        compiler_params=pltpu.CompilerParams(vmem_limit_bytes=VMEM_BYTES),
        cost_estimate=pl.CostEstimate(flops=1_000, bytes_accessed=1_000, transcendentals=0),
        name="near_pass",
    )(core, lists, live, *arrays)


def local(
    points,
    values,
    near_list,
    near_count,
    basis,
    transfer,
    coupling,
    partners,
    transfer_top,
    coupling_top,
    partners_top,
):
    leaves = basis.shape[0]
    position = lax.axis_index("leaf")
    core = lax.axis_index("rhs")
    count = lax.axis_size("leaf")
    forward = [(i, i + 1) for i in range(count - 1)]
    backward = [(target, source) for source, target in forward]
    swap = [(0, 1), (1, 0)]
    across = lax.ppermute(values, "rhs", swap)

    def ring(x, stride):
        spot = (position // stride) % 4
        turned = []
        for shift in range(3, 0, -1):
            to = [(i, i + stride * ((i // stride + shift) % 4 - i // stride % 4)) for i in range(count)]
            turned.append(lax.ppermute(x, "leaf", to))
        return turned, spot

    def in_order(turned, x, spot):
        blocks = [*turned, x]
        ordered = []
        for k in range(4):
            block = blocks[3]
            for j in range(3):
                block = jnp.where(spot == (k - j - 1) % 4, blocks[j], block)
            ordered.append(block)
        return jnp.concatenate(ordered, axis=0)

    after = lax.optimization_barrier
    core = core[None].astype(jnp.int32)
    place = position[None].astype(jnp.int32)
    coupling = coupling.transpose(1, 2, 3, 0)
    first = unbatch(coupling, 0)
    across, first, coupling = after((across, first, coupling))
    packed = pack(points, values, across)
    outward = [(2 * i, 2 * i + 2) for i in range(count - 1)]
    outward += [(2 * i + 3, 2 * i + 1) for i in range(count - 1)]
    beside = lax.ppermute(packed, ("leaf", "rhs"), outward)
    place, packed = after((place, packed))
    up, share, trans, lists, live, codes = up_pass(
        place, near_list.T, near_count[None], partners.T, basis, values, transfer.transpose(1, 2, 0)
    )
    begin = near_pass(12, core, lists, live, points, (packed,))
    share, beside, begin = after((share, beside, begin))
    turned, spot = ring(share[None], 1)
    passed = lax.dynamic_index_in_dim(beside, 1 - core[0], 0, keepdims=False)
    passed = lax.ppermute(passed, "rhs", swap)
    level = in_order(turned, share[None], spot)
    level = jnp.where(jnp.arange(128) < 64, level[0] + level[1], level[2] + level[3])[None]
    turned, spot = ring(level, 4)
    turned, passed, up = after((turned, passed, up))
    level = in_order(turned, level, spot)
    up_low = lax.ppermute(up, "leaf", forward)
    up_high = lax.ppermute(up, "leaf", backward)
    mine, other = near_pass(12, core, lists, live, points, (beside, passed), begin)
    level, mine, other, coupling = after((level, mine, other, coupling))
    turned, spot = ring(level, 16)
    given = lax.ppermute(other, "rhs", swap)
    second = unbatch(coupling, 1)
    turned, given, up_low, up_high, second = after((turned, given, up_low, up_high, second))
    return finish(
        core,
        place,
        codes,
        partners_top.T,
        (*turned, level),
        mine,
        given,
        transfer_top,
        coupling_top,
        up_low,
        up,
        up_high,
        first,
        second,
        trans,
        basis,
    )


def solution(mesh):
    placed = (
        P(None, "leaf"),
        P("rhs", "leaf"),
        P("leaf", None),
        P("leaf"),
        P("leaf", None, None),
        P("leaf", None, None),
        P("leaf", None, None, None),
        P("leaf", None),
        P(),
        P(),
        P(),
    )
    return jax.shard_map(
        local, mesh=mesh, in_specs=placed, out_specs=P("rhs", "leaf"), check_vma=False
    )
```

```python
import jax, jax.numpy as jnp, functools
from jax import lax
from jax.sharding import PartitionSpec as P
from jax.experimental import pallas as pl
from jax.experimental.pallas import tpu as pltpu
NT = (((1,), (1,)), ((), ()))
SM = pl.BlockSpec(memory_space=pltpu.SMEM)
VM = pl.BlockSpec(memory_space=pltpu.VMEM)
HBM = pl.BlockSpec(memory_space=pltpu.HBM)
PITCH = 136
VMEM_BYTES = 62 << 20
SLOTS = 28
f32 = jnp.float32
bf16 = jnp.bfloat16

def split(x):
    hi = x.astype(bf16)
    return hi, (x - hi.astype(f32)).astype(bf16)

def stack(x):
    hi, lo = split(x)
    return jnp.concatenate([hi, lo], axis=0)

def fold(x):
    half = x.shape[0] // 2
    return x[:half] + x[half:]

def both(x):
    return x + pltpu.roll(x, 64, 1)

def low_lanes(shape):
    return lax.broadcasted_iota(jnp.int32, shape, 1) < 64

def plan(place, near_list, near_count, partners, lists, live, codes):
    slots, leaves = near_list.shape
    local = near_list[...] - place * leaves
    count = near_count[...]
    inside = (local >= 0) & (local < leaves)
    row = lax.broadcasted_iota(jnp.int32, (SLOTS, leaves), 0)
    for side in range(2):
        rank = jnp.zeros((1, leaves), jnp.int32)
        found = jnp.full((SLOTS, leaves), (1 + side) * leaves, jnp.int32)
        for s in range(slots):
            here = inside[s : s + 1] if side == 0 else jnp.logical_not(inside[s : s + 1])
            picked = here & (s < count)
            ids = local[s : s + 1]
            if side == 1:
                ids = jnp.where(ids < 0, ids + leaves, ids)
            found = jnp.where((row == rank) & picked, ids, found)
            rank = rank + picked.astype(jnp.int32)
        lists[side] = found
        live[side : side + 1] = rank
    nodes = partners.shape[1]
    node = lax.broadcasted_iota(jnp.int32, (1, nodes), 1)
    span = jnp.full((1, nodes), leaves, jnp.int32)
    start = jnp.zeros((1, nodes), jnp.int32)
    width, tile, first = leaves // 2, leaves // 2, leaves
    while width >= 1:
        span = jnp.where(node >= first, width, span)
        start = jnp.where(node >= first, 2 * tile, start)
        tile, first, width = tile + max(1, width // 2), first + width, width // 2
    shifted = partners[...] - place * span
    side = jnp.where(shifted < 0, 0, jnp.where(shifted < span, 1, 2))
    codes[...] = side * (2 * leaves) + start + shifted - (side - 1) * span


def up_body(
    place, near_list, near_count, partners, basis_hbm, values_hbm, moves_hbm,
    up, share, trans_hbm, lists, live, codes, rows, basis, values, moves, trans, sem,
):
    leaves = basis.shape[0]
    columns = values.shape[0]
    nodes = moves.shape[2]
    reads = []
    for i in range(4):
        at = pl.ds(16 * i, 16)
        reads.append(pltpu.make_async_copy(moves_hbm.at[at], moves.at[at], sem.at[i]))
    reads.append(pltpu.make_async_copy(values_hbm, values, sem.at[4]))
    reads.append(pltpu.make_async_copy(basis_hbm, basis, sem.at[5]))
    for read in reads:
        read.start()
    plan(place[0], near_list, near_count, partners, lists, live, codes)
    for i in range(4):
        reads[i].wait()

        @pl.loop(16 * i, 16 * i + 16, unroll=8)
        def _(r):
            block = jnp.transpose(moves[r])
            rows[pl.ds(pl.multiple_of(r * PITCH, 8), nodes)] = jnp.concatenate([block, block], axis=1)

    left = low_lanes((64, 128))

    def node(n):
        x = rows[pl.ds(n, 64, stride=PITCH), :]
        hi = x.astype(bf16).astype(f32)
        trans[n] = jnp.where(left, hi, x - hi).astype(bf16)

    whole = nodes // 8 * 8
    pl.loop(0, whole, unroll=8)(node)
    for n in range(whole, nodes):
        node(n)
    trans[nodes] = jnp.zeros(trans.shape[1:], bf16)
    write = pltpu.make_async_copy(trans, trans_hbm, sem.at[6])
    write.start()

    half = low_lanes((columns, 128))

    for read in reads[4:]:
        read.wait()
    def leaf_up(i):
        v = stack(values[:, pl.ds(pl.multiple_of(i * 128, 128), 128)])
        return both(fold(lax.dot_general(v, stack(basis[i]), NT, preferred_element_type=f32)))

    @pl.loop(0, leaves // 2, unroll=8)
    def _(p):
        up[p] = jnp.where(half, leaf_up(2 * p), leaf_up(2 * p + 1))

    def lift(tile, row):
        t = jnp.concatenate([trans[row], trans[row + 1]], axis=0)
        return both(fold(jnp.dot(stack(tile), t, preferred_element_type=f32)))

    def pair(tile_a, tile_b, row):
        return jnp.where(half, lift(tile_a, row), lift(tile_b, row + 2))

    start, row, width = 0, 0, leaves
    while width > 16:
        after = start + width // 2

        @pl.loop(0, width // 16)
        def _(g, start=start, row=row, after=after):
            made = []
            for p in range(4):
                q = 4 * g + p
                made.append(pair(up[start + 2 * q], up[start + 2 * q + 1], row + 4 * q))
            for p in range(4):
                up[after + 4 * g + p] = made[p]

        start, row, width = after, row + width, width // 2
    tiles = [up[start + p] for p in range(width // 2)]
    while width > 1:
        after = start + width // 2
        if width >= 4:
            tiles = [pair(tiles[2 * p], tiles[2 * p + 1], row + 4 * p) for p in range(width // 4)]
        else:
            tiles = [lift(tiles[0], row)]
        if after < leaves - 1:
            for p, tile in enumerate(tiles):
                up[after + p] = tile
        start, row, width = after, row + width, width // 2
    up[leaves - 1] = tiles[0]
    share[...] = both(fold(jnp.dot(stack(tiles[0])[:, 0:64], trans[row], preferred_element_type=f32)))
    write.wait()


def up_pass(place, near_list, near_count, partners, basis, values, moves):
    leaves = basis.shape[0]
    columns = values.shape[0]
    nodes = moves.shape[2]
    return pl.pallas_call(
        up_body,
        out_shape=(
            jax.ShapeDtypeStruct((leaves, columns, 128), f32),
            jax.ShapeDtypeStruct((columns, 128), f32),
            jax.ShapeDtypeStruct((nodes + 1, 64, 128), bf16),
            jax.ShapeDtypeStruct((2, SLOTS, leaves), jnp.int32),
            jax.ShapeDtypeStruct((2, leaves), jnp.int32),
            jax.ShapeDtypeStruct(partners.shape, jnp.int32),
        ),
        in_specs=[SM, VM, VM, VM, HBM, HBM, HBM],
        out_specs=(VM, VM, HBM, VM, VM, VM),
        scratch_shapes=[
            pltpu.VMEM((64 * PITCH, 128), f32),
            pltpu.VMEM(basis.shape, f32),
            pltpu.VMEM(values.shape, f32),
            pltpu.VMEM(moves.shape, f32),
            pltpu.VMEM((nodes + 1, 64, 128), bf16),
            pltpu.SemaphoreType.DMA((7,)),
        ],
        compiler_params=pltpu.CompilerParams(vmem_limit_bytes=VMEM_BYTES),
        cost_estimate=pl.CostEstimate(flops=400_000_000, bytes_accessed=8_000_000, transcendentals=0),
        name="up_pass",
    )(place, near_list, near_count, partners, basis, values, moves)


CHUNK = 32


def unbatch_body(part, matrices, out, held, rows, made, in_sem, out_sem):
    nodes = matrices.shape[3]
    pieces = 4
    step = matrices.shape[1] // pieces
    reads = []
    for i in range(pieces):
        at = pl.ds(i * step, step)
        reads.append(
            pltpu.make_async_copy(matrices.at[pl.ds(2 * part, 2), at], held.at[:, at], in_sem.at[i])
        )
        reads[-1].start()
    for i in range(pieces):
        reads[i].wait()

        @pl.loop(i * step, (i + 1) * step, unroll=8)
        def _(r):
            x = jnp.concatenate([held[0, r], held[1, r]], axis=0)
            rows[pl.ds(pl.multiple_of(r * PITCH, 8), nodes)] = jnp.transpose(x)

    def one(n):
        hi, lo = split(rows[pl.ds(n, 64, stride=PITCH), :])
        made[n, 0:64] = hi
        made[n, 64:128] = lo

    writes = []
    for c, begin in enumerate(range(0, nodes, CHUNK)):
        size = min(CHUNK, nodes - begin)
        whole = begin + size // 8 * 8
        pl.loop(begin, whole, unroll=8)(one)
        for n in range(whole, begin + size):
            one(n)
        at = pl.ds(begin, size)
        writes.append(pltpu.make_async_copy(made.at[at], out.at[at], out_sem.at[c]))
        writes[-1].start()
    for write in writes:
        write.wait()


def pack_body(points, values_hbm, across_hbm, out_hbm, values, across, packed, sem):
    leaves = values.shape[1] // 128
    block = leaves // 2
    takes = []
    for side in range(2):
        at = pl.ds(side * block * 128, block * 128)
        for k, (source, dest) in enumerate(((values_hbm, values), (across_hbm, across))):
            takes.append(
                pltpu.make_async_copy(source.at[:, at], dest.at[:, at], sem.at[2 * side + k])
            )
            takes[-1].start()
    for c in range(3):
        for j in range(leaves):
            packed[j // block, 2 * block + c, j % block : j % block + 1] = points[
                c : c + 1, 128 * j : 128 * j + 128
            ]
    sends = []
    for side in range(2):
        takes[2 * side].wait()
        takes[2 * side + 1].wait()

        @pl.loop(0, block, unroll=8)
        def _(j, side=side):
            at = pl.ds(pl.multiple_of((side * block + j) * 128, 128), 128)
            packed[side, j] = values[:, at]
            packed[side, block + j] = across[:, at]

        sends.append(pltpu.make_async_copy(packed.at[side], out_hbm.at[side], sem.at[4 + side]))
        sends[-1].start()
    for send in sends:
        send.wait()


def pack(points, values, across):
    columns, width = values.shape
    packed = (2, width // 128 + 3, columns, 128)
    return pl.pallas_call(
        pack_body,
        out_shape=jax.ShapeDtypeStruct(packed, f32),
        in_specs=[VM, HBM, HBM],
        out_specs=HBM,
        scratch_shapes=[
            pltpu.VMEM(values.shape, f32),
            pltpu.VMEM(values.shape, f32),
            pltpu.VMEM(packed, f32),
            pltpu.SemaphoreType.DMA((6,)),
        ],
        compiler_params=pltpu.CompilerParams(vmem_limit_bytes=VMEM_BYTES),
        name="pack",
    )(points, values, across)


def unbatch(matrices, part):
    nodes = matrices.shape[3]
    return pl.pallas_call(
        functools.partial(unbatch_body, part),
        out_shape=jax.ShapeDtypeStruct((nodes, 128, 128), bf16),
        in_specs=[HBM],
        out_specs=HBM,
        scratch_shapes=[
            pltpu.VMEM((2, *matrices.shape[1:]), f32),
            pltpu.VMEM((64 * PITCH, 128), f32),
            pltpu.VMEM((nodes, 128, 128), bf16),
            pltpu.SemaphoreType.DMA((4,)),
            pltpu.SemaphoreType.DMA((-(-nodes // CHUNK),)),
        ],
        compiler_params=pltpu.CompilerParams(vmem_limit_bytes=VMEM_BYTES),
        cost_estimate=pl.CostEstimate(flops=1_000, bytes_accessed=1_000, transcendentals=0),
        name="unbatch",
    )(matrices)


def top_chain(place, partners, gathered, moves, up, block, arrived):
    spot = place[0]
    columns = gathered[0].shape[1]
    half = low_lanes((columns, 128))
    for j, ref in enumerate(gathered):
        up[pl.ds(4 * ((spot // 16 + 1 + j) % 4), 4)] = ref[...]
    def lift(tile, r):
        t = jnp.concatenate([moves[r], moves[r + 1]], axis=0)
        hi, lo = split(t)
        x = stack(up[tile])
        z = fold(jnp.dot(x, hi, preferred_element_type=f32)) + jnp.dot(x[:columns], lo, preferred_element_type=f32)
        return jnp.concatenate([z, z], axis=1)
    tile0, row, width = 0, 0, 32
    tiles, rows = [], []
    while width >= 4:
        tiles.append(tile0)
        rows.append(row)
        nxt = tile0 + width // 2
        if width > 4:
            for p in range(width // 4):
                up[nxt + p] = jnp.where(half, lift(tile0 + 2 * p, row + 4 * p), lift(tile0 + 2 * p + 1, row + 4 * p + 2))
        tile0, row, width = nxt, row + width, width // 2
    def push(d, r):
        hi, lo = split(moves[r])
        x = stack(d)
        return fold(lax.dot_general(x, hi, NT, preferred_element_type=f32)) + lax.dot_general(x[:columns], lo, NT, preferred_element_type=f32)
    arrived()
    fars = []
    for level in range(4):
        index = rows[level] + spot // (2 << level)
        far = jnp.zeros((columns, 64), f32)
        for k in range(4):
            p = partners[k, index]
            tile = up[tiles[level] + p // 2]
            x = stack(jnp.where(p % 2 == 0, tile, pltpu.roll(tile, 64, 1))[:, 0:64])
            hi, lo = split(block[level, k])
            far = far + fold(lax.dot_general(x, hi, NT, preferred_element_type=f32))
            far = far + lax.dot_general(x[:columns], lo, NT, preferred_element_type=f32)
        fars.append(far)
    down = jnp.zeros((columns, 64), f32)
    down = push(down, row + spot // 32)
    for level in range(3, -1, -1):
        down = push(down, rows[level] + spot // (2 << level)) + fars[level]
    return jnp.concatenate([down, down], axis=1)


def couple(codes, far, gather, tiles, held, takes, reads):
    _, leaves, columns, _ = tiles.shape
    nodes = held.shape[1]
    half = low_lanes((columns, 128))
    left = low_lanes((2 * columns, 128))
    for side in range(3):
        takes[side].wait()

        @pl.loop(0, leaves, unroll=16)
        def _(t, side=side):
            x = tiles[side, t]
            gather[0, side * leaves + t] = stack(x)
            gather[1, side * leaves + t] = stack(pltpu.roll(x, 64, 1))

    def pick(n, k, side):
        code = codes[k, n]
        return gather[(code & 1) ^ side, code >> 1]

    def one(n):
        x = jnp.concatenate(
            [
                jnp.where(left, pick(n, 0, 0), pick(n, 1, 1)),
                jnp.where(left, pick(n, 2, 0), pick(n, 3, 1)),
            ],
            axis=1,
        )
        m = jnp.concatenate([held[0, n], held[1, n]], axis=1)
        return both(fold(lax.dot_general(x, m, NT, preferred_element_type=f32)))

    for i in range(3):
        reads[2 * i].wait()
        reads[2 * i + 1].wait()

        @pl.loop(21 * i, 21 * i + 21, unroll=7)
        def _(t):
            far[t] = jnp.where(half, one(2 * t), one(2 * t + 1))

    far[leaves - 1] = one(nodes - 1)


def descend(core, parent, far, trans, basis, mine, given, out, ones, twos, moved, based):
    leaves = basis.shape[0]
    columns = out.shape[0]
    half = low_lanes((columns, 128))

    def push(d, tile):
        t = jnp.concatenate([trans[2 * tile], trans[2 * tile + 1]], axis=0)
        return fold(lax.dot_general(stack(d), t, NT, preferred_element_type=f32)) + far[tile]

    def spread(tile):
        turned = pltpu.roll(tile, 64, 1)
        return jnp.where(half, tile, turned), jnp.where(half, turned, tile)

    last = leaves - 1
    above = stack(parent)
    moved.wait()
    t = trans[2 * last]
    t = jnp.concatenate([t, t], axis=0)
    sources = [fold(lax.dot_general(above, t, NT, preferred_element_type=f32)) + far[last]]
    start, width = last, 1
    while width < 16:
        start = start - width
        made = [push(d, start + i) for i, d in enumerate(sources)]
        sources = [d for tile in made for d in spread(tile)]
        width = 2 * width
    start = start - width
    for i, d in enumerate(sources):
        ones[i] = push(d, start + i)

    @pl.loop(0, width, unroll=8)
    def _(i):
        for u, d in enumerate(spread(ones[i])):
            twos[2 * i + u] = push(d, 2 * i + u)

    based.wait()

    @pl.loop(0, leaves // 2, unroll=4)
    def _(i):
        for u, d in enumerate(spread(twos[i])):
            leaf = 2 * i + u
            out[:, pl.ds(pl.multiple_of(leaf * 128, 128), 128)] = fold(
                jnp.dot(stack(d), stack(basis[leaf]), preferred_element_type=f32)
            )

    size = mine.shape[1]
    out[:, pl.ds(pl.multiple_of(core[0] * size, size), size)] += mine[...]
    out[:, pl.ds(pl.multiple_of((1 - core[0]) * size, size), size)] += given[...]


def finish_body(
    core, place, codes, partners, three, two, one, level, mine, given,
    moves_hbm, matrices, low, own, high, first, second, trans_hbm, basis_hbm, out,
    moves, block, up, tiles, held, trans, basis, gather, far, ones, twos, sem,
):
    spot = place[0]
    queue = []

    def bring(source, dest):
        copy = pltpu.make_async_copy(source, dest, sem.at[len(queue)])
        copy.start()
        queue.append(copy)
        return copy

    lifted = bring(moves_hbm, moves)
    blocks = []
    width, row = 32, 0
    for i in range(4):
        blocks.append(bring(matrices.at[row + spot // (2 << i)], block.at[i]))
        row, width = row + width, width // 2
    takes = [bring(ref, tiles.at[side]) for side, ref in enumerate((low, own, high))]
    nodes = first.shape[0]
    reads = []
    for i in range(3):
        at = pl.ds(42 * i, nodes - 84 if i == 2 else 42)
        for h, x in enumerate((first, second)):
            reads.append(bring(x.at[at], held.at[h, at]))
    moved = bring(trans_hbm, trans)
    based = bring(basis_hbm, basis)

    def arrived():
        for copy in blocks:
            copy.wait()

    lifted.wait()
    parent = top_chain(place, partners, (three, two, one, level), moves, up, block, arrived)
    couple(codes, far, gather, tiles, held, takes, reads)
    descend(core, parent, far, trans, basis, mine, given, out, ones, twos, moved, based)


def finish(core, place, codes, partners, gathered, mine, given, moves, matrices, low, own, high, first, second, trans, basis):
    leaves, columns, _ = own.shape
    return pl.pallas_call(
        finish_body,
        out_shape=jax.ShapeDtypeStruct((columns, leaves * 128), f32),
        in_specs=[SM] * 4 + [VM] * 6 + [HBM] * 9,
        out_specs=VM,
        scratch_shapes=[
            pltpu.VMEM(moves.shape, f32),
            pltpu.VMEM((4, *matrices.shape[1:]), f32),
            pltpu.VMEM((32, columns, 128), f32),
            pltpu.VMEM((3, leaves, columns, 128), f32),
            pltpu.VMEM((2, *first.shape), bf16),
            pltpu.VMEM(trans.shape, bf16),
            pltpu.VMEM(basis.shape, f32),
            pltpu.VMEM((2, 3 * leaves, 2 * columns, 128), bf16),
            pltpu.VMEM((leaves, columns, 128), f32),
            pltpu.VMEM((leaves // 4, columns, 128), f32),
            pltpu.VMEM((leaves // 2, columns, 128), f32),
            pltpu.SemaphoreType.DMA((16,)),
        ],
        compiler_params=pltpu.CompilerParams(vmem_limit_bytes=VMEM_BYTES),
        cost_estimate=pl.CostEstimate(flops=1_000_000_000, bytes_accessed=20_000_000, transcendentals=0),
        name="finish",
    )(core, place, codes, partners, *gathered, mine, given, moves, matrices, low, own, high, first, second, trans, basis)


near_weight = 0.1
smoothing = 0.0025
PAIR = 2

def near_body(unroll, chunks, core, lists, live, targets, *refs):
    origins, refs = refs[:chunks], refs[chunks:]
    begin = None
    if chunks == 2:
        begin, refs = refs[0:2], refs[2:]
    mine, other, columns_of, total, weights, places, sem, *sources = refs
    leaves = mine.shape[1] // 128
    width = 2 * leaves
    core = core[0]
    side = chunks - 1
    mark = core * leaves
    reads = []
    for i, (origin, source) in enumerate(zip(origins, sources)):
        reads.append(pltpu.make_async_copy(origin, source, sem.at[i]))
        reads[-1].start()
    weights[chunks * width] = jnp.zeros(weights.shape[1:], bf16)
    places[chunks * width] = jnp.zeros(places.shape[1:], f32)
    blank = jnp.zeros((5, 128), f32)

    @pl.loop(0, leaves // 16)
    def _(g):
        rows = []
        for u in range(16):
            at = pl.ds(pl.multiple_of((core * leaves + 16 * g + u) * 128, 128), 128)
            rows += [targets[:, at], blank]
        t = jnp.transpose(jnp.concatenate(rows, axis=0))
        for u in range(16):
            for c in range(3):
                columns_of[16 * g + u, c] = jnp.broadcast_to(t[:, 8 * u + c : 8 * u + c + 1], (128, 128))
            total[16 * g + u] = jnp.zeros((128, 128), f32)

    for read in reads:
        read.wait()

    def load(block, base, turn):
        @pl.loop(0, leaves // 8)
        def _(g):
            for u in range(8):
                j = 8 * g + u
                x = [block[j], block[leaves + j]]
                weights[base + j] = stack(near_weight * jnp.concatenate(x[::-1] if turn else x, axis=0))
                for c in range(3):
                    places[base + j, c : c + 1] = block[2 * leaves + c, pl.ds(j, 1)]

    base = width * core if chunks == 2 else 0
    load(sources[0].at[0], base, False)
    load(sources[0].at[1], base + leaves, False)
    if chunks == 2:
        load(sources[1], width - leaves * core, True)
    items = lax.fori_loop(
        0, leaves, lambda i, s: s + jnp.maximum((live[side, mark + i] + PAIR - 1) // PAIR, 1), jnp.int32(0)
    )

    def block(leaf, slot):
        kernels, parts = [], []
        for u in range(PAIR):
            j = lists[side, slot + u, mark + leaf]
            s = places[j]
            d = columns_of[leaf, 0] - s[0:1]
            squared = d * d + smoothing
            d = columns_of[leaf, 1] - s[1:2]
            squared = squared + d * d
            d = columns_of[leaf, 2] - s[2:3]
            squared = squared + d * d
            kernels += split(lax.rsqrt(squared))
            x = weights[j]
            parts += [x, x]
        return lax.dot_general(
            jnp.concatenate(kernels, axis=1),
            jnp.concatenate(parts, axis=1),
            NT,
            preferred_element_type=f32,
        )

    def step(b, carry):
        leaf, slot = carry
        made = []
        for u in range(unroll):
            place = jnp.where(b * unroll + u < items, leaf, leaves)
            made.append((place, block(leaf, slot)))
            done = slot + PAIR >= live[side, mark + leaf]
            leaf = jnp.where(done, jnp.minimum(leaf + 1, leaves - 1), leaf)
            slot = jnp.where(done, 0, slot + PAIR)
        for place, x in made:
            total[place] += x
        return leaf, slot

    lax.fori_loop(0, (items + unroll - 1) // unroll, step, (jnp.int32(0), jnp.int32(0)))

    @pl.loop(0, leaves, unroll=8)
    def _(leaf):
        at = pl.ds(pl.multiple_of(leaf * 128, 128), 128)
        x = jnp.transpose(both(total[leaf]))
        if begin is None:
            mine[:, at] = x[0:32]
            other[:, at] = x[32:64]
        else:
            mine[:, at] = begin[0][:, at] + x[0:32]
            other[:, at] = begin[1][:, at] + x[32:64]


def near_pass(unroll, core, lists, live, targets, sources, begin=()):
    leaves = lists.shape[2] // 2
    chunks = len(sources)
    held = chunks * 2 * leaves + 1
    side = jax.ShapeDtypeStruct((32, leaves * 128), f32)
    arrays = (targets, *sources, *begin)
    return pl.pallas_call(
        functools.partial(near_body, unroll, chunks),
        out_shape=(side, side),
        in_specs=[SM, SM, SM, VM] + [HBM] * len(sources) + [VM] * len(begin),
        out_specs=(VM, VM),
        scratch_shapes=[
            pltpu.VMEM((leaves, 3, 128, 128), f32),
            pltpu.VMEM((leaves + 1, 128, 128), f32),
            pltpu.VMEM((held, 128, 128), bf16),
            pltpu.VMEM((held, 8, 128), f32),
            pltpu.SemaphoreType.DMA((len(sources),)),
            *[pltpu.VMEM(x.shape, f32) for x in sources],
        ],
        compiler_params=pltpu.CompilerParams(vmem_limit_bytes=VMEM_BYTES),
        cost_estimate=pl.CostEstimate(flops=1_000, bytes_accessed=1_000, transcendentals=0),
        name="near_pass",
    )(core, lists, live, *arrays)


def local(
    points,
    values,
    near_list,
    near_count,
    basis,
    transfer,
    coupling,
    partners,
    transfer_top,
    coupling_top,
    partners_top,
):
    leaves = basis.shape[0]
    position = lax.axis_index("leaf")
    core = lax.axis_index("rhs")
    count = lax.axis_size("leaf")
    forward = [(i, i + 1) for i in range(count - 1)]
    backward = [(target, source) for source, target in forward]
    swap = [(0, 1), (1, 0)]
    across = lax.ppermute(values, "rhs", swap)

    def ring(x, stride):
        spot = (position // stride) % 4
        turned = []
        for shift in range(3, 0, -1):
            to = [(i, i + stride * ((i // stride + shift) % 4 - i // stride % 4)) for i in range(count)]
            turned.append(lax.ppermute(x, "leaf", to))
        return turned, spot

    def in_order(turned, x, spot):
        blocks = [*turned, x]
        ordered = []
        for k in range(4):
            block = blocks[3]
            for j in range(3):
                block = jnp.where(spot == (k - j - 1) % 4, blocks[j], block)
            ordered.append(block)
        return jnp.concatenate(ordered, axis=0)

    after = lax.optimization_barrier
    core = core[None].astype(jnp.int32)
    place = position[None].astype(jnp.int32)
    coupling = coupling.transpose(1, 2, 3, 0)
    first = unbatch(coupling, 0)
    across, first, coupling = after((across, first, coupling))
    packed = pack(points, values, across)
    outward = [(2 * i, 2 * i + 2) for i in range(count - 1)]
    outward += [(2 * i + 3, 2 * i + 1) for i in range(count - 1)]
    beside = lax.ppermute(packed, ("leaf", "rhs"), outward)
    place, packed = after((place, packed))
    up, share, trans, lists, live, codes = up_pass(
        place, near_list.T, near_count[None], partners.T, basis, values, transfer.transpose(1, 2, 0)
    )
    begin = near_pass(12, core, lists, live, points, (packed,))
    share, beside, begin = after((share, beside, begin))
    turned, spot = ring(share[None], 1)
    passed = lax.dynamic_index_in_dim(beside, 1 - core[0], 0, keepdims=False)
    passed = lax.ppermute(passed, "rhs", swap)
    level = in_order(turned, share[None], spot)
    level = jnp.where(jnp.arange(128) < 64, level[0] + level[1], level[2] + level[3])[None]
    turned, spot = ring(level, 4)
    turned, passed, up = after((turned, passed, up))
    level = in_order(turned, level, spot)
    turned, spot = ring(level, 16)
    up_low = lax.ppermute(up, "leaf", forward)
    up_high = lax.ppermute(up, "leaf", backward)
    mine, other = near_pass(12, core, lists, live, points, (beside, passed), begin)
    mine, other, coupling = after((mine, other, coupling))
    second = unbatch(coupling, 1)
    turned, other, second = after((turned, other, second))
    given = lax.ppermute(other, "rhs", swap)
    return finish(
        core,
        place,
        codes,
        partners_top.T,
        (*turned, level),
        mine,
        given,
        transfer_top,
        coupling_top,
        up_low,
        up,
        up_high,
        first,
        second,
        trans,
        basis,
    )


def solution(mesh):
    placed = (
        P(None, "leaf"),
        P("rhs", "leaf"),
        P("leaf", None),
        P("leaf"),
        P("leaf", None, None),
        P("leaf", None, None),
        P("leaf", None, None, None),
        P("leaf", None),
        P(),
        P(),
        P(),
    )
    return jax.shard_map(
        local, mesh=mesh, in_specs=placed, out_specs=P("rhs", "leaf"), check_vma=False
    )
```
